32 devices in a mesh: dp: 4 (over y, x), tensor: 8 (over z, core).
Axes of the slice: x: 2, y: 2, z: 4, core: 2. Of those that a mesh axis runs over, the one named last changes fastest.
Arguments:
- inputs: bfloat16 [4, 2048, 2048], P('dp'), may hold values from -6 to 6
- segment_ids: int32 [4, 2048], P('dp'), may hold values from 0 to 7, never falling along the last dimension, each value on 1 to 1024 neighbouring positions
- norm_gain: bfloat16 [2048], replicated, may hold values from 0.5 to 1.5
- norm_bias: bfloat16 [2048], replicated, may hold values from -2 to 2
- qkv_weight: bfloat16 [2048, 3, 2048], P(None, None, 'tensor'), may hold values from -0.125 to 0.125
- qkv_bias: bfloat16 [3, 2048], P(None, 'tensor'), may hold values from -2 to 2
- out_weight: bfloat16 [2048, 2048], P('tensor'), may hold values from -0.5 to 0.5
- out_bias: bfloat16 [2048], replicated, may hold values from -2 to 2
- up_weight: bfloat16 [2048, 8192], P(None, 'tensor'), may hold values from -0.125 to 0.125
- up_bias: bfloat16 [8192], P('tensor'), may hold values from -2 to 2
- down_weight: bfloat16 [8192, 2048], P('tensor'), may hold values from -0.0625 to 0.0625
- down_bias: bfloat16 [2048], replicated, may hold values from -2 to 2
- cotangent: bfloat16 [4, 2048, 2048], P('dp'), may hold values from -6 to 6
Outputs:
- output: bfloat16 [4, 2048, 2048], P('dp')
- input_grad: bfloat16 [4, 2048, 2048], P('dp')
- norm_gain_grad: float32 [2048], P('dp')
- norm_bias_grad: float32 [2048], P('dp')
- qkv_weight_grad: float32 [2048, 3, 2048], P('dp', None, 'tensor')
- qkv_bias_grad: float32 [3, 32, 64], P(None, 'tensor', 'dp')
- out_weight_grad: float32 [2048, 2048], P('tensor', 'dp')
- out_bias_grad: float32 [2048], P('dp')
- up_weight_grad: float32 [2048, 8192], P('dp', 'tensor')
- up_bias_grad: float32 [128, 64], P('tensor', 'dp')
- down_weight_grad: float32 [8192, 2048], P('tensor', 'dp')
- down_bias_grad: float32 [2048], P('dp')
The draws below stay inside these ranges and needn't reach their ends.
Inputs may be any that keep to these rules, and one draw needn't show every extreme that they name: `segment_ids`: along each row the ids never fall; every document holds 1 to 1024 tokens, and one document of each row holds exactly 1024.
All inputs are finite; a program needn't handle non-finite values.
Results may differ from the reference program's by a relative error of at most 0.017.
Values may be sent and summed in bfloat16 or wider, within the bound.
A program may use at most 256 MiB of HBM per device.

```python
import math
import jax
import jax.numpy as jnp
import numpy as np
from jax import lax

D = 2048
HEADS = 32
HD = 64
FF = 8192
ROT = 32
TOK = 2048
ROWS = 4
DOCS = 8


def block_scale(rng, extent, cuts, smallest, high):
    def one(dim, blocks):
        steps = jax.random.uniform(jax.random.fold_in(jax.random.fold_in(rng, 6), dim), (blocks,), jnp.float32, smallest / len(cuts), high / len(cuts))
        return jnp.repeat(jnp.exp(steps), extent[dim] // blocks).reshape((-1,) + (1,) * (len(extent) - dim - 1))

    loudness = one(*cuts[0])
    for cut in cuts[1:]:
        loudness = loudness * one(*cut)
    return loudness


def length_profile(amount, total, bound, slope):
    weights = [(1 << 20) // math.isqrt(rank ** slope) + 1 for rank in range(2, amount + 1)]
    surplus, given = total - bound - (amount - 1), [1] * (amount - 1)
    while surplus > 0:
        candidates = [i for i in range(amount - 1) if given[i] < bound]
        whole, remaining = sum([weights[i] for i in candidates]), surplus
        for i in candidates:
            more = min(bound - given[i], max(1, remaining * weights[i] // whole), surplus)
            given[i] = given[i] + more
            surplus = surplus - more
    return np.array([bound] + given)


def uneven(own_key, count, total, limit, skew):
    if count == 2:
        one = jax.random.randint(own_key, (), max(1, total - limit), min(limit, total - 1) + 1)
        return jnp.stack([one, total - one])
    sizes = jnp.asarray(length_profile(count, total, limit, skew), jnp.int32)
    couples = (count - 1) // 2
    giver, sink = sizes[1:1 + 2 * couples:2], sizes[2:2 + 2 * couples:2]
    margin = jnp.minimum(giver - 1, limit - sink)
    shifted = jax.random.randint(jax.random.fold_in(own_key, 1), (couples,), 0, 1 << 20) % (margin + 1)
    sizes = sizes.at[1:1 + 2 * couples:2].set(giver - shifted).at[2:2 + 2 * couples:2].set(sink + shifted)
    return sizes[jax.random.permutation(jax.random.fold_in(own_key, 2), count)]


def scatter_about(rng, extent, width, limit, shards=(), held_as=jnp.bfloat16):
    factor_of = block_scale(rng, extent, shards, -0.22, 0.18) if shards else 1.0
    entries = jax.random.normal(rng, extent, jnp.float32) * width * factor_of
    return jnp.minimum(jnp.maximum(entries, -limit), limit).astype(held_as)


def setup_inputs(seed: int = 0) -> dict:
    arg_keys = jax.random.split(jax.random.key(seed), 14)
    inputs = scatter_about(arg_keys[0], (ROWS, TOK, D), 1.0, 6.0, ((0, 4),))
    segment_ids = jax.vmap(lambda own: jnp.searchsorted(jnp.cumsum(uneven(own, DOCS, TOK, TOK // 2, 1)), jnp.arange(TOK), side="right"))(jax.random.split(arg_keys[1], ROWS)).reshape((ROWS, TOK)).astype(jnp.int32)
    norm_gain = jnp.clip(1.0 + 0.1 * jax.random.normal(arg_keys[2], (D,), jnp.float32), 0.5, 1.5).astype(jnp.bfloat16)
    norm_bias = scatter_about(arg_keys[3], (D,), 0.3, 2.0)
    qkv_weight = scatter_about(arg_keys[4], (D, 3, D), D ** -0.5, 0.125, ((2, 8),))
    qkv_bias = scatter_about(arg_keys[5], (3, D), 0.3, 2.0, ((1, 8),))
    out_weight = scatter_about(arg_keys[6], (D, D), (D // 16) ** -0.5, 0.5, ((0, 8),))
    out_bias = scatter_about(arg_keys[7], (D,), 0.3, 2.0)
    up_weight = scatter_about(arg_keys[8], (D, FF), D ** -0.5, 0.125, ((1, 8),))
    up_bias = scatter_about(arg_keys[9], (FF,), 0.3, 2.0, ((0, 8),))
    down_weight = scatter_about(arg_keys[10], (FF, D), FF ** -0.5, 0.0625, ((0, 8),))
    down_bias = scatter_about(arg_keys[11], (D,), 0.3, 2.0)
    cotangent = scatter_about(arg_keys[12], (ROWS, TOK, D), 1.0, 6.0, ((0, 4),))
    return dict(inputs=inputs, segment_ids=segment_ids, norm_gain=norm_gain, norm_bias=norm_bias, qkv_weight=qkv_weight, qkv_bias=qkv_bias, out_weight=out_weight, out_bias=out_bias, up_weight=up_weight, up_bias=up_bias, down_weight=down_weight, down_bias=down_bias, cotangent=cotangent)


highest = lax.Precision.HIGHEST

@jax.custom_vjp
def low(v):
    return lax.optimization_barrier(v.astype(jnp.bfloat16)).astype(jnp.float32)

@jax.custom_vjp
def low_back(v):
    return v

def low_keep(v):
    return (low(v), None)

def low_pass(kept, grad):
    return (grad,)

def back_keep(v):
    return (v, None)

def back_low(kept, grad):
    return (low(grad),)
low.defvjp(low_keep, low_pass)
low_back.defvjp(back_keep, back_low)

def positions_of(segment_row):
    length = segment_row.shape[0]
    places = jnp.arange(length, dtype=jnp.int32)
    earlier = jnp.concatenate([segment_row[:1] - 1, segment_row[:-1]])
    starts = jnp.where(segment_row != earlier, places, jnp.zeros_like(places))
    return places - lax.cummax(starts, axis=0)

def rotary_tables(segment_row):
    places = positions_of(segment_row).astype(jnp.float32)
    freqs = 10000.0 ** (-jnp.arange(ROT // 2, dtype=jnp.float32) * 2.0 / ROT)
    angles = places[:, None] * freqs[None, :]
    return (jnp.cos(angles), jnp.sin(angles))

def rotate(vectors, cosine, sine):
    first = vectors[..., :ROT // 2]
    second = vectors[..., ROT // 2:ROT]
    cos_wide = cosine[:, None, :]
    sin_wide = sine[:, None, :]
    return jnp.concatenate([first * cos_wide - second * sin_wide, second * cos_wide + first * sin_wide, vectors[..., ROT:]], axis=-1)

def layer_norm(values, gain, shift):
    average = lax.optimization_barrier(jnp.mean(values, axis=-1, keepdims=True))
    centered = values - average
    variance = lax.optimization_barrier(jnp.mean(centered * centered, axis=-1, keepdims=True))
    return centered * lax.rsqrt(variance + 1e-05) * gain + shift

def attend(queries, keys, values, segment_row):
    length = queries.shape[0]
    block_rows = min(512, length)
    places = jnp.arange(length, dtype=jnp.int32)
    scaling = HD ** (-0.5)

    def one_block(block_data):
        q_block, q_segment, q_place = block_data
        scores = jnp.einsum('qhd,khd->hqk', q_block, keys, precision=highest) * scaling
        scores = low_back(scores)
        allowed = (q_segment[:, None] == segment_row[None, :]) & (q_place[:, None] >= places[None, :])
        scores = jnp.where(allowed[None], scores, -1e+30)
        row_max = lax.optimization_barrier(jnp.max(scores, axis=-1, keepdims=True))
        raised = jnp.exp(scores - row_max)
        probability = raised / lax.optimization_barrier(jnp.sum(raised, axis=-1, keepdims=True))
        return jnp.einsum('hqk,khd->qhd', low(probability), values, precision=highest)
    blocks = length // block_rows
    pieces = lax.map(jax.checkpoint(one_block), (queries.reshape(blocks, block_rows, HEADS, HD), segment_row.reshape(blocks, block_rows), places.reshape(blocks, block_rows)))
    return pieces.reshape(length, HEADS * HD)

def forward(inputs_row, segment_row, cosine, sine, norm_gain, norm_bias, qkv_weight, qkv_bias, out_weight, out_bias, up_weight, up_bias, down_weight, down_bias):
    length = inputs_row.shape[0]
    normed = low(layer_norm(inputs_row, norm_gain, norm_bias))
    packed = jnp.dot(normed, qkv_weight.reshape(D, 3 * D), precision=highest).reshape(length, 3, D) + qkv_bias[None]
    packed = low_back(packed)
    split = packed.reshape(length, 3, HEADS, HD)
    queries = low(rotate(split[:, 0], cosine, sine))
    keys = low(rotate(split[:, 1], cosine, sine))
    values = low(split[:, 2])
    mixed = low(low_back(attend(queries, keys, values, segment_row)))
    attn_branch = jnp.dot(mixed, out_weight, precision=highest)
    hidden_pre = low_back(jnp.dot(normed, up_weight, precision=highest) + up_bias)
    hidden = low(jax.nn.gelu(hidden_pre, approximate=True))
    mlp_branch = jnp.dot(hidden, down_weight, precision=highest)
    return inputs_row + attn_branch + mlp_branch + out_bias + down_bias

def reference(inputs, segment_ids, norm_gain, norm_bias, qkv_weight, qkv_bias, out_weight, out_bias, up_weight, up_bias, down_weight, down_bias, cotangent):
    params = tuple((param.astype(jnp.float32) for param in (norm_gain, norm_bias, qkv_weight, qkv_bias, out_weight, out_bias, up_weight, up_bias, down_weight, down_bias)))
    starting = tuple((jnp.zeros(param.shape, jnp.float32) for param in params))

    def per_row(totals, row_data):
        inputs_row, segment_row, grad_row = row_data
        cosine, sine = rotary_tables(segment_row)

        def apply_layer(inputs_float, *weights):
            return forward(inputs_float, segment_row, cosine, sine, *weights)
        result, pullback = jax.vjp(apply_layer, inputs_row.astype(jnp.float32), *params)
        grads = pullback(grad_row.astype(jnp.float32))
        totals = tuple((running + update for running, update in zip(totals, grads[1:])))
        return (totals, (result.astype(jnp.bfloat16), grads[0].astype(jnp.bfloat16)))
    totals, (outputs, input_grads) = lax.scan(per_row, starting, (inputs, segment_ids, cotangent))
    gain_grad, shift_grad, qkv_w_grad, qkv_b_grad, out_w_grad, out_b_grad, up_w_grad, up_b_grad, down_w_grad, down_b_grad = totals
    return (outputs, input_grads, gain_grad, shift_grad, qkv_w_grad, qkv_b_grad.reshape(3, HEADS, HD), out_w_grad, out_b_grad, up_w_grad, up_b_grad.reshape(FF // HD, HD), down_w_grad, down_b_grad)
```

```python
from functools import partial

import jax
import jax.numpy as jnp
from jax import lax
from jax.experimental import pallas as pl
from jax.experimental.pallas import tpu as pltpu
from jax.sharding import PartitionSpec as P

HD = 64
ROT = 32
PAIR = 2 * HD
TILE = 256
CHUNKS = 4
NEG = -1e30
MIB = 1 << 20
F32 = jnp.float32
BF16 = jnp.bfloat16


class Chain:
    def __init__(self):
        self.link = jnp.zeros((8, 128), F32)

    def __call__(
        self, kernel, name, grid, ins, outs, scalars=(), scratch=(), alias=(), flops=0.0, moved=0.0, mib=58
    ):
        taken, given = len(scalars) + len(ins), len(outs)

        def body(*refs):
            kernel(*refs[:taken], *refs[taken + 1 : taken + 1 + given], *refs[taken + 2 + given :])

        anywhere = pl.BlockSpec(memory_space=pl.ANY)
        results = pl.pallas_call(
            body,
            grid_spec=pltpu.PrefetchScalarGridSpec(
                num_scalar_prefetch=len(scalars),
                grid=(grid,),
                in_specs=[spec for _, spec in ins] + [anywhere],
                out_specs=[spec for _, _, spec in outs] + [anywhere],
                scratch_shapes=list(scratch),
            ),
            out_shape=[jax.ShapeDtypeStruct(shape, dtype) for shape, dtype, _ in outs]
            + [jax.ShapeDtypeStruct(self.link.shape, F32)],
            input_output_aliases={taken: given, **{len(scalars) + i: o for i, o in alias}},
            compiler_params=pltpu.CompilerParams(
                dimension_semantics=("arbitrary",), vmem_limit_bytes=mib * MIB
            ),
            cost_estimate=pl.CostEstimate(
                flops=int(flops), bytes_accessed=int(moved), transcendentals=0
            ),
            name=name,
        )(*scalars, *[array for array, _ in ins], self.link)
        self.link = results[-1]
        return results[:-1]


def whole(shape):
    zeros = (0,) * len(shape)
    return pl.BlockSpec(shape, lambda *i: zeros)


def rows(n, height=TILE):
    return pl.BlockSpec((height, n), lambda i, *s: (i, 0))


def nn(a, b):
    return lax.dot_general(a, b, (((1,), (0,)), ((), ())), preferred_element_type=F32)


def nt(a, b):
    return lax.dot_general(a, b, (((1,), (1,)), ((), ())), preferred_element_type=F32)


def tn(a, b):
    return lax.dot_general(a, b, (((0,), (0,)), ((), ())), preferred_element_type=F32)


def column(row, width):
    return jnp.broadcast_to(row, (width, row.shape[1])).T


def rotated(x, cos_wide, sin_wide):
    lane = lax.broadcasted_iota(jnp.int32, x.shape, 1) % HD
    half = ROT // 2
    other = jnp.where(
        lane < half, pltpu.roll(x, PAIR - half, 1), pltpu.roll(x, half, 1)
    )
    return x * cos_wide + other * sin_wide


def row_stats(x):
    mean = jnp.mean(x, axis=-1, keepdims=True)
    centered = x - mean
    inverse = lax.rsqrt(jnp.mean(centered * centered, axis=-1, keepdims=True) + 1e-05)
    return centered * inverse, mean, inverse


def gelu_both(u):
    c = 0.7978845608028654
    u2 = u * u
    gate = 0.5 + 0.5 * jnp.tanh(u * (c + (c * 0.044715) * u2))
    value = u * gate
    slope = gate + value * (1.0 - gate) * (2.0 * c + (6.0 * c * 0.044715) * u2)
    return value, slope


def first_kernel(
    x0_ref, x1_ref, x2_ref, small_ref, wq_ref, bq_ref, wu_ref, bu_ref, start_ref, freq_ref,
    normed_ref, stats_ref, q_ref, k_ref, v_ref, hidden_ref, slope_ref, cos_ref, sin_ref,
    even, odd, even_stats,
):
    s = pl.program_id(0)
    gain, shift = small_ref[0:1], small_ref[1:2]
    lane = lax.broadcasted_iota(jnp.int32, (TILE, PAIR), 1)

    def norm(x):
        scaled, mean, inverse = row_stats(x.astype(F32))
        return (scaled * gain + shift).astype(BF16), jnp.where(lane == 0, mean, inverse)

    @pl.when(s == 0)
    def _():
        even[...], even_stats[...] = norm(x0_ref[...])

    half = ROT // 2
    unit = lax.broadcasted_iota(jnp.int32, (half, PAIR), 1) % HD
    index = lax.broadcasted_iota(jnp.int32, (half, PAIR), 0)
    first_half = (unit == index).astype(F32)
    second_half = (unit == index + half).astype(F32)
    bias = bq_ref[...].astype(F32)

    def spread(a, b):
        return lax.dot_general(
            a, b, (((0,), (0,)), ((), ())), precision=lax.Precision.HIGHEST,
            preferred_element_type=F32,
        )

    def project(t, normed):
        here = slice(t * TILE, (t + 1) * TILE)
        place = lax.broadcasted_iota(jnp.int32, (1, TILE), 1) + (2 * s + t) * TILE
        angle = freq_ref[...] * (place - start_ref[:, here]).astype(F32)
        cos_wide = spread(jnp.cos(angle), first_half + second_half)
        cos_wide = jnp.where(lane % HD < ROT, cos_wide, 1.0)
        sin_wide = spread(jnp.sin(angle), second_half - first_half)
        cos_ref[here], sin_ref[here] = cos_wide, sin_wide
        for c, out in enumerate((q_ref, k_ref, v_ref)):
            packed = nn(normed, wq_ref[c]) + bias[c : c + 1]
            if c == 2:
                out[here] = packed.astype(BF16)
            else:
                for p in range(packed.shape[1] // PAIR):
                    cut = slice(p * PAIR, (p + 1) * PAIR)
                    turned = rotated(packed[:, cut], cos_wide, sin_wide).astype(BF16)
                    out[here, cut] = turned * (HD**-0.5) if c == 0 else turned
        units = wu_ref.shape[1]
        for n in range(0, units, TILE):
            cut = slice(n, n + TILE)
            value, slope = gelu_both(nn(normed, wu_ref[:, cut]) + bu_ref[:, cut])
            hidden_ref[here, cut] = value.astype(BF16)
            slope_ref[here, cut] = slope.astype(BF16)

    normed = even[...]
    normed_ref[:TILE] = normed
    stats_ref[:TILE] = even_stats[...]
    after, after_stats = norm(x1_ref[...])
    odd[...] = after
    normed_ref[TILE:] = after
    stats_ref[TILE:] = after_stats
    project(0, normed)
    even[...], even_stats[...] = norm(x2_ref[...])
    project(1, odd[...])


def first(chain, x, small, wq, bq, wu, bu, start):
    length, d = x.shape
    width, units = wq.shape[2], wu.shape[1]
    tiles = length // TILE
    freq = 10000.0 ** (-jnp.arange(ROT // 2, dtype=F32) * 2.0 / ROT)
    at = lambda f: pl.BlockSpec((TILE, d), lambda s: (f(s), 0))
    big = lambda n: rows(n, 2 * TILE)
    return chain(
        first_kernel,
        "first",
        tiles // 2,
        [
            (x, at(lambda s: 0)),
            (x, at(lambda s: 2 * s + 1)),
            (x, at(lambda s: jnp.minimum(2 * s + 2, tiles - 1))),
            (small, whole(small.shape)), (wq, whole(wq.shape)), (bq, whole(bq.shape)),
            (wu, whole(wu.shape)), (bu[None].astype(F32), whole((1, units))),
            (start[None], pl.BlockSpec((1, 2 * TILE), lambda s: (0, s))),
            (jnp.broadcast_to(freq[:, None], (ROT // 2, TILE)), whole((ROT // 2, TILE))),
        ],
        [((length, d), BF16, big(d)), ((length, PAIR), F32, big(PAIR))]
        + [((length, n), BF16, big(n)) for n in (width, width, width, units, units)]
        + [((length, PAIR), F32, big(PAIR))] * 2,
        scratch=[pltpu.VMEM((TILE, d), BF16)] * 2 + [pltpu.VMEM((TILE, PAIR), F32)],
        flops=2 * length * d * (3 * width + units),
        moved=2 * length * d * 4,
    )


def attend_kernel(start_sref, start_ref, q_ref, k_ref, v_ref, mixed_ref, log_ref):
    i = pl.program_id(0)
    pairs = q_ref.shape[1] // PAIR
    left = lax.broadcasted_iota(jnp.int32, (TILE, PAIR), 1) < HD
    zero = jnp.zeros((TILE, PAIR), BF16)
    start = column(start_ref[...], TILE) - lax.broadcasted_iota(jnp.int32, (TILE, TILE), 1)
    ahead = lax.broadcasted_iota(jnp.int32, (TILE, TILE), 0) - lax.broadcasted_iota(
        jnp.int32, (TILE, TILE), 1
    )
    heads = []
    for p in range(pairs):
        q = q_ref[:, p * PAIR : (p + 1) * PAIR]
        heads += [jnp.where(left, q, zero), jnp.where(left, zero, q)]

    def step(j, carry):
        tops, totals, sums = carry
        base = j * TILE
        allowed = (start <= base) & (ahead >= base - i * TILE)
        new_tops, new_totals, new_sums = [], [], []
        for p in range(pairs):
            cut = slice(p * PAIR, (p + 1) * PAIR)
            k = k_ref[pl.ds(pl.multiple_of(base, TILE), TILE), cut]
            v = v_ref[pl.ds(pl.multiple_of(base, TILE), TILE), cut]
            shrink, grown = [], []
            for e in range(2):
                h = 2 * p + e
                s = jnp.where(allowed, nt(heads[h], k), NEG)
                top = jnp.maximum(tops[h], jnp.max(s, axis=1, keepdims=True))
                alpha = jnp.exp(tops[h] - top)
                w = jnp.exp(s - top)
                new_tops.append(top)
                new_totals.append(totals[h] * alpha + jnp.sum(w, axis=1, keepdims=True))
                shrink.append(alpha)
                vh = jnp.where(left, v, zero) if e == 0 else jnp.where(left, zero, v)
                grown.append(nn(w.astype(BF16), vh))
            new_sums.append(sums[p] * jnp.where(left, *shrink) + (grown[0] + grown[1]))
        return tuple(new_tops), tuple(new_totals), tuple(new_sums)

    empty = (
        tuple(jnp.full((TILE, 1), NEG, F32) for _ in range(2 * pairs)),
        tuple(jnp.zeros((TILE, 1), F32) for _ in range(2 * pairs)),
        tuple(jnp.zeros((TILE, PAIR), F32) for _ in range(pairs)),
    )
    low = start_sref[i * TILE] // TILE
    tops, totals, sums = lax.fori_loop(low, i + 1, step, empty)
    lane = lax.broadcasted_iota(jnp.int32, (TILE, PAIR), 1)
    logs = jnp.zeros((TILE, PAIR), F32)
    for p in range(pairs):
        scale = jnp.where(left, 1.0 / totals[2 * p], 1.0 / totals[2 * p + 1])
        mixed_ref[:, p * PAIR : (p + 1) * PAIR] = (sums[p] * scale).astype(BF16)
        for h in (2 * p, 2 * p + 1):
            logs = jnp.where(lane == h, tops[h] + jnp.log(totals[h]), logs)
    log_ref[...] = logs.T[:8]


def attend(chain, start, q, k, v):
    length, width = q.shape
    full = whole((length, width))
    return chain(
        attend_kernel,
        "attend",
        length // TILE,
        [
            (start[None], pl.BlockSpec((1, TILE), lambda i, *s: (0, i))),
            (q, rows(width)), (k, full), (v, full),
        ],
        [
            ((length, width), BF16, rows(width)),
            ((8, length), F32, pl.BlockSpec((8, TILE), lambda i, *s: (0, i))),
        ],
        scalars=(start,),
        flops=15e9,
        moved=8 * length * width,
    )


def attend_back_kernel(
    begin, start_sref, start_ref, log_ref, delta_ref, q_ref, k_ref, v_ref, g_ref, cos_ref, sin_ref,
    totals_in, gq_ref, gk_ref, gv_ref, bias_ref, totals,
):
    j = pl.program_id(0) + begin
    length, width = q_ref.shape
    pairs = width // PAIR
    here = pl.ds(pl.multiple_of(j * TILE, TILE), TILE)

    @pl.when(pl.program_id(0) == 0)
    def _():
        totals[...] = totals_in[...] if begin else jnp.zeros_like(totals)
        bias_ref[...] = jnp.zeros_like(bias_ref)

    left = lax.broadcasted_iota(jnp.int32, (TILE, PAIR), 1) < HD
    zero = jnp.zeros((TILE, PAIR), BF16)
    key_place = j * TILE + lax.broadcasted_iota(jnp.int32, (TILE, TILE), 0)
    ahead = lax.broadcasted_iota(jnp.int32, (TILE, TILE), 1) - lax.broadcasted_iota(
        jnp.int32, (TILE, TILE), 0
    )

    def halves(x):
        return jnp.where(left, x, zero), jnp.where(left, zero, x)

    keys = [k_ref[here, p * PAIR : (p + 1) * PAIR] for p in range(pairs)]
    split = [halves(k) for k in keys]
    values = [v_ref[here, p * PAIR : (p + 1) * PAIR] for p in range(pairs)]

    def step(i, carry):
        gks, gvs = carry
        there = pl.ds(pl.multiple_of(i * TILE, TILE), TILE)
        allowed = (key_place >= start_ref[:, there]) & (ahead >= (j - i) * TILE)
        new_gk, new_gv = [], []
        for p in range(pairs):
            cut = slice(p * PAIR, (p + 1) * PAIR)
            qs = halves(q_ref[there, cut])
            gs = halves(g_ref[there, cut])
            gk, gv = gks[p], gvs[p]
            gq = totals[there, cut]
            for e in range(2):
                h = 2 * p + e
                s = nt(keys[p], qs[e]) - log_ref[h : h + 1, there]
                w = jnp.exp(jnp.where(allowed, s, NEG))
                gp = nt(values[p], gs[e])
                ds = (w * (gp - delta_ref[h : h + 1, there])).astype(BF16)
                gv = gv + nn(w.astype(BF16), gs[e])
                gk = gk + nn(ds, qs[e])
                gq = gq + tn(ds, split[p][e])
            totals[there, cut] = gq
            new_gk.append(gk)
            new_gv.append(gv)
        return tuple(new_gk), tuple(new_gv)

    high = sum((start_sref[b * TILE] < (j + 1) * TILE).astype(jnp.int32) for b in range(length // TILE))
    empty = tuple(jnp.zeros((TILE, PAIR), F32) for _ in range(pairs))
    gks, gvs = lax.fori_loop(j, high, step, (empty, empty))
    cos_wide, sin_wide = cos_ref[...], -sin_ref[...]
    for p in range(pairs):
        cut = slice(p * PAIR, (p + 1) * PAIR)
        gq = rotated(totals[here, cut] * (HD**-0.5), cos_wide, sin_wide).astype(BF16)
        gk = rotated(gks[p], cos_wide, sin_wide).astype(BF16)
        gv = gvs[p].astype(BF16)
        for c, (g, out) in enumerate(((gq, gq_ref), (gk, gk_ref), (gv, gv_ref))):
            out[:, cut] = g
            bias_ref[c : c + 1, cut] += jnp.sum(g.astype(F32), axis=0, keepdims=True)


def attend_back(chain, begin, end, start, log, delta, q, k, v, g, cos_wide, sin_wide, before):
    length, width = q.shape
    full = whole((length, width))
    shifted = pl.BlockSpec((TILE, PAIR), lambda i, *s: (i + begin, 0))
    return chain(
        partial(attend_back_kernel, begin),
        f"attend_back_{begin}",
        end - begin,
        [
            (start[None], whole((1, length))), (log, whole((8, length))), (delta, whole((8, length))),
            (q, full), (k, full), (v, full), (g, full), (cos_wide, shifted), (sin_wide, shifted),
            (before, full if begin else pl.BlockSpec(memory_space=pl.ANY)),
        ],
        [(((end - begin) * TILE, width), BF16, rows(width))] * 3
        + [((8, width), F32, whole((8, width))), ((length, width), F32, full)],
        scalars=(start,),
        flops=17e9,
        moved=14 * length * width,
    )


def half_rows(chunks, half):
    def spec(n):
        def index(i, core):
            return (2 * (i % chunks) + jnp.where(i < chunks, 1 - core[0], core[0]), 0)

        return pl.BlockSpec((half, n), index)

    return spec


def store_part(total, parts):
    for n, part in enumerate(parts):

        @pl.when(pl.program_id(0) == n)
        def _():
            part[...] = total


def branch_kernel(core_ref, mixed_ref, hidden_ref, wo_ref, wd_ref, *parts):
    total = (nn(mixed_ref[...], wo_ref[...]) + nn(hidden_ref[...], wd_ref[...])).astype(BF16)
    store_part(total, parts)


def branch(chain, core, chunks, mixed, hidden, wo, wd):
    length, d = mixed.shape[0], wo.shape[1]
    half = length // (2 * chunks)
    spec = half_rows(chunks, half)
    return chain(
        branch_kernel,
        "branch",
        2 * chunks,
        [
            (mixed, spec(mixed.shape[1])), (hidden, spec(hidden.shape[1])),
            (wo, whole(wo.shape)), (wd, whole(wd.shape)),
        ],
        [((half, d), BF16, whole((half, d)))] * (2 * chunks),
        scalars=(core,),
        flops=2 * length * d * (wo.shape[0] + wd.shape[0]),
        moved=2 * length * d * 3,
    )


def back_kernel(g_ref, slope_ref, mixed_ref, wo_ref, wd_ref, pre_ref, gm_ref, delta_ref, sums_ref, up_ref):
    @pl.when(pl.program_id(0) == 0)
    def _():
        sums_ref[...] = jnp.zeros_like(sums_ref)
        up_ref[...] = jnp.zeros_like(up_ref)

    g = g_ref[...]
    for n in range(0, wd_ref.shape[0], TILE):
        cut = slice(n, n + TILE)
        pre = (nt(g, wd_ref[cut]) * slope_ref[:, cut].astype(F32)).astype(BF16)
        pre_ref[:, cut] = pre
        up_ref[0:1, cut] += jnp.sum(pre.astype(F32), axis=0, keepdims=True)
    gm = nt(g, wo_ref[...]).astype(BF16)
    gm_ref[...] = gm
    product = gm.astype(F32) * mixed_ref[...].astype(F32)
    coarse = product.astype(BF16)
    fine = (product - coarse.astype(F32)).astype(BF16)
    width = gm.shape[1]
    pick = (
        lax.broadcasted_iota(jnp.int32, (8, width), 1) // HD
        == lax.broadcasted_iota(jnp.int32, (8, width), 0)
    ).astype(BF16)
    delta_ref[...] = nt(pick, coarse) + nt(pick, fine)
    sums_ref[0:1] += jnp.sum(g.astype(F32), axis=0, keepdims=True)


def back(chain, g, slope, mixed, wo, wd):
    length, d = g.shape
    width, units = wo.shape[0], wd.shape[0]
    return chain(
        back_kernel,
        "back",
        length // TILE,
        [
            (g, rows(d)), (slope, rows(units)), (mixed, rows(width)),
            (wo, whole(wo.shape)), (wd, whole(wd.shape)),
        ],
        [
            ((length, units), BF16, rows(units)), ((length, width), BF16, rows(width)),
            ((8, length), F32, pl.BlockSpec((8, TILE), lambda i, *s: (0, i))),
            ((8, d), F32, whole((8, d))), ((8, units), F32, whole((8, units))),
        ],
        flops=2 * length * d * (width + units),
        moved=2 * length * d * 2,
    )


def normed_back_kernel(core_ref, gq_ref, gk_ref, gv_ref, pre_ref, x_ref, stats_ref, wq_ref, wu_ref, *outs):
    parts, sums_ref = outs[:-1], outs[-1]

    @pl.when(pl.program_id(0) == 0)
    def _():
        sums_ref[...] = jnp.zeros_like(sums_ref)

    mean, inverse = stats_ref[:, 0:1], stats_ref[:, 1:2]
    pieces = []
    for n in range(0, wu_ref.shape[0], 2 * TILE):
        cut = slice(n, n + 2 * TILE)
        total = nt(pre_ref[...], wu_ref[cut])
        for c, g in enumerate((gq_ref, gk_ref, gv_ref)):
            total = total + nt(g[...], wq_ref[c, cut])
        pieces.append(total.astype(BF16))
        scaled = (x_ref[:, cut].astype(F32) - mean) * inverse
        sums_ref[0:1, cut] += jnp.sum(total * scaled, axis=0, keepdims=True)
        sums_ref[1:2, cut] += jnp.sum(total, axis=0, keepdims=True)
    store_part(jnp.concatenate(pieces, axis=1), parts)


def normed_back(chain, core, chunks, gq, gk, gv, pre, x, stats, wq, wu):
    length, d = x.shape
    width, units = wq.shape[2], wu.shape[1]
    half = length // (2 * chunks)
    spec = half_rows(chunks, half)
    return chain(
        normed_back_kernel,
        "normed_back",
        2 * chunks,
        [(a, spec(width)) for a in (gq, gk, gv)]
        + [
            (pre, spec(units)), (x, spec(d)), (stats, spec(PAIR)),
            (wq, whole(wq.shape)), (wu, whole(wu.shape)),
        ],
        [((half, d), BF16, whole((half, d)))] * (2 * chunks) + [((8, d), F32, whole((8, d)))],
        scalars=(core,),
        flops=2 * length * d * (3 * width + units),
        moved=2 * length * d * 4,
    )


def weight_grad_kernel(counts, *refs):
    lefts, right, outs = refs[: len(counts)], refs[len(counts)], refs[len(counts) + 1 :]
    i = pl.program_id(0)
    done = 0
    for left, out, count in zip(lefts, outs, counts):

        @pl.when((i >= done) & (i < done + count))
        def _(left=left, out=out):
            out[...] = tn(left[...], right[...]).astype(BF16)

        done += count


def weight_grad(chain, name, lefts, right):
    length, d = right.shape
    counts = tuple(a.shape[1] // min(TILE, a.shape[1]) for a in lefts)
    ins, outs, done = [], [], 0
    for a, count in zip(lefts, counts):
        wide = a.shape[1] // count
        place = lambda i, done=done, count=count: jnp.clip(i - done, 0, count - 1)
        ins.append((a, pl.BlockSpec((length, wide), lambda i, f=place: (0, f(i)))))
        outs.append(((a.shape[1], d), BF16, pl.BlockSpec((wide, d), lambda i, f=place: (f(i), 0))))
        done += count
    total = sum(a.shape[1] for a in lefts)
    return chain(
        partial(weight_grad_kernel, counts),
        name,
        done,
        ins + [(right, whole(right.shape))],
        outs,
        flops=2 * length * d * total,
        moved=2 * length * (d + total),
    )


def add_kernel(a_ref, b_ref, out_ref):
    out_ref[...] = (a_ref[...].astype(F32) + b_ref[...].astype(F32)).astype(BF16)


def plus(chain, a, b):
    height, d = a.shape
    block = rows(d, height // 2)
    return chain(
        add_kernel, "plus", 2, [(a, block), (b, block)], [(a.shape, BF16, block)],
        flops=height * d, moved=6 * height * d, mib=16,
    )[0]


def choose_kernel(flag_ref, a_ref, b_ref, out_ref):
    out_ref[...] = jnp.where(flag_ref[0] > 0, b_ref[...], a_ref[...])


def choose(chain, flag, a, b):
    height, d = a.shape
    block = rows(d, height // 2)
    return chain(
        choose_kernel, "choose", 2, [(a, block), (b, block)], [(a.shape, BF16, block)],
        scalars=(flag,), flops=height * d, moved=6 * height * d, mib=16,
    )[0]


def assemble_kernel(core_ref, a_ref, b_ref, *rest):
    rest[-1][...] = jnp.where(core_ref[0] == pl.program_id(0), a_ref[...], b_ref[...])


def assemble(chain, core, chunk, length, a, b, so_far):
    height, d = a.shape
    block = whole((height, d))
    anywhere = pl.BlockSpec(memory_space=pl.ANY)
    return chain(
        assemble_kernel, "assemble", 2,
        [(a, block), (b, block)] + ([] if so_far is None else [(so_far, anywhere)]),
        [((length, d), BF16, pl.BlockSpec((height, d), lambda i, *s: (2 * chunk + i, 0)))],
        scalars=(core,), alias=() if so_far is None else ((2, 0),),
        flops=height * d, moved=6 * height * d, mib=16,
    )[0]


def close_output_kernel(core_ref, a_ref, b_ref, x_ref, small_ref, out_ref):
    total = a_ref[...].astype(F32) + b_ref[...].astype(F32)
    biases = small_ref[2:3] + small_ref[3:4]
    out_ref[...] = (x_ref[...].astype(F32) + total + biases).astype(BF16)


def close_grad_kernel(core_ref, a_ref, b_ref, x_ref, stats_ref, g_ref, small_ref, out_ref):
    u = (a_ref[...].astype(F32) + b_ref[...].astype(F32)) * small_ref[0:1]
    mean, inverse = stats_ref[:, 0:1], stats_ref[:, 1:2]
    scaled = (x_ref[...].astype(F32) - mean) * inverse
    back_u = inverse * (
        u
        - jnp.mean(u, axis=-1, keepdims=True)
        - scaled * jnp.mean(u * scaled, axis=-1, keepdims=True)
    )
    out_ref[...] = (g_ref[...].astype(F32) + back_u).astype(BF16)


def close(chain, kernel, name, core, chunk, a, b, own, small):
    height, d = a.shape
    part = height // 2
    block = rows(d, part)

    def mine(n):
        return pl.BlockSpec((part, n), lambda i, core: (2 * (2 * chunk + core[0]) + i, 0))

    return chain(
        kernel, name, 2,
        [(a, block), (b, block)] + [(o, mine(o.shape[1])) for o in own] + [(small, whole(small.shape))],
        [(a.shape, BF16, block)],
        scalars=(core,), flops=4 * height * d, moved=2 * height * d * (3 + len(own)), mib=16,
    )[0]


def swap_cores(value, size):
    return lax.ppermute(value, "tensor", [(i, i ^ 1) for i in range(size)])


def along(value, hops):
    return lax.ppermute(
        value, "tensor", [(2 * a + c, 2 * b + c) for a, b in hops for c in (0, 1)]
    )


def flow(chain, size, core, chunk, other, mine, closing, results, key, length):
    chips = size // 2
    chip = lax.axis_index("tensor") // 2
    distance = jnp.where(chip < chips // 2, chips // 2 - 1 - chip, chip - chips // 2)
    swapped = swap_cores(other, size)
    yield
    total = plus(chain, mine, swapped)
    for s in range(chips // 2 - 1):
        came = along(total, [(s, s + 1), (chips - 1 - s, chips - 2 - s)])
        yield
        total = plus(chain, total, came)
    a, b = chips // 2 - 1, chips // 2
    came = along(total, [(a, b), (b, a)])
    yield
    value = closing(chunk, total, came)
    for s in range(chips // 2 - 1):
        a, b = chips // 2 - 1 - s, chips // 2 + s
        came = along(value, [(a, a - 1), (b, b + 1)])
        yield
        value = choose(chain, (distance == s + 1).astype(jnp.int32)[None], value, came)
    peer = swap_cores(value, size)
    yield
    results[key] = assemble(chain, core, chunk, length, value, peer, results.get(key))


def on_device(
    size,
    inputs,
    segment_ids,
    norm_gain,
    norm_bias,
    qkv_weight,
    qkv_bias,
    out_weight,
    out_bias,
    up_weight,
    up_bias,
    down_weight,
    down_bias,
    cotangent,
):
    x, g, segment_row = inputs[0], cotangent[0], segment_ids[0]
    length, d = x.shape
    width, units = qkv_weight.shape[2], up_weight.shape[1]
    count = lax.axis_size("dp")
    core = (lax.axis_index("tensor") % 2).astype(jnp.int32)[None]

    start = jnp.sum((segment_row[None, :] < segment_row[:, None]).astype(jnp.int32), axis=1)
    small = jnp.stack([norm_gain, norm_bias, out_bias, down_bias] + [norm_gain] * 4).astype(F32)
    wq = qkv_weight.transpose(1, 0, 2)

    chain = Chain()
    normed, stats, q, k, v, hidden, slope, cos_wide, sin_wide = first(
        chain, x, small, wq, qkv_bias, up_weight, up_bias, start
    )
    mixed, log = attend(chain, start, q, k, v)
    parts = branch(chain, core, CHUNKS, mixed, hidden, out_weight, down_weight)

    results, flows = {}, []

    def close_output(chunk, a, b):
        return close(chain, close_output_kernel, "close_output", core, chunk, a, b, [x], small)

    def close_grad(chunk, a, b):
        return close(chain, close_grad_kernel, "close_grad", core, chunk, a, b, [x, stats, g], small)

    def launch(parts, closing, key):
        return [
            flow(chain, size, core, c, parts[c], parts[CHUNKS + c], closing, results, key, length)
            for c in range(CHUNKS)
        ]

    waiting = launch(parts, close_output, "output")
    for f in waiting:
        next(f)

    def advance():
        flows[:] = [f for f in flows if next(f, flows) is None]
        if waiting:
            f = waiting.pop(0)
            next(f)
            flows.append(f)

    def scatter(value):
        return lax.psum_scatter(value, "dp", scatter_dimension=1, tiled=True).astype(F32)

    advance()
    down_grad, out_grad = weight_grad(chain, "weight_grad_g", [hidden, mixed], g)
    down_share, out_share = scatter(down_grad), scatter(out_grad)
    advance()
    pre, gm, delta, g_sums, up_sums = back(chain, g, slope, mixed, out_weight, down_weight)
    advance()
    tiles = length // TILE
    cutoff = (3 * tiles) // 8
    args = (start, log, delta, q, k, v, gm, cos_wide, sin_wide)
    *one, one_sums, totals = attend_back(chain, 0, cutoff, *args, log)
    advance()
    *two, two_sums, _ = attend_back(chain, cutoff, tiles, *args, totals)
    advance()
    packed = [jnp.concatenate([a, b]) for a, b in zip(one, two)]
    *parts, norm_sums = normed_back(chain, core, CHUNKS, *packed, pre, x, stats, wq, up_weight)
    waiting += launch(parts, close_grad, "grad")
    for f in waiting:
        next(f)
    advance()
    up_grad, *qkv_grads = weight_grad(chain, "weight_grad_n", [pre] + packed, normed)
    up_share = scatter(up_grad).T
    qkv_share = scatter(jnp.concatenate(qkv_grads)).reshape(3, width, d // count).transpose(2, 0, 1)
    while flows:
        advance()

    hop = 1
    while hop < size:
        norm_sums = norm_sums + lax.ppermute(norm_sums, "tensor", [(i, i ^ hop) for i in range(size)])
        hop *= 2
    by_share = lambda a: a.reshape(-1, count, HD // count).swapaxes(0, 1).reshape(count, -1)
    narrow = jnp.concatenate([by_share(up_sums[0]), by_share((one_sums + two_sums)[:3])], axis=1)
    narrow = jnp.pad(narrow, ((0, 0), (0, d // count - narrow.shape[1]))).reshape(1, d)
    vectors = jnp.concatenate([g_sums[:1], narrow, norm_sums[:2], jnp.zeros((12, d), F32)])
    vectors = scatter(vectors.astype(BF16))
    up_b_share = vectors[1, : units // count].reshape(-1, HD // count)
    qkv_b_share = vectors[1, units // count : (units + 3 * width) // count].reshape(3, -1, HD // count)

    return (
        results["output"][None],
        results["grad"][None],
        vectors[2],
        vectors[3],
        qkv_share,
        qkv_b_share,
        out_share,
        vectors[0],
        up_share,
        up_b_share,
        down_share,
        vectors[0],
    )


def solution(mesh):
    placed = (
        P("dp", None, None),
        P("dp", None),
        P(),
        P(),
        P(None, None, "tensor"),
        P(None, "tensor"),
        P("tensor", None),
        P(),
        P(None, "tensor"),
        P("tensor"),
        P("tensor", None),
        P(),
        P("dp", None, None),
    )
    return jax.shard_map(
        partial(on_device, mesh.shape["tensor"]),
        mesh=mesh,
        in_specs=placed,
        out_specs=(
            P("dp", None, None),
            P("dp", None, None),
            P("dp"),
            P("dp"),
            P("dp", None, "tensor"),
            P(None, "tensor", "dp"),
            P("tensor", "dp"),
            P("dp"),
            P("dp", "tensor"),
            P("tensor", "dp"),
            P("tensor", "dp"),
            P("dp"),
        ),
        check_vma=False,
    )
```

```python
from functools import partial

import jax
import jax.numpy as jnp
from jax import lax
from jax.experimental import pallas as pl
from jax.experimental.pallas import tpu as pltpu
from jax.sharding import PartitionSpec as P

HD = 64
ROT = 32
PAIR = 2 * HD
TILE = 256
CHUNKS = 4
NEG = -1e30
MIB = 1 << 20
F32 = jnp.float32
BF16 = jnp.bfloat16


class Chain:
    def __init__(self):
        self.link = jnp.zeros((8, 128), F32)

    def __call__(
        self, kernel, name, grid, ins, outs, scalars=(), scratch=(), alias=(), mib=58, flops=1, collective=None
    ):
        taken, given = len(scalars) + len(ins), len(outs)

        def body(*refs):
            kernel(*refs[:taken], *refs[taken + 1 : taken + 1 + given], *refs[taken + 2 + given :])

        anywhere = pl.BlockSpec(memory_space=pltpu.HBM)
        results = pl.pallas_call(
            body,
            grid_spec=pltpu.PrefetchScalarGridSpec(
                num_scalar_prefetch=len(scalars),
                grid=(grid,),
                in_specs=[spec for _, spec in ins] + [anywhere],
                out_specs=[spec for _, _, spec in outs] + [anywhere],
                scratch_shapes=list(scratch),
            ),
            out_shape=[jax.ShapeDtypeStruct(shape, dtype) for shape, dtype, _ in outs]
            + [jax.ShapeDtypeStruct(self.link.shape, F32)],
            input_output_aliases={taken: given, **{len(scalars) + i: o for i, o in alias}},
            compiler_params=pltpu.CompilerParams(
                dimension_semantics=("arbitrary",), vmem_limit_bytes=mib * MIB,
                collective_id=collective, has_side_effects=collective is not None,
            ),
            cost_estimate=pl.CostEstimate(flops=int(flops), bytes_accessed=1, transcendentals=0),
            name=name,
        )(*scalars, *[array for array, _ in ins], self.link)
        self.link = results[-1]
        return results[:-1]


def whole(shape):
    zeros = (0,) * len(shape)
    return pl.BlockSpec(shape, lambda *i: zeros)


def rows(n, height=TILE):
    return pl.BlockSpec((height, n), lambda i, *s: (i, 0))


def nn(a, b):
    return lax.dot_general(a, b, (((1,), (0,)), ((), ())), preferred_element_type=F32)


def nt(a, b):
    return lax.dot_general(a, b, (((1,), (1,)), ((), ())), preferred_element_type=F32)


def tn(a, b):
    return lax.dot_general(a, b, (((0,), (0,)), ((), ())), preferred_element_type=F32)


def column(row, width):
    return jnp.broadcast_to(row, (width, row.shape[1])).T


def rotated(x, cos_wide, sin_wide):
    lane = lax.broadcasted_iota(jnp.int32, x.shape, 1) % HD
    half = ROT // 2
    other = jnp.where(
        lane < half, pltpu.roll(x, PAIR - half, 1), pltpu.roll(x, half, 1)
    )
    return x * cos_wide + other * sin_wide


def row_stats(x):
    mean = jnp.mean(x, axis=-1, keepdims=True)
    centered = x - mean
    inverse = lax.rsqrt(jnp.mean(centered * centered, axis=-1, keepdims=True) + 1e-05)
    return centered * inverse, mean, inverse


def gelu_both(u):
    c = 0.7978845608028654
    u2 = u * u
    gate = 0.5 + 0.5 * jnp.tanh(u * (c + (c * 0.044715) * u2))
    value = u * gate
    slope = gate + value * (1.0 - gate) * (2.0 * c + (6.0 * c * 0.044715) * u2)
    return value, slope


def first_kernel(
    x0_ref, x1_ref, x2_ref, small_ref, wq_ref, bq_ref, wu_ref, bu_ref, start_ref, freq_ref,
    normed_ref, stats_ref, q_ref, k_ref, v_ref, hidden_ref, slope_ref, cos_ref, sin_ref,
    even, odd, even_stats,
):
    s = pl.program_id(0)
    gain, shift = small_ref[0:1], small_ref[1:2]
    lane = lax.broadcasted_iota(jnp.int32, (TILE, PAIR), 1)

    def norm(x):
        scaled, mean, inverse = row_stats(x.astype(F32))
        return (scaled * gain + shift).astype(BF16), jnp.where(lane == 0, mean, inverse)

    @pl.when(s == 0)
    def _():
        even[...], even_stats[...] = norm(x0_ref[...])

    half = ROT // 2
    unit = lax.broadcasted_iota(jnp.int32, (half, PAIR), 1) % HD
    index = lax.broadcasted_iota(jnp.int32, (half, PAIR), 0)
    first_half = (unit == index).astype(F32)
    second_half = (unit == index + half).astype(F32)
    bias = bq_ref[...].astype(F32)

    def spread(a, b):
        return lax.dot_general(
            a, b, (((0,), (0,)), ((), ())), precision=lax.Precision.HIGHEST,
            preferred_element_type=F32,
        )

    def project(t, normed):
        here = slice(t * TILE, (t + 1) * TILE)
        place = lax.broadcasted_iota(jnp.int32, (1, TILE), 1) + (2 * s + t) * TILE
        angle = freq_ref[...] * (place - start_ref[:, here]).astype(F32)
        cos_wide = spread(jnp.cos(angle), first_half + second_half)
        cos_wide = jnp.where(lane % HD < ROT, cos_wide, 1.0)
        sin_wide = spread(jnp.sin(angle), second_half - first_half)
        cos_ref[here], sin_ref[here] = cos_wide, sin_wide
        for c, out in enumerate((q_ref, k_ref, v_ref)):
            packed = nn(normed, wq_ref[c]) + bias[c : c + 1]
            if c == 2:
                out[here] = packed.astype(BF16)
            else:
                for p in range(packed.shape[1] // PAIR):
                    cut = slice(p * PAIR, (p + 1) * PAIR)
                    turned = rotated(packed[:, cut], cos_wide, sin_wide).astype(BF16)
                    out[here, cut] = turned * (HD**-0.5) if c == 0 else turned
        units = wu_ref.shape[1]
        for n in range(0, units, TILE):
            cut = slice(n, n + TILE)
            value, slope = gelu_both(nn(normed, wu_ref[:, cut]) + bu_ref[:, cut])
            hidden_ref[here, cut] = value.astype(BF16)
            slope_ref[here, cut] = slope.astype(BF16)

    normed = even[...]
    normed_ref[:TILE] = normed
    stats_ref[:TILE] = even_stats[...]
    after, after_stats = norm(x1_ref[...])
    odd[...] = after
    normed_ref[TILE:] = after
    stats_ref[TILE:] = after_stats
    project(0, normed)
    even[...], even_stats[...] = norm(x2_ref[...])
    project(1, odd[...])


def first(chain, x, small, wq, bq, wu, bu, start):
    length, d = x.shape
    width, units = wq.shape[2], wu.shape[1]
    tiles = length // TILE
    freq = 10000.0 ** (-jnp.arange(ROT // 2, dtype=F32) * 2.0 / ROT)
    at = lambda f: pl.BlockSpec((TILE, d), lambda s: (f(s), 0))
    big = lambda n: rows(n, 2 * TILE)
    return chain(
        first_kernel,
        "first",
        tiles // 2,
        [
            (x, at(lambda s: 0)),
            (x, at(lambda s: 2 * s + 1)),
            (x, at(lambda s: jnp.minimum(2 * s + 2, tiles - 1))),
            (small, whole(small.shape)), (wq, whole(wq.shape)), (bq, whole(bq.shape)),
            (wu, whole(wu.shape)), (bu[None].astype(F32), whole((1, units))),
            (start[None], pl.BlockSpec((1, 2 * TILE), lambda s: (0, s))),
            (jnp.broadcast_to(freq[:, None], (ROT // 2, TILE)), whole((ROT // 2, TILE))),
        ],
        [((length, d), BF16, big(d)), ((length, PAIR), F32, big(PAIR))]
        + [((length, n), BF16, big(n)) for n in (width, width, width, units, units)]
        + [((length, PAIR), F32, big(PAIR))] * 2,
        scratch=[pltpu.VMEM((TILE, d), BF16)] * 2 + [pltpu.VMEM((TILE, PAIR), F32)],
    )


def attend_kernel(start_sref, start_ref, q_ref, k_ref, v_ref, mixed_ref, log_ref):
    i = pl.program_id(0)
    pairs = q_ref.shape[1] // PAIR
    left = lax.broadcasted_iota(jnp.int32, (TILE, PAIR), 1) < HD
    zero = jnp.zeros((TILE, PAIR), BF16)
    start = column(start_ref[...], TILE) - lax.broadcasted_iota(jnp.int32, (TILE, TILE), 1)
    ahead = lax.broadcasted_iota(jnp.int32, (TILE, TILE), 0) - lax.broadcasted_iota(
        jnp.int32, (TILE, TILE), 1
    )
    heads = []
    for p in range(pairs):
        q = q_ref[:, p * PAIR : (p + 1) * PAIR]
        heads += [jnp.where(left, q, zero), jnp.where(left, zero, q)]

    def step(j, carry):
        tops, totals, sums = carry
        base = j * TILE
        allowed = (start <= base) & (ahead >= base - i * TILE)
        new_tops, new_totals, new_sums = [], [], []
        for p in range(pairs):
            cut = slice(p * PAIR, (p + 1) * PAIR)
            k = k_ref[pl.ds(pl.multiple_of(base, TILE), TILE), cut]
            v = v_ref[pl.ds(pl.multiple_of(base, TILE), TILE), cut]
            shrink, grown = [], []
            for e in range(2):
                h = 2 * p + e
                s = jnp.where(allowed, nt(heads[h], k), NEG)
                top = jnp.maximum(tops[h], jnp.max(s, axis=1, keepdims=True))
                alpha = jnp.exp(tops[h] - top)
                w = jnp.exp(s - top)
                new_tops.append(top)
                new_totals.append(totals[h] * alpha + jnp.sum(w, axis=1, keepdims=True))
                shrink.append(alpha)
                vh = jnp.where(left, v, zero) if e == 0 else jnp.where(left, zero, v)
                grown.append(nn(w.astype(BF16), vh))
            new_sums.append(sums[p] * jnp.where(left, *shrink) + (grown[0] + grown[1]))
        return tuple(new_tops), tuple(new_totals), tuple(new_sums)

    empty = (
        tuple(jnp.full((TILE, 1), NEG, F32) for _ in range(2 * pairs)),
        tuple(jnp.zeros((TILE, 1), F32) for _ in range(2 * pairs)),
        tuple(jnp.zeros((TILE, PAIR), F32) for _ in range(pairs)),
    )
    low = start_sref[i * TILE] // TILE
    tops, totals, sums = lax.fori_loop(low, i + 1, step, empty)
    lane = lax.broadcasted_iota(jnp.int32, (TILE, PAIR), 1)
    logs = jnp.zeros((TILE, PAIR), F32)
    for p in range(pairs):
        scale = jnp.where(left, 1.0 / totals[2 * p], 1.0 / totals[2 * p + 1])
        mixed_ref[:, p * PAIR : (p + 1) * PAIR] = (sums[p] * scale).astype(BF16)
        for h in (2 * p, 2 * p + 1):
            logs = jnp.where(lane == h, tops[h] + jnp.log(totals[h]), logs)
    log_ref[...] = logs.T[:8]


def attend(chain, start, q, k, v):
    length, width = q.shape
    full = whole((length, width))
    return chain(
        attend_kernel,
        "attend",
        length // TILE,
        [
            (start[None], pl.BlockSpec((1, TILE), lambda i, *s: (0, i))),
            (q, rows(width)), (k, full), (v, full),
        ],
        [
            ((length, width), BF16, rows(width)),
            ((8, length), F32, pl.BlockSpec((8, TILE), lambda i, *s: (0, i))),
        ],
        scalars=(start,),
    )


def attend_back_kernel(
    begin, start_sref, start_ref, log_ref, delta_ref, q_ref, k_ref, v_ref, g_ref, cos_ref, sin_ref,
    totals_in, *refs,
):
    gq_ref, gk_ref, gv_ref, bias_ref, totals = refs[-5:]
    j = pl.program_id(0) + begin
    length, width = q_ref.shape
    pairs = width // PAIR
    here = pl.ds(pl.multiple_of(j * TILE, TILE), TILE)

    @pl.when(pl.program_id(0) == 0)
    def _():
        totals[...] = totals_in[...] if begin else jnp.zeros_like(totals)
        bias_ref[...] = jnp.zeros_like(bias_ref)

    left = lax.broadcasted_iota(jnp.int32, (TILE, PAIR), 1) < HD
    zero = jnp.zeros((TILE, PAIR), BF16)
    key_place = j * TILE + lax.broadcasted_iota(jnp.int32, (TILE, TILE), 0)
    ahead = lax.broadcasted_iota(jnp.int32, (TILE, TILE), 1) - lax.broadcasted_iota(
        jnp.int32, (TILE, TILE), 0
    )

    def halves(x):
        return jnp.where(left, x, zero), jnp.where(left, zero, x)

    keys = [k_ref[here, p * PAIR : (p + 1) * PAIR] for p in range(pairs)]
    split = [halves(k) for k in keys]
    values = [v_ref[here, p * PAIR : (p + 1) * PAIR] for p in range(pairs)]

    def step(i, carry):
        gks, gvs = carry
        there = pl.ds(pl.multiple_of(i * TILE, TILE), TILE)
        allowed = (key_place >= start_ref[:, there]) & (ahead >= (j - i) * TILE)
        new_gk, new_gv = [], []
        for p in range(pairs):
            cut = slice(p * PAIR, (p + 1) * PAIR)
            qs = halves(q_ref[there, cut])
            gs = halves(g_ref[there, cut])
            gk, gv = gks[p], gvs[p]
            gq = totals[there, cut]
            for e in range(2):
                h = 2 * p + e
                s = nt(keys[p], qs[e]) - log_ref[h : h + 1, there]
                w = jnp.exp(jnp.where(allowed, s, NEG))
                gp = nt(values[p], gs[e])
                ds = (w * (gp - delta_ref[h : h + 1, there])).astype(BF16)
                gv = gv + nn(w.astype(BF16), gs[e])
                gk = gk + nn(ds, qs[e])
                gq = gq + tn(ds, split[p][e])
            totals[there, cut] = gq
            new_gk.append(gk)
            new_gv.append(gv)
        return tuple(new_gk), tuple(new_gv)

    high = sum((start_sref[b * TILE] < (j + 1) * TILE).astype(jnp.int32) for b in range(length // TILE))
    empty = tuple(jnp.zeros((TILE, PAIR), F32) for _ in range(pairs))
    gks, gvs = lax.fori_loop(j, high, step, (empty, empty))
    cos_wide, sin_wide = cos_ref[...], -sin_ref[...]
    for p in range(pairs):
        cut = slice(p * PAIR, (p + 1) * PAIR)
        gq = rotated(totals[here, cut] * (HD**-0.5), cos_wide, sin_wide).astype(BF16)
        gk = rotated(gks[p], cos_wide, sin_wide).astype(BF16)
        gv = gvs[p].astype(BF16)
        for c, (g, out) in enumerate(((gq, gq_ref), (gk, gk_ref), (gv, gv_ref))):
            out[:, cut] = g
            bias_ref[c : c + 1, cut] += jnp.sum(g.astype(F32), axis=0, keepdims=True)


def attend_back(chain, begin, end, start, log, delta, q, k, v, g, cos_wide, sin_wide, before):
    length, width = q.shape
    full = whole((length, width))
    shifted = lambda n: pl.BlockSpec((TILE, n), lambda i, *s: (i + begin, 0))
    anywhere = pl.BlockSpec(memory_space=pl.ANY)
    so_far = before[:3] if begin else []
    return chain(
        partial(attend_back_kernel, begin),
        f"attend_back_{begin}",
        end - begin,
        [
            (start[None], whole((1, length))), (log, whole((8, length))), (delta, whole((8, length))),
            (q, full), (k, full), (v, full), (g, full), (cos_wide, shifted(PAIR)), (sin_wide, shifted(PAIR)),
            (before[-1], full if begin else anywhere),
        ]
        + [(a, anywhere) for a in so_far],
        [((length, width), BF16, shifted(width))] * 3
        + [((8, width), F32, whole((8, width))), ((length, width), F32, full)],
        scalars=(start,),
        alias=tuple((10 + n, n) for n in range(len(so_far))),
    )


def place_of(chunk, core):
    return 4 * (chunk // 2) + 2 * core + chunk % 2


def own_rows(chunks, half):
    def spec(n):
        def index(i):
            core = lax.rem(lax.axis_index("tensor"), 2)
            steps = chunks // 2
            return (2 * lax.rem(i, steps) + jnp.where(i < steps, 1 - core, core), 0)

        return pl.BlockSpec((2 * half, n), index)

    return spec


def paired(product, chunks, ins, *refs):
    given, extra, sums, sent, came, send_sem, recv_sem = (
        refs[:ins], refs[ins : len(refs) - chunks - 4], refs[-chunks - 4 : -4], *refs[-4:]
    )
    i = pl.program_id(0)
    steps = chunks // 2
    half = sums[0].shape[0]
    d = sums[0].shape[1]
    me = lax.axis_index("tensor")
    peer = me + 1 - 2 * lax.rem(me, 2)
    barrier = pltpu.get_barrier_semaphore()

    def copy(n):
        return pltpu.make_async_remote_copy(
            src_ref=sent.at[n], dst_ref=came.at[n], send_sem=send_sem.at[n], recv_sem=recv_sem.at[n],
            device_id={"tensor": peer}, device_id_type=pl.DeviceIdType.MESH,
        )

    @pl.when(i == 0)
    def _():
        pl.semaphore_signal(
            barrier, inc=1, device_id={"tensor": peer}, device_id_type=pl.DeviceIdType.MESH
        )
        for e in extra:
            e[...] = jnp.zeros_like(e)

    for n in range(steps):

        @pl.when(i == n)
        def _(n=n):
            for cut in range(0, d, 2 * TILE):
                cut = slice(cut, cut + 2 * TILE)
                total = product(cut, given, extra).astype(BF16)
                sent[2 * n, :, cut] = total[:half]
                sent[2 * n + 1, :, cut] = total[half:]
            if n == 0:
                pl.semaphore_wait(barrier, 1)
            copy(2 * n).start()
            copy(2 * n + 1).start()

        @pl.when(i == steps + n)
        def _(n=n):
            copy(2 * n).wait()
            copy(2 * n + 1).wait()
            for cut in range(0, d, 2 * TILE):
                cut = slice(cut, cut + 2 * TILE)
                total = product(cut, given, extra)
                sums[2 * n][:, cut] = (total[:half] + came[2 * n, :, cut].astype(F32)).astype(BF16)
                sums[2 * n + 1][:, cut] = (
                    total[half:] + came[2 * n + 1, :, cut].astype(F32)
                ).astype(BF16)


def pair_call(chain, product, name, collective, chunks, half, d, ins, extra):
    return chain(
        partial(paired, product, chunks, len(ins)),
        name,
        chunks,
        ins,
        extra + [((half, d), BF16, whole((half, d)))] * chunks,
        scratch=[pltpu.VMEM((chunks, half, d), BF16)] * 2 + [pltpu.SemaphoreType.DMA((chunks,))] * 2,
        collective=collective,
    )


def branch_product(cut, given, extra):
    mixed, hidden, wo, wd = given
    return nn(mixed[...], wo[:, cut]) + nn(hidden[...], wd[:, cut])


def branch(chain, chunks, mixed, hidden, wo, wd):
    length, d = mixed.shape[0], wo.shape[1]
    half = length // (2 * chunks)
    spec = own_rows(chunks, half)
    ins = [
        (mixed, spec(mixed.shape[1])), (hidden, spec(hidden.shape[1])),
        (wo, whole(wo.shape)), (wd, whole(wd.shape)),
    ]
    return pair_call(chain, branch_product, "branch", 1, chunks, half, d, ins, [])


def back_kernel(g_ref, slope_ref, mixed_ref, wo_ref, wd_ref, pre_ref, gm_ref, delta_ref, sums_ref, up_ref):
    @pl.when(pl.program_id(0) == 0)
    def _():
        sums_ref[...] = jnp.zeros_like(sums_ref)
        up_ref[...] = jnp.zeros_like(up_ref)

    g = g_ref[...]
    for n in range(0, wd_ref.shape[0], TILE):
        cut = slice(n, n + TILE)
        pre = (nt(g, wd_ref[cut]) * slope_ref[:, cut].astype(F32)).astype(BF16)
        pre_ref[:, cut] = pre
        up_ref[0:1, cut] += jnp.sum(pre.astype(F32), axis=0, keepdims=True)
    gm = nt(g, wo_ref[...]).astype(BF16)
    gm_ref[...] = gm
    product = gm.astype(F32) * mixed_ref[...].astype(F32)
    coarse = product.astype(BF16)
    fine = (product - coarse.astype(F32)).astype(BF16)
    width = gm.shape[1]
    pick = (
        lax.broadcasted_iota(jnp.int32, (8, width), 1) // HD
        == lax.broadcasted_iota(jnp.int32, (8, width), 0)
    ).astype(BF16)
    delta_ref[...] = nt(pick, coarse) + nt(pick, fine)
    sums_ref[0:1] += jnp.sum(g.astype(F32), axis=0, keepdims=True)


def back(chain, g, slope, mixed, wo, wd):
    length, d = g.shape
    width, units = wo.shape[0], wd.shape[0]
    return chain(
        back_kernel,
        "back",
        length // TILE,
        [
            (g, rows(d)), (slope, rows(units)), (mixed, rows(width)),
            (wo, whole(wo.shape)), (wd, whole(wd.shape)),
        ],
        [
            ((length, units), BF16, rows(units)), ((length, width), BF16, rows(width)),
            ((8, length), F32, pl.BlockSpec((8, TILE), lambda i, *s: (0, i))),
            ((8, d), F32, whole((8, d))), ((8, units), F32, whole((8, units))),
        ],
    )


def normed_back_product(cut, given, extra):
    gq, gk, gv, pre, x, stats, wq, wu = given
    (sums,) = extra
    total = nt(pre[...], wu[cut])
    for c, g in enumerate((gq, gk, gv)):
        total = total + nt(g[...], wq[c, cut])
    scaled = (x[:, cut].astype(F32) - stats[:, 0:1]) * stats[:, 1:2]
    sums[0:1, cut] += jnp.sum(total * scaled, axis=0, keepdims=True)
    sums[1:2, cut] += jnp.sum(total, axis=0, keepdims=True)
    return total


def normed_back(chain, chunks, gq, gk, gv, pre, x, stats, wq, wu):
    length, d = x.shape
    width, units = wq.shape[2], wu.shape[1]
    half = length // (2 * chunks)
    spec = own_rows(chunks, half)
    ins = [(a, spec(width)) for a in (gq, gk, gv)] + [
        (pre, spec(units)), (x, spec(d)), (stats, spec(PAIR)),
        (wq, whole(wq.shape)), (wu, whole(wu.shape)),
    ]
    return pair_call(
        chain, normed_back_product, "normed_back", 2, chunks, half, d, ins,
        [((8, d), F32, whole((8, d)))],
    )


def weight_grad_kernel(counts, *refs):
    *lefts, right, out = refs
    i = pl.program_id(0)
    done = 0
    for left, count in zip(lefts, counts):

        @pl.when((i >= done) & (i < done + count))
        def _(left=left):
            out[...] = tn(left[...], right[...]).astype(BF16)

        done += count


def weight_grad(chain, name, lefts, right):
    length, d = right.shape
    wide = min(TILE, *[a.shape[1] for a in lefts])
    counts = tuple(a.shape[1] // wide for a in lefts)
    ins, done = [], 0
    for a, count in zip(lefts, counts):
        place = lambda i, done=done, count=count: jnp.clip(i - done, 0, count - 1)
        ins.append((a, pl.BlockSpec((length, wide), lambda i, f=place: (0, f(i)))))
        done += count
    return chain(
        partial(weight_grad_kernel, counts),
        name,
        done,
        ins + [(right, whole(right.shape))],
        [((done * wide, d), BF16, rows(d, wide))],
    )[0]


def widen_kernel(turned, share_ref, *outs):
    at = 0
    for out, turn in zip(outs, turned):
        if len(out.shape) == 3:
            for c in range(out.shape[0]):
                out[c] = share_ref[at : at + out.shape[2]].astype(F32).T
                at += out.shape[2]
        elif turn:
            out[...] = share_ref[at : at + out.shape[1]].astype(F32).T
            at += out.shape[1]
        else:
            out[...] = share_ref[at : at + out.shape[0]].astype(F32)
            at += out.shape[0]


def widen(chain, share, shapes, turned):
    return chain(
        partial(widen_kernel, turned), "widen", 1, [(share, whole(share.shape))],
        [(shape, F32, whole(shape)) for shape in shapes], mib=32,
    )


def add_kernel(a_ref, b_ref, out_ref):
    out_ref[...] = (a_ref[...].astype(F32) + b_ref[...].astype(F32)).astype(out_ref.dtype)


def plus(chain, a, b):
    block = whole(a.shape)
    return chain(
        add_kernel, "plus", 1, [(a, block), (b, block)], [(a.shape, a.dtype, block)], mib=16
    )[0]


def choose_kernel(flag_ref, a_ref, b_ref, out_ref):
    out_ref[...] = jnp.where(flag_ref[0] > 0, b_ref[...], a_ref[...])


def choose(chain, flag, a, b):
    height, d = a.shape
    block = rows(d, height // 2)
    return chain(
        choose_kernel, "choose", 2, [(a, block), (b, block)], [(a.shape, BF16, block)],
        scalars=(flag,),
    )[0]


def assemble_kernel(core_ref, a_ref, b_ref, *rest):
    rest[-1][...] = jnp.where(core_ref[0] == pl.program_id(0), a_ref[...], b_ref[...])


def assemble(chain, core, chunk, length, a, b, so_far):
    height, d = a.shape
    block = whole((height, d))
    anywhere = pl.BlockSpec(memory_space=pl.ANY)
    return chain(
        assemble_kernel, "assemble", 2,
        [(a, block), (b, block)] + ([] if so_far is None else [(so_far, anywhere)]),
        [((length, d), BF16, pl.BlockSpec((height, d), lambda i, *s: (place_of(chunk, i), 0)))],
        scalars=(core,), alias=() if so_far is None else ((2, 0),), flops=300e9, mib=16,
    )[0]


def close_kernel(closing, core_ref, *refs):
    refs[-1][...] = closing(*refs[:-1])


def close(chain, closing, core, chunk, a, b, own, small):
    height, d = a.shape
    part = height // 2
    block = rows(d, part)

    def mine(n):
        return pl.BlockSpec((part, n), lambda i, core: (2 * place_of(chunk, core[0]) + i, 0))

    return chain(
        partial(close_kernel, closing), "close", 2,
        [(a, block), (b, block)] + [(o, mine(o.shape[1])) for o in own] + [(small, whole(small.shape))],
        [(a.shape, BF16, block)],
        scalars=(core,),
    )[0]


def swap_cores(value, size):
    return lax.ppermute(value, "tensor", [(i, i ^ 1) for i in range(size)])


def along(value, hops):
    return lax.ppermute(
        value, "tensor", [(2 * a + c, 2 * b + c) for a, b in hops for c in (0, 1)]
    )


def ends_kernel(first_leg, last_leg, role_ref, *refs):
    refs = list(refs)
    keep_ref = refs.pop(0) if first_leg else None
    came_ref = refs.pop(0)
    sent_ref = refs.pop(0) if last_leg else None
    if first_leg:
        total_ref = refs.pop(0)
        total_ref[...] = (keep_ref[...].astype(F32) + came_ref[...].astype(F32)).astype(BF16)
    if last_leg:
        (done_ref,) = refs
        done_ref[...] = jnp.where(role_ref[1] > 0, sent_ref[...], came_ref[...])


def ends(chain, role, keep, came, sent):
    height, d = came.shape
    block = rows(d, height // 2)
    ins = [a for a in (keep, came, sent) if a is not None]
    legs = (keep is not None, sent is not None)
    return chain(
        partial(ends_kernel, *legs), "ends", 2,
        [(a, block) for a in ins], [(came.shape, BF16, block)] * sum(legs), scalars=(role,), mib=16,
    )


def send_kernel(closing, fresh, role_ref, *refs):
    *taken, send_ref = refs
    if not fresh:
        send_ref[...] = closing(*taken)
        return

    @pl.when(role_ref[1] == 0)
    def _():
        send_ref[...] = taken[0][...]

    @pl.when(role_ref[1] > 0)
    def _():
        send_ref[...] = closing(*taken[1:])


def send(chain, role, fresh, closing, chunk, total, came, own, small):
    height, d = total.shape
    part = height // 2
    block = rows(d, part)

    def here(n):
        return pl.BlockSpec((part, n), lambda i, role: (2 * place_of(chunk, role[0]) + i, 0))

    ins = [(a, block) for a in ([] if fresh is None else [fresh]) + [total, came]]
    ins += [(o, here(o.shape[1])) for o in own] + [(small, whole(small.shape))]
    return chain(
        partial(send_kernel, closing, fresh is not None), "send", 2, ins,
        [((height, d), BF16, block)], scalars=(role,), mib=24,
    )[0]


def output_rows(a_ref, b_ref, x_ref, small_ref):
    total = a_ref[...].astype(F32) + b_ref[...].astype(F32)
    biases = small_ref[2:3] + small_ref[3:4]
    return (x_ref[...].astype(F32) + total + biases).astype(BF16)


def grad_rows(a_ref, b_ref, x_ref, stats_ref, g_ref, small_ref):
    u = (a_ref[...].astype(F32) + b_ref[...].astype(F32)) * small_ref[0:1]
    mean, inverse = stats_ref[:, 0:1], stats_ref[:, 1:2]
    scaled = (x_ref[...].astype(F32) - mean) * inverse
    back_u = inverse * (
        u
        - jnp.mean(u, axis=-1, keepdims=True)
        - scaled * jnp.mean(u * scaled, axis=-1, keepdims=True)
    )
    return (g_ref[...].astype(F32) + back_u).astype(BF16)


LAG = 3


class Line:
    OUTER = ((0, 1), (1, 0), (2, 3), (3, 2))
    MIDDLE = ((1, 2), (2, 1))

    def __init__(self, chain, size, role, results, length):
        self.chain, self.size, self.role = chain, size, role
        self.results, self.length = results, length
        self.chunks, self.sent, self.came = [], [], []
        self.totals, self.middle, self.rows = [], [], []

    def add(self, sums, closing, own, small, key):
        self.chunks += [(s, closing, c, own, small, key) for c, s in enumerate(sums)]

    def send(self, n):
        sent = self.chunks[n][0] if n < len(self.chunks) else None
        if n >= LAG:
            _, closing, chunk, own, small, _ = self.chunks[n - LAG]
            sent = send(
                self.chain, self.role, sent, closing, chunk,
                self.totals[n - LAG], self.middle[n - LAG], own, small,
            )
        self.sent.append(sent)
        self.came.append(along(sent, self.OUTER))

    def take(self, n, last):
        out = ends(
            self.chain, self.role, self.chunks[n][0] if n < last else None, self.came[n],
            self.sent[n] if n >= LAG else None,
        )
        if n < last:
            self.totals.append(out[0])
            self.middle.append(along(out[0], self.MIDDLE))
        if n >= LAG:
            self.rows.append((out[-1], swap_cores(out[-1], self.size)))

    def place(self, c):
        mine, other = self.rows[c]
        _, _, chunk, _, _, key = self.chunks[c]
        self.results[key] = assemble(
            self.chain, self.role, chunk, self.length, mine, other, self.results.get(key)
        )


def flow(chain, size, core, chunk, total, closing, results, key, length):
    chips = size // 2
    chip = lax.axis_index("tensor") // 2
    distance = jnp.where(chip < chips // 2, chips // 2 - 1 - chip, chip - chips // 2)
    for s in range(chips // 2 - 1):
        came = along(total, [(s, s + 1), (chips - 1 - s, chips - 2 - s)])
        yield
        total = plus(chain, total, came)
    a, b = chips // 2 - 1, chips // 2
    came = along(total, [(a, b), (b, a)])
    yield
    value = closing(chunk, total, came)
    for s in range(chips // 2 - 1):
        a, b = chips // 2 - 1 - s, chips // 2 + s
        came = along(value, [(a, a - 1), (b, b + 1)])
        yield
        value = choose(chain, (distance == s + 1).astype(jnp.int32)[None], value, came)
    peer = swap_cores(value, size)
    yield
    results[key] = assemble(chain, core, chunk, length, value, peer, results.get(key))


def on_device(
    size,
    inputs,
    segment_ids,
    norm_gain,
    norm_bias,
    qkv_weight,
    qkv_bias,
    out_weight,
    out_bias,
    up_weight,
    up_bias,
    down_weight,
    down_bias,
    cotangent,
):
    x, g, segment_row = inputs[0], cotangent[0], segment_ids[0]
    length, d = x.shape
    width, units = qkv_weight.shape[2], up_weight.shape[1]
    count = lax.axis_size("dp")
    core = (lax.axis_index("tensor") % 2).astype(jnp.int32)[None]

    start = jnp.sum((segment_row[None, :] < segment_row[:, None]).astype(jnp.int32), axis=1)
    small = jnp.stack([norm_gain, norm_bias, out_bias, down_bias] + [norm_gain] * 4).astype(F32)
    wq = qkv_weight.transpose(1, 0, 2)

    chain = Chain()
    normed, stats, q, k, v, hidden, slope, cos_wide, sin_wide = first(
        chain, x, small, wq, qkv_bias, up_weight, up_bias, start
    )
    mixed, log = attend(chain, start, q, k, v)
    parts = branch(chain, CHUNKS, mixed, hidden, out_weight, down_weight)

    results = {}
    four = size == 8
    middle = (lax.axis_index("tensor") // 2 + 1) // 2 == 1
    role = jnp.stack([core[0], middle.astype(jnp.int32)])
    line = Line(chain, size, role, results, length)

    def summed(parts, closing, own, key):
        if four:
            line.add(parts, closing, own, small, key)
            return
        finish = lambda chunk, a, b: close(chain, closing, core, chunk, a, b, own, small)
        flows = [
            flow(chain, size, core, c, parts[c], finish, results, key, length)
            for c in range(CHUNKS)
        ]
        while flows:
            flows = [f for f in flows if next(f, flows) is None]

    last = 2 * CHUNKS

    def step(n, send_next=True):
        if four:
            line.take(n, last)
            if send_next:
                line.send(n + LAG - 1)
            if n >= LAG + 1:
                line.place(n - LAG - 1)

    def scatter(value):
        return lax.psum_scatter(value, "dp", scatter_dimension=1, tiled=True)

    stay = lambda a: pltpu.with_memory_space_constraint(a, pltpu.HBM)
    summed(parts, output_rows, [stay(x)], "output")
    if four:
        for n in range(LAG - 1):
            line.send(n)
    pre, gm, delta, g_sums, up_sums = back(chain, g, slope, mixed, out_weight, down_weight)
    step(0)
    tiles = length // TILE
    cutoff = (3 * tiles) // 8
    args = (start, log, delta, q, k, v, gm, cos_wide, sin_wide)
    one = attend_back(chain, 0, cutoff, *args, [log])
    step(1)
    two = attend_back(chain, cutoff, tiles, *args, one)
    packed, qkv_sums = two[:3], one[3] + two[3]
    step(2, send_next=False)
    norm_sums, *parts = normed_back(chain, CHUNKS, *packed, pre, x, stats, wq, up_weight)
    summed(parts, grad_rows, [stay(x), stay(stats), stay(g)], "grad")
    if four:
        line.send(LAG + 1)
    step(3)
    near = scatter(weight_grad(chain, "weight_grad_g", [hidden, mixed], g))
    step(4)
    far = scatter(weight_grad(chain, "weight_grad_n", [pre, *packed], normed))
    by_share = lambda a: a.reshape(-1, count, HD // count).swapaxes(0, 1).reshape(count, -1)
    narrow = jnp.concatenate([by_share(up_sums[0]), by_share(qkv_sums[:3])], axis=1)
    narrow = jnp.pad(narrow, ((0, 0), (0, d // count - narrow.shape[1]))).reshape(1, d)
    hops = [(n, "tensor", size) for n in range(size.bit_length() - 1)]
    hops += [(n, "dp", count) for n in range(count.bit_length() - 1)]
    vectors = norm_sums
    for n in range(5, max(last + LAG, 5 + len(hops))):
        if hops:
            bit, axis, extent = hops.pop(0)
            if axis == "dp" and bit == 0:
                vectors = jnp.concatenate([vectors[:2], g_sums[:1], narrow, jnp.zeros((4, d), F32)])
            pairs = [(i, i ^ (1 << bit)) for i in range(extent)]
            vectors = plus(chain, vectors, lax.ppermute(vectors, axis, pairs))
        if n < last + LAG:
            step(n, n + LAG - 1 < last + LAG)
        if n == last + LAG - 3:
            part = d // count
            down_share, out_share = widen(chain, near, [(units, part), (width, part)], (False, False))
    up_share, qkv_share = widen(chain, far, [(part, units), (3, part, width)], (True, True))
    if four:
        line.place(last - 1)
    vectors = lax.dynamic_slice_in_dim(vectors, lax.axis_index("dp") * (d // count), d // count, 1)
    up_b_share = vectors[3, : units // count].reshape(-1, HD // count)
    qkv_b_share = vectors[3, units // count : (units + 3 * width) // count].reshape(3, -1, HD // count)

    return (
        results["output"][None],
        results["grad"][None],
        vectors[0],
        vectors[1],
        qkv_share.transpose(1, 0, 2),
        qkv_b_share,
        out_share,
        vectors[2],
        up_share,
        up_b_share,
        down_share,
        vectors[2],
    )


def solution(mesh):
    placed = (
        P("dp", None, None),
        P("dp", None),
        P(),
        P(),
        P(None, None, "tensor"),
        P(None, "tensor"),
        P("tensor", None),
        P(),
        P(None, "tensor"),
        P("tensor"),
        P("tensor", None),
        P(),
        P("dp", None, None),
    )
    return jax.shard_map(
        partial(on_device, mesh.shape["tensor"]),
        mesh=mesh,
        in_specs=placed,
        out_specs=(
            P("dp", None, None),
            P("dp", None, None),
            P("dp"),
            P("dp"),
            P("dp", None, "tensor"),
            P(None, "tensor", "dp"),
            P("tensor", "dp"),
            P("dp"),
            P("dp", "tensor"),
            P("tensor", "dp"),
            P("tensor", "dp"),
            P("dp"),
        ),
        check_vma=False,
    )
```

```python
from functools import partial

import jax
import jax.numpy as jnp
from jax import lax
from jax.experimental import pallas as pl
from jax.experimental.pallas import tpu as pltpu
from jax.sharding import PartitionSpec as P

HD = 64
ROT = 32
PAIR = 2 * HD
TILE = 256
CHUNKS = 4
NEG = -1e30
MIB = 1 << 20
F32 = jnp.float32
BF16 = jnp.bfloat16


class Chain:
    def __init__(self):
        self.link = jnp.zeros((8, 128), F32)

    def __call__(
        self, kernel, name, grid, ins, outs, scalars=(), scratch=(), alias=(), mib=58, flops=1, collective=None
    ):
        taken, given = len(scalars) + len(ins), len(outs)

        def body(*refs):
            kernel(*refs[:taken], *refs[taken + 1 : taken + 1 + given], *refs[taken + 2 + given :])

        anywhere = pl.BlockSpec(memory_space=pltpu.HBM)
        results = pl.pallas_call(
            body,
            grid_spec=pltpu.PrefetchScalarGridSpec(
                num_scalar_prefetch=len(scalars),
                grid=(grid,),
                in_specs=[spec for _, spec in ins] + [anywhere],
                out_specs=[spec for _, _, spec in outs] + [anywhere],
                scratch_shapes=list(scratch),
            ),
            out_shape=[jax.ShapeDtypeStruct(shape, dtype) for shape, dtype, _ in outs]
            + [jax.ShapeDtypeStruct(self.link.shape, F32)],
            input_output_aliases={taken: given, **{len(scalars) + i: o for i, o in alias}},
            compiler_params=pltpu.CompilerParams(
                dimension_semantics=("arbitrary",), vmem_limit_bytes=mib * MIB,
                collective_id=collective, has_side_effects=collective is not None,
            ),
            cost_estimate=pl.CostEstimate(flops=int(flops), bytes_accessed=1, transcendentals=0),
            name=name,
        )(*scalars, *[array for array, _ in ins], self.link)
        self.link = results[-1]
        return results[:-1]


def whole(shape):
    zeros = (0,) * len(shape)
    return pl.BlockSpec(shape, lambda *i: zeros)


def rows(n, height=TILE):
    return pl.BlockSpec((height, n), lambda i, *s: (i, 0))


def nn(a, b):
    return lax.dot_general(a, b, (((1,), (0,)), ((), ())), preferred_element_type=F32)


def nt(a, b):
    return lax.dot_general(a, b, (((1,), (1,)), ((), ())), preferred_element_type=F32)


def tn(a, b):
    return lax.dot_general(a, b, (((0,), (0,)), ((), ())), preferred_element_type=F32)


def rotated(x, cos_wide, sin_wide):
    lane = lax.broadcasted_iota(jnp.int32, x.shape, 1) % HD
    half = ROT // 2
    other = jnp.where(
        lane < half, pltpu.roll(x, PAIR - half, 1), pltpu.roll(x, half, 1)
    )
    return x * cos_wide + other * sin_wide


def row_stats(x):
    mean = jnp.mean(x, axis=-1, keepdims=True)
    centered = x - mean
    inverse = lax.rsqrt(jnp.mean(centered * centered, axis=-1, keepdims=True) + 1e-05)
    return centered * inverse, mean, inverse


def gelu_both(u):
    c = 0.7978845608028654
    u2 = u * u
    gate = 0.5 + 0.5 * jnp.tanh(u * (c + (c * 0.044715) * u2))
    value = u * gate
    slope = gate + value * (1.0 - gate) * (2.0 * c + (6.0 * c * 0.044715) * u2)
    return value, slope


def first_kernel(
    x0_ref, x1_ref, x2_ref, small_ref, wq_ref, bq_ref, wu_ref, bu_ref, start_ref, freq_ref,
    normed_ref, stats_ref, q_ref, k_ref, v_ref, hidden_ref, slope_ref, cos_ref, sin_ref,
    even, odd, even_stats,
):
    s = pl.program_id(0)
    gain, shift = small_ref[0:1], small_ref[1:2]
    lane = lax.broadcasted_iota(jnp.int32, (TILE, PAIR), 1)

    def norm(x):
        scaled, mean, inverse = row_stats(x.astype(F32))
        return (scaled * gain + shift).astype(BF16), jnp.where(lane == 0, mean, inverse)

    @pl.when(s == 0)
    def _():
        even[...], even_stats[...] = norm(x0_ref[...])

    half = ROT // 2
    unit = lax.broadcasted_iota(jnp.int32, (half, PAIR), 1) % HD
    index = lax.broadcasted_iota(jnp.int32, (half, PAIR), 0)
    first_half = (unit == index).astype(F32)
    second_half = (unit == index + half).astype(F32)
    bias = bq_ref[...].astype(F32)

    def spread(a, b):
        return lax.dot_general(
            a, b, (((0,), (0,)), ((), ())), precision=lax.Precision.HIGHEST,
            preferred_element_type=F32,
        )

    def project(t, normed):
        here = slice(t * TILE, (t + 1) * TILE)
        place = lax.broadcasted_iota(jnp.int32, (1, TILE), 1) + (2 * s + t) * TILE
        angle = freq_ref[...] * (place - start_ref[:, here]).astype(F32)
        cos_wide = spread(jnp.cos(angle), first_half + second_half)
        cos_wide = jnp.where(lane % HD < ROT, cos_wide, 1.0)
        sin_wide = spread(jnp.sin(angle), second_half - first_half)
        cos_ref[here], sin_ref[here] = cos_wide, sin_wide
        for c, out in enumerate((q_ref, k_ref, v_ref)):
            packed = nn(normed, wq_ref[c]) + bias[c : c + 1]
            if c == 2:
                out[here] = packed.astype(BF16)
            else:
                for p in range(packed.shape[1] // PAIR):
                    cut = slice(p * PAIR, (p + 1) * PAIR)
                    turned = rotated(packed[:, cut], cos_wide, sin_wide).astype(BF16)
                    out[here, cut] = turned * (HD**-0.5) if c == 0 else turned
        units = wu_ref.shape[1]
        for n in range(0, units, TILE):
            cut = slice(n, n + TILE)
            value, slope = gelu_both(nn(normed, wu_ref[:, cut]) + bu_ref[:, cut])
            hidden_ref[here, cut] = value.astype(BF16)
            slope_ref[here, cut] = slope.astype(BF16)

    normed = even[...]
    normed_ref[:TILE] = normed
    stats_ref[:TILE] = even_stats[...]
    after, after_stats = norm(x1_ref[...])
    odd[...] = after
    normed_ref[TILE:] = after
    stats_ref[TILE:] = after_stats
    project(0, normed)
    even[...], even_stats[...] = norm(x2_ref[...])
    project(1, odd[...])


def first(chain, x, small, wq, bq, wu, bu, start):
    length, d = x.shape
    width, units = wq.shape[2], wu.shape[1]
    tiles = length // TILE
    freq = 10000.0 ** (-jnp.arange(ROT // 2, dtype=F32) * 2.0 / ROT)
    at = lambda f: pl.BlockSpec((TILE, d), lambda s: (f(s), 0))
    big = lambda n: rows(n, 2 * TILE)
    return chain(
        first_kernel,
        "first",
        tiles // 2,
        [
            (x, at(lambda s: 0)),
            (x, at(lambda s: 2 * s + 1)),
            (x, at(lambda s: jnp.minimum(2 * s + 2, tiles - 1))),
            (small, whole(small.shape)), (wq, whole(wq.shape)), (bq, whole(bq.shape)),
            (wu, whole(wu.shape)), (bu[None].astype(F32), whole((1, units))),
            (start[None], pl.BlockSpec((1, 2 * TILE), lambda s: (0, s))),
            (jnp.broadcast_to(freq[:, None], (ROT // 2, TILE)), whole((ROT // 2, TILE))),
        ],
        [((length, d), BF16, big(d)), ((length, PAIR), F32, big(PAIR))]
        + [((length, n), BF16, big(n)) for n in (width, width, width, units, units)]
        + [((length, PAIR), F32, big(PAIR))] * 2,
        scratch=[pltpu.VMEM((TILE, d), BF16)] * 2 + [pltpu.VMEM((TILE, PAIR), F32)],
    )


def halves(x):
    left = lax.broadcasted_iota(jnp.int32, x.shape, 1) < HD
    zero = jnp.zeros(x.shape, x.dtype)
    return [jnp.where(left, x, zero), jnp.where(left, zero, x)]


def pair_cuts(width):
    return [slice(p, p + PAIR) for p in range(0, width, PAIR)]


def attend_kernel(start_sref, start_ref, q_ref, k_ref, v_ref, mixed_ref, log_ref):
    i = pl.program_id(0)
    cuts = pair_cuts(q_ref.shape[1])
    heads = range(2 * len(cuts))
    key_row = lax.broadcasted_iota(jnp.int32, (TILE, TILE), 0)
    query = lax.broadcasted_iota(jnp.int32, (TILE, TILE), 1) + i * TILE
    start = start_ref[...]
    queries = [q for cut in cuts for q in halves(q_ref[:, cut])]

    def step(j, carry):
        tops, totals, sums = carry
        there = pl.ds(pl.multiple_of(j * TILE, TILE), TILE)
        place = key_row + j * TILE
        allowed = (place >= start) & (place <= query)
        k = [k_ref[there, cut] for cut in cuts]
        v = [v_ref[there, cut] for cut in cuts]
        s = [nt(k[h // 2], queries[h]) for h in heads]
        s = [jnp.where(allowed, a, NEG) for a in s]
        top = [jnp.maximum(tops[h], jnp.max(s[h], axis=0, keepdims=True)) for h in heads]
        alpha = [jnp.exp(tops[h] - top[h]) for h in heads]
        w = [jnp.exp(s[h] - top[h]) for h in heads]
        totals = [totals[h] * alpha[h] + jnp.sum(w[h], axis=0, keepdims=True) for h in heads]
        w = [a.astype(BF16) for a in w]
        add = [tn(v[h // 2], w[h])[h % 2 * HD : (h % 2 + 1) * HD] for h in heads]
        sums = [sums[h] * alpha[h] + add[h] for h in heads]
        return tuple(top), tuple(totals), tuple(sums)

    empty = (
        tuple(jnp.full((1, TILE), NEG, F32) for _ in heads),
        tuple(jnp.zeros((1, TILE), F32) for _ in heads),
        tuple(jnp.zeros((HD, TILE), F32) for _ in heads),
    )
    low = start_sref[i * TILE] // TILE
    tops, totals, sums = lax.fori_loop(low, i + 1, step, empty)
    log_ref[...] = jnp.zeros_like(log_ref)
    for h in heads:
        log_ref[h : h + 1] = tops[h] + jnp.log(totals[h])
    mixed_ref[...] = jnp.concatenate([sums[h] * (1.0 / totals[h]) for h in heads]).T.astype(BF16)


def attend(chain, start, q, k, v):
    length, width = q.shape
    full = whole((length, width))
    return chain(
        attend_kernel,
        "attend",
        length // TILE,
        [
            (start[None], pl.BlockSpec((1, TILE), lambda i, *s: (0, i))),
            (q, rows(width)), (k, full), (v, full),
        ],
        [
            ((length, width), BF16, rows(width)),
            ((8, length), F32, pl.BlockSpec((8, TILE), lambda i, *s: (0, i))),
        ],
        scalars=(start,),
    )


def attend_back_kernel(
    begin, start_sref, start_ref, log_ref, delta_ref, q_ref, k_ref, v_ref, g_ref, cos_ref, sin_ref,
    totals_in, *refs,
):
    gq_ref, gk_ref, gv_ref, bias_ref, totals = refs[-5:]
    j = pl.program_id(0) + begin
    length, width = q_ref.shape
    cuts = pair_cuts(width)
    heads = range(2 * len(cuts))
    here = pl.ds(pl.multiple_of(j * TILE, TILE), TILE)

    @pl.when(pl.program_id(0) == 0)
    def _():
        totals[...] = totals_in[...] if begin else jnp.zeros_like(totals)
        bias_ref[...] = jnp.zeros_like(bias_ref)

    place = j * TILE + lax.broadcasted_iota(jnp.int32, (TILE, TILE), 0)
    query = lax.broadcasted_iota(jnp.int32, (TILE, TILE), 1)
    keys = [k_ref[here, cut] for cut in cuts]
    split = [half for k in keys for half in halves(k)]
    values = [v_ref[here, cut] for cut in cuts]

    def step(i, carry):
        gk, gv = carry
        there = pl.ds(pl.multiple_of(i * TILE, TILE), TILE)
        allowed = (place >= start_ref[:, there]) & (place <= query + i * TILE)
        qs = [half for cut in cuts for half in halves(q_ref[there, cut])]
        gs = [half for cut in cuts for half in halves(g_ref[there, cut])]
        s = [nt(keys[h // 2], qs[h]) for h in heads]
        gp = [nt(values[h // 2], gs[h]) for h in heads]
        w = [jnp.exp(jnp.where(allowed, s[h] - log_ref[h : h + 1, there], NEG)) for h in heads]
        ds = [(w[h] * (gp[h] - delta_ref[h : h + 1, there])).astype(BF16) for h in heads]
        w = [a.astype(BF16) for a in w]
        both = lambda f: tuple(f(h) + f(h + 1) for h in heads[::2])
        gv = [a + b for a, b in zip(gv, both(lambda h: nn(w[h], gs[h])))]
        gk = [a + b for a, b in zip(gk, both(lambda h: nn(ds[h], qs[h])))]
        for cut, gq in zip(cuts, both(lambda h: tn(ds[h], split[h]))):
            totals[there, cut] += gq
        return tuple(gk), tuple(gv)

    high = sum((start_sref[b * TILE] < (j + 1) * TILE).astype(jnp.int32) for b in range(length // TILE))
    empty = tuple(jnp.zeros((TILE, PAIR), F32) for _ in cuts)
    gks, gvs = lax.fori_loop(j, high, step, (empty, empty))
    cos_wide, sin_wide = cos_ref[...], -sin_ref[...]
    for cut, gk, gv in zip(cuts, gks, gvs):
        gq = rotated(totals[here, cut] * (HD**-0.5), cos_wide, sin_wide).astype(BF16)
        gk = rotated(gk, cos_wide, sin_wide).astype(BF16)
        for c, (g, out) in enumerate(((gq, gq_ref), (gk, gk_ref), (gv.astype(BF16), gv_ref))):
            out[:, cut] = g
            bias_ref[c : c + 1, cut] += jnp.sum(g.astype(F32), axis=0, keepdims=True)


def attend_back(chain, begin, end, start, log, delta, q, k, v, g, cos_wide, sin_wide, before):
    length, width = q.shape
    full = whole((length, width))
    shifted = lambda n: pl.BlockSpec((TILE, n), lambda i, *s: (i + begin, 0))
    anywhere = pl.BlockSpec(memory_space=pl.ANY)
    so_far = before[:3] if begin else []
    return chain(
        partial(attend_back_kernel, begin),
        f"attend_back_{begin}",
        end - begin,
        [
            (start[None], whole((1, length))), (log, whole((8, length))), (delta, whole((8, length))),
            (q, full), (k, full), (v, full), (g, full), (cos_wide, shifted(PAIR)), (sin_wide, shifted(PAIR)),
            (before[-1], full if begin else anywhere),
        ]
        + [(a, anywhere) for a in so_far],
        [((length, width), BF16, shifted(width))] * 3
        + [((8, width), F32, whole((8, width))), ((length, width), F32, full)],
        scalars=(start,),
        alias=tuple((10 + n, n) for n in range(len(so_far))),
    )


def place_of(chunk, core):
    return 4 * (chunk // 2) + 2 * core + chunk % 2


def own_rows(chunks, half):
    def spec(n):
        def index(i):
            core = lax.rem(lax.axis_index("tensor"), 2)
            steps = chunks // 2
            return (2 * lax.rem(i, steps) + jnp.where(i < steps, 1 - core, core), 0)

        return pl.BlockSpec((2 * half, n), index)

    return spec


def paired(product, chunks, ins, *refs):
    given, extra, sums, held, came, send_sem, recv_sem = (
        refs[:ins], refs[ins : len(refs) - chunks - 4], refs[-chunks - 4 : -4], *refs[-4:]
    )
    i = pl.program_id(0)
    steps = chunks // 2
    half, d = sums[0].shape
    me = lax.axis_index("tensor")
    peer = me + 1 - 2 * lax.rem(me, 2)
    barrier = pltpu.get_barrier_semaphore()

    def copy(n):
        return pltpu.make_async_remote_copy(
            src_ref=held.at[n], dst_ref=came.at[n], send_sem=send_sem.at[n], recv_sem=recv_sem.at[n],
            device_id={"tensor": peer}, device_id_type=pl.DeviceIdType.MESH,
        )

    @pl.when(i == 0)
    def _():
        pl.semaphore_signal(
            barrier, inc=1, device_id={"tensor": peer}, device_id_type=pl.DeviceIdType.MESH
        )
        for e in extra:
            e[...] = jnp.zeros_like(e)

    for cut in range(0, d, 2 * TILE):
        cut = slice(cut, cut + 2 * TILE)
        total = product(cut, given, extra).astype(BF16)
        held[pl.ds(2 * i, 2), :, cut] = total.reshape(2, half, 2 * TILE)

    @pl.when(i == 0)
    def _():
        pl.semaphore_wait(barrier, 1)

    for n in range(steps):

        @pl.when(i == n)
        def _(n=n):
            copy(2 * n).start()
            copy(2 * n + 1).start()

        @pl.when(i == steps + n)
        def _(n=n):
            for c in (2 * n, 2 * n + 1):
                copy(c).wait()
                total = held[chunks + c].astype(F32) + came[c].astype(F32)
                sums[c][...] = total.astype(BF16)


def pair_call(chain, product, name, collective, chunks, half, d, ins, extra):
    return chain(
        partial(paired, product, chunks, len(ins)),
        name,
        chunks,
        ins,
        extra + [((half, d), BF16, whole((half, d)))] * chunks,
        scratch=[pltpu.VMEM((2 * chunks, half, d), BF16), pltpu.VMEM((chunks, half, d), BF16)]
        + [pltpu.SemaphoreType.DMA((chunks,))] * 2,
        collective=collective,
    )


def branch_product(cut, given, extra):
    mixed, hidden, wo, wd = given
    return nn(mixed[...], wo[:, cut]) + nn(hidden[...], wd[:, cut])


def branch(chain, chunks, mixed, hidden, wo, wd):
    length, d = mixed.shape[0], wo.shape[1]
    half = length // (2 * chunks)
    spec = own_rows(chunks, half)
    ins = [
        (mixed, spec(mixed.shape[1])), (hidden, spec(hidden.shape[1])),
        (wo, whole(wo.shape)), (wd, whole(wd.shape)),
    ]
    return pair_call(chain, branch_product, "branch", 1, chunks, half, d, ins, [])


def back_kernel(g_ref, slope_ref, mixed_ref, wo_ref, wd_ref, pre_ref, gm_ref, delta_ref, sums_ref, up_ref):
    @pl.when(pl.program_id(0) == 0)
    def _():
        sums_ref[...] = jnp.zeros_like(sums_ref)
        up_ref[...] = jnp.zeros_like(up_ref)

    g = g_ref[...]
    for n in range(0, wd_ref.shape[0], 2 * TILE):
        cut = slice(n, n + 2 * TILE)
        pre = (nt(g, wd_ref[cut]) * slope_ref[:, cut].astype(F32)).astype(BF16)
        pre_ref[:, cut] = pre
        up_ref[0:1, cut] += jnp.sum(pre.astype(F32), axis=0, keepdims=True)
    gm = nt(g, wo_ref[...]).astype(BF16)
    gm_ref[...] = gm
    product = gm.astype(F32) * mixed_ref[...].astype(F32)
    coarse = product.astype(BF16)
    fine = (product - coarse.astype(F32)).astype(BF16)
    width = gm.shape[1]
    pick = (
        lax.broadcasted_iota(jnp.int32, (8, width), 1) // HD
        == lax.broadcasted_iota(jnp.int32, (8, width), 0)
    ).astype(BF16)
    delta_ref[...] = nt(pick, coarse) + nt(pick, fine)
    sums_ref[0:1] += jnp.sum(g.astype(F32), axis=0, keepdims=True)


def back(chain, g, slope, mixed, wo, wd):
    length, d = g.shape
    width, units = wo.shape[0], wd.shape[0]
    big = lambda n: rows(n, 2 * TILE)
    return chain(
        back_kernel,
        "back",
        length // (2 * TILE),
        [
            (g, big(d)), (slope, big(units)), (mixed, big(width)),
            (wo, whole(wo.shape)), (wd, whole(wd.shape)),
        ],
        [
            ((length, units), BF16, big(units)), ((length, width), BF16, big(width)),
            ((8, length), F32, pl.BlockSpec((8, 2 * TILE), lambda i, *s: (0, i))),
            ((8, d), F32, whole((8, d))), ((8, units), F32, whole((8, units))),
        ],
    )


def normed_back_product(cut, given, extra):
    gq, gk, gv, pre, x, stats, wq, wu = given
    (sums,) = extra
    total = nt(pre[...], wu[cut])
    for c, g in enumerate((gq, gk, gv)):
        total = total + nt(g[...], wq[c, cut])
    scaled = (x[:, cut].astype(F32) - stats[:, 0:1]) * stats[:, 1:2]
    sums[0:1, cut] += jnp.sum(total * scaled, axis=0, keepdims=True)
    sums[1:2, cut] += jnp.sum(total, axis=0, keepdims=True)
    return total


def normed_back(chain, chunks, gq, gk, gv, pre, x, stats, wq, wu):
    length, d = x.shape
    width, units = wq.shape[2], wu.shape[1]
    half = length // (2 * chunks)
    spec = own_rows(chunks, half)
    ins = [(a, spec(width)) for a in (gq, gk, gv)] + [
        (pre, spec(units)), (x, spec(d)), (stats, spec(PAIR)),
        (wq, whole(wq.shape)), (wu, whole(wu.shape)),
    ]
    return pair_call(
        chain, normed_back_product, "normed_back", 2, chunks, half, d, ins,
        [((8, d), F32, whole((8, d)))],
    )


def weight_grad_kernel(counts, *refs):
    *lefts, right, out = refs
    i = pl.program_id(0)
    done = 0
    for left, count in zip(lefts, counts):

        @pl.when((i >= done) & (i < done + count))
        def _(left=left):
            out[...] = tn(left[...], right[...]).astype(BF16)

        done += count


def weight_grad(chain, name, lefts, right):
    length, d = right.shape
    wide = min(TILE, *[a.shape[1] for a in lefts])
    counts = tuple(a.shape[1] // wide for a in lefts)
    ins, done = [], 0
    for a, count in zip(lefts, counts):
        place = lambda i, done=done, count=count: jnp.clip(i - done, 0, count - 1)
        ins.append((a, pl.BlockSpec((length, wide), lambda i, f=place: (0, f(i)))))
        done += count
    return chain(
        partial(weight_grad_kernel, counts),
        name,
        done,
        ins + [(right, whole(right.shape))],
        [((done * wide, d), BF16, rows(d, wide))],
    )[0]


def vectors_kernel(size, count, vectors, total, came, part, wide, sems):
    row, me = lax.axis_index("dp"), lax.axis_index("tensor")
    barrier = pltpu.get_barrier_semaphore()
    mesh = pl.DeviceIdType.MESH
    half = part.shape[0] // 2

    def by_row(n):
        peer = lax.rem(row + n, count)
        return pltpu.make_async_remote_copy(
            src_ref=vectors.at[peer], dst_ref=came.at[n], send_sem=sems.at[0, n],
            recv_sem=sems.at[1, n], device_id={"dp": peer}, device_id_type=mesh,
        )

    def by_column(n):
        peer = lax.rem(me + n, size)
        return pltpu.make_async_remote_copy(
            src_ref=part.at[pl.ds(0, half)], dst_ref=wide.at[n], send_sem=sems.at[2, n],
            recv_sem=sems.at[3, n], device_id={"tensor": peer}, device_id_type=mesh,
        )

    for n in range(1, count):
        pl.semaphore_signal(
            barrier, inc=1, device_id={"dp": lax.rem(row + n, count)}, device_id_type=mesh
        )
    for n in range(1, size):
        pl.semaphore_signal(
            barrier, inc=1, device_id={"tensor": lax.rem(me + n, size)}, device_id_type=mesh
        )
    pl.semaphore_wait(barrier, count + size - 2)
    for n in range(1, count):
        by_row(n).start()
    mine = vectors[row]
    for n in range(1, count):
        by_row(n).wait()
        mine = mine + came[n]
    part[...] = mine
    for n in range(1, size):
        by_column(n).start()
    upper = mine[:half]
    for n in range(1, size):
        by_column(n).wait()
        upper = upper + wide[n]
    total[:half] = upper
    total[half:] = mine[half:]


def add_vectors(chain, vectors, size, count):
    small = vectors.shape[1:]
    return chain(
        partial(vectors_kernel, size, count), "add_vectors", 1, [(vectors, whole(vectors.shape))],
        [(small, F32, whole(small))],
        scratch=[
            pltpu.VMEM((count, *small), F32), pltpu.VMEM(small, F32),
            pltpu.VMEM((size, small[0] // 2, small[1]), F32),
            pltpu.SemaphoreType.DMA((4, max(size, count))),
        ],
        collective=6,
    )[0]


def widen_kernel(turned, share_ref, *outs):
    at = 0
    for out, turn in zip(outs, turned):
        if len(out.shape) == 3:
            for c in range(out.shape[0]):
                out[c] = share_ref[at : at + out.shape[2]].astype(F32).T
                at += out.shape[2]
        elif turn:
            out[...] = share_ref[at : at + out.shape[1]].astype(F32).T
            at += out.shape[1]
        else:
            out[...] = share_ref[at : at + out.shape[0]].astype(F32)
            at += out.shape[0]


def widen(chain, share, shapes, turned):
    return chain(
        partial(widen_kernel, turned), "widen", 1, [(share, whole(share.shape))],
        [(shape, F32, whole(shape)) for shape in shapes], mib=32,
    )


def add_kernel(a_ref, b_ref, out_ref):
    out_ref[...] = (a_ref[...].astype(F32) + b_ref[...].astype(F32)).astype(out_ref.dtype)


def plus(chain, a, b):
    block = whole(a.shape)
    return chain(
        add_kernel, "plus", 1, [(a, block), (b, block)], [(a.shape, a.dtype, block)], mib=16
    )[0]


def choose_kernel(flag_ref, a_ref, b_ref, out_ref):
    out_ref[...] = jnp.where(flag_ref[0] > 0, b_ref[...], a_ref[...])


def choose(chain, flag, a, b):
    height, d = a.shape
    block = rows(d, height // 2)
    return chain(
        choose_kernel, "choose", 2, [(a, block), (b, block)], [(a.shape, BF16, block)],
        scalars=(flag,),
    )[0]


def assemble_kernel(core_ref, a_ref, b_ref, *rest):
    rest[-1][...] = jnp.where(core_ref[0] == pl.program_id(0), a_ref[...], b_ref[...])


def assemble(chain, core, chunk, length, a, b, so_far):
    height, d = a.shape
    block = whole((height, d))
    anywhere = pl.BlockSpec(memory_space=pl.ANY)
    return chain(
        assemble_kernel, "assemble", 2,
        [(a, block), (b, block)] + ([] if so_far is None else [(so_far, anywhere)]),
        [((length, d), BF16, pl.BlockSpec((height, d), lambda i, *s: (place_of(chunk, i), 0)))],
        scalars=(core,), alias=() if so_far is None else ((2, 0),), mib=16,
    )[0]


def close_kernel(closing, core_ref, *refs):
    refs[-1][...] = closing(*refs[:-1])


def close(chain, closing, core, chunk, a, b, own, small):
    height, d = a.shape
    part = height // 2
    block = rows(d, part)

    def mine(n):
        return pl.BlockSpec((part, n), lambda i, core: (2 * place_of(chunk, core[0]) + i, 0))

    return chain(
        partial(close_kernel, closing), "close", 2,
        [(a, block), (b, block)] + [(o, mine(o.shape[1])) for o in own] + [(small, whole(small.shape))],
        [(a.shape, BF16, block)],
        scalars=(core,),
    )[0]


def swap_cores(value, size):
    return lax.ppermute(value, "tensor", [(i, i ^ 1) for i in range(size)])


def along(value, hops):
    return lax.ppermute(
        value, "tensor", [(2 * a + c, 2 * b + c) for a, b in hops for c in (0, 1)]
    )


def ends_kernel(first_leg, last_leg, role_ref, *refs):
    refs = list(refs)
    keep_ref = refs.pop(0) if first_leg else None
    came_ref = refs.pop(0)
    sent_ref = refs.pop(0) if last_leg else None
    if first_leg:
        total_ref = refs.pop(0)
        total_ref[...] = (keep_ref[...].astype(F32) + came_ref[...].astype(F32)).astype(BF16)
    if last_leg:
        (done_ref,) = refs
        done_ref[...] = jnp.where(role_ref[1] > 0, sent_ref[...], came_ref[...])


def ends(chain, role, keep, came, sent):
    height, d = came.shape
    block = rows(d, height // 2)
    ins = [a for a in (keep, came, sent) if a is not None]
    legs = (keep is not None, sent is not None)
    return chain(
        partial(ends_kernel, *legs), "ends", 2,
        [(a, block) for a in ins], [(came.shape, BF16, block)] * sum(legs), scalars=(role,), mib=16,
    )


def send_kernel(closing, fresh, role_ref, *refs):
    *taken, send_ref = refs
    if not fresh:
        send_ref[...] = closing(*taken)
        return

    @pl.when(role_ref[1] == 0)
    def _():
        send_ref[...] = taken[0][...]

    @pl.when(role_ref[1] > 0)
    def _():
        send_ref[...] = closing(*taken[1:])


def send(chain, role, fresh, closing, chunk, total, came, own, small):
    height, d = total.shape
    part = height // 2
    block = rows(d, part)

    def here(n):
        return pl.BlockSpec((part, n), lambda i, role: (2 * place_of(chunk, role[0]) + i, 0))

    ins = [(a, block) for a in ([] if fresh is None else [fresh]) + [total, came]]
    ins += [(o, here(o.shape[1])) for o in own] + [(small, whole(small.shape))]
    return chain(
        partial(send_kernel, closing, fresh is not None), "send", 2, ins,
        [((height, d), BF16, block)], scalars=(role,), mib=24,
    )[0]


def output_rows(a_ref, b_ref, x_ref, small_ref):
    total = a_ref[...].astype(F32) + b_ref[...].astype(F32)
    biases = small_ref[2:3] + small_ref[3:4]
    return (x_ref[...].astype(F32) + total + biases).astype(BF16)


def grad_rows(a, b, x, stats, g, small):
    u = (a[...].astype(F32) + b[...].astype(F32)) * small[0:1]
    mean, inverse = stats[:, 0:1], stats[:, 1:2]
    scaled = (x[...].astype(F32) - mean) * inverse
    back_u = inverse * (
        u
        - jnp.mean(u, axis=-1, keepdims=True)
        - scaled * jnp.mean(u * scaled, axis=-1, keepdims=True)
    )
    return (g[...].astype(F32) + back_u).astype(BF16)


PIECE = TILE // 2


def line_kernel(
    gq, gk, gv, pre, x_block, stats_block, wq, wu, small, extra, x_all, g_all, stats_all, *refs
):
    chunks = len(refs) - 28
    parts, refs = refs[:chunks], refs[chunks:]
    output, grad, vectors = refs[:3]
    held, came, own, lines, across, x_own, g_own, stats_own, sums, by_dp, mine, by_tensor = refs[3:15]
    (
        load_sem, part_sem, peer_send, peer_recv, in_send, in_recv, mid_send, mid_recv, out_send, out_recv,
        fin_send, fin_recv, keep_sem,
    ) = refs[15:28]
    i = pl.program_id(0)
    pieces = 2 * chunks
    d = came.shape[2]
    row, me = lax.axis_index("dp"), lax.axis_index("tensor")
    count, size = by_dp.shape[0], by_tensor.shape[0]
    core = lax.rem(me, 2)
    chip = me // 2
    peer = me + 1 - 2 * core
    beside = 2 * (chip + 1 - 2 * lax.rem(chip, 2)) + core
    facing = 2 * (3 - chip) + core
    middle = (chip == 1) | (chip == 2)
    end = jnp.logical_not(middle)
    mesh = pl.DeviceIdType.MESH
    barrier = pltpu.get_barrier_semaphore()

    def remote(source, target, send_sem, recv_sem, device, axis="tensor"):
        return pltpu.make_async_remote_copy(
            src_ref=source, dst_ref=target, send_sem=send_sem, recv_sem=recv_sem,
            device_id={axis: device}, device_id_type=mesh,
        )

    def place(p):
        start = place_of(p // 2, core) * TILE + lax.rem(p, 2) * PIECE
        return pl.ds(pl.multiple_of(start, PIECE), PIECE)

    def peer_copy(c):
        return remote(held.at[c], came.at[c], peer_send.at[c], peer_recv.at[c], peer)

    def in_copy(p):
        return remote(own.at[p], lines.at[p], in_send.at[p], in_recv.at[p], beside)

    def mid_copy(p):
        return remote(own.at[p], across.at[p], mid_send.at[p], mid_recv.at[p], facing)

    def out_copy(p):
        return remote(lines.at[p], lines.at[p], out_send.at[p], out_recv.at[p], beside)

    def fin_copy(p, result, q):
        return remote(lines.at[p], result.at[place(q)], fin_send.at[p], fin_recv.at[p], peer)

    def keep_copy(p, result, q):
        return pltpu.make_async_copy(lines.at[p], result.at[place(q)], keep_sem.at[p])

    def loads(p):
        return [
            pltpu.make_async_copy(array.at[place(p)], here.at[p], load_sem.at[n, p])
            for n, (array, here) in enumerate(((x_all, x_own), (g_all, g_own), (stats_all, stats_own)))
        ]

    def part_copy(c, r):
        p = 2 * c + r
        return pltpu.make_async_copy(
            parts[c].at[pl.ds(r * PIECE, PIECE)], own.at[p], part_sem.at[p]
        )

    def dp_copy(n):
        device = lax.rem(row + n, count)
        wide = d // count
        source = sums.at[:, pl.ds(pl.multiple_of(device * wide, 128), wide)]
        return remote(source, by_dp.at[n], load_sem.at[3, n], load_sem.at[4, n], device, "dp")

    def tensor_copy(n):
        device = lax.rem(me + n, size)
        return remote(mine, by_tensor.at[n], load_sem.at[5, n], load_sem.at[6, n], device)

    def of(p, action):
        @pl.when(p < pieces)
        def _():
            action(p, output, p)

        @pl.when(p >= pieces)
        def _():
            action(p, grad, p - pieces)

    def hand_over(p, result, q):
        fin_copy(p, result, q).start()
        keep_copy(p, result, q).start()

    def take_in(p):
        in_copy(p).wait_recv()
        own[p] = (own[p].astype(F32) + lines[p].astype(F32)).astype(BF16)
        mid_copy(p).start()

    def finish(p):
        mid_copy(p).wait_recv()

        @pl.when(p < pieces)
        def _():
            for load in loads(p):
                load.wait()
            lines[p] = output_rows(own[p], across[p], x_own[p], small[...])

        @pl.when(p >= pieces)
        def _():
            q = p - pieces
            lines[p] = grad_rows(own[p], across[p], x_own[q], stats_own[q], g_own[q], small[...])

        out_copy(p).start()
        of(p, hand_over)

    def each(action, first=0, last=2 * pieces):
        lax.fori_loop(first, last, lambda p, _: (action(p), 0)[1], 0)

    @pl.when(i == 0)
    def _():
        for n in range(1, count):
            pl.semaphore_signal(
                barrier, inc=1, device_id={"dp": lax.rem(row + n, count)}, device_id_type=mesh
            )
        for n in range(1, size):
            pl.semaphore_signal(
                barrier, inc=1, device_id={"tensor": lax.rem(me + n, size)}, device_id_type=mesh
            )
        for c in range(chunks):
            for r in range(2):
                part_copy(c, r).start()
        sums[...] = extra[...]
        pl.semaphore_wait(barrier, count + size - 2)
        for c in range(chunks):
            for r in range(2):
                part_copy(c, r).wait()

    @pl.when((i == 0) & end)
    def _():
        each(lambda p: in_copy(p).start(), 0, pieces)

    @pl.when((i == 0) & middle)
    def _():
        each(lambda p: [load.start() for load in loads(p)], 0, pieces)

    ours = lax.rem(i, 2)
    half = i // 2
    to = pl.ds(pieces + 2 * half, 2)
    for cut in range(0, d, 2 * TILE):
        cut = slice(cut, cut + 2 * TILE)
        total = nt(pre[...], wu[cut])
        for c, g in enumerate((gq, gk, gv)):
            total = total + nt(g[...], wq[c, cut])
        scaled = (x_block[:, cut].astype(F32) - stats_block[:, 0:1]) * stats_block[:, 1:2]
        sums[0:1, cut] += jnp.sum(total * scaled, axis=0, keepdims=True)
        sums[1:2, cut] += jnp.sum(total, axis=0, keepdims=True)
        total = total.astype(BF16)

        @pl.when(ours == 0)
        def _():
            held[half, :, cut] = total

        @pl.when(ours == 1)
        def _():
            own[to, :, cut] = total.reshape(2, PIECE, 2 * TILE)

    @pl.when(ours == 0)
    def _():
        peer_copy(half).start()

    @pl.when(ours == 1)
    def _():
        peer_copy(half).wait_recv()
        total = own[to].astype(F32) + came[half].reshape(2, PIECE, d).astype(F32)
        own[to] = total.astype(BF16)

    @pl.when((ours == 1) & end)
    def _():
        in_copy(pieces + 2 * half).start()
        in_copy(pieces + 2 * half + 1).start()

    early = 4
    begin = pieces - early

    @pl.when((i >= begin) & middle)
    def _():
        take_in(i - begin)

    @pl.when((i > begin) & middle)
    def _():
        finish(i - begin - 1)

    @pl.when(i == pieces - 1)
    def _():
        for n in range(1, count):
            dp_copy(n).start()

    def both(p, _):
        take_in(p)
        finish(p - 1)
        return 0

    def pass_on(p):
        out_copy(p).wait_recv()
        of(p, hand_over)

    some = early + 2

    @pl.when((i == pieces - 1) & middle)
    def _():
        lax.fori_loop(early, some, both, 0)

    @pl.when((i == pieces - 1) & end)
    def _():
        each(pass_on, 0, some)

    @pl.when(i == pieces - 1)
    def _():
        wide = d // count
        total = sums[:, pl.ds(pl.multiple_of(row * wide, 128), wide)]
        for n in range(1, count):
            dp_copy(n).wait()
            total = total + by_dp[n]
        mine[...] = total
        for n in range(1, size):
            tensor_copy(n).start()

    @pl.when((i == pieces - 1) & middle)
    def _():
        lax.fori_loop(some, 2 * pieces, both, 0)
        finish(2 * pieces - 1)
        each(lambda p: (mid_copy(p).wait_send(), out_copy(p).wait_send()))

    @pl.when((i == pieces - 1) & end)
    def _():
        each(pass_on, some)
        each(lambda p: in_copy(p).wait_send())

    @pl.when(i == pieces - 1)
    def _():
        total = mine[...]
        for n in range(1, size):
            tensor_copy(n).wait()
            total = total + by_tensor[n]
        vectors[...] = jnp.concatenate([total[:2], mine[2:]])
        for c in range(chunks):
            peer_copy(c).wait_send()
        each(lambda p: of(p, lambda *a: (fin_copy(*a).wait(), keep_copy(*a).wait())))


def line_sums(chain, parts, size, count, gq, gk, gv, pre, x, stats, wq, wu, small, extra, g):
    length, d = x.shape
    width, units = wq.shape[2], wu.shape[1]
    chunks = len(parts)
    pieces = 2 * chunks

    def block(n):
        def index(i):
            core = lax.rem(lax.axis_index("tensor"), 2)
            mine = lax.rem(i, 2)
            return (place_of(i // 2, lax.rem(core + 1 + mine, 2)), 0)

        return pl.BlockSpec((TILE, n), index)

    def once(shape):
        zeros = (0,) * len(shape)
        return pl.BlockSpec(shape, lambda *i: zeros, pipeline_mode=pl.Buffered(1))

    far = pl.BlockSpec(memory_space=pltpu.HBM)
    rows_of = lambda n: pltpu.VMEM((n, PIECE, d), BF16)
    sems = pltpu.SemaphoreType.DMA
    vector = (8, d // count)
    return chain(
        line_kernel,
        "line_sums",
        pieces,
        [(a, block(width)) for a in (gq, gk, gv)]
        + [
            (pre, block(units)), (x, block(d)), (stats, block(PAIR)), (wq, once(wq.shape)),
            (wu, once(wu.shape)), (small, once(small.shape)), (extra, once(extra.shape)),
            (x, far), (g, far), (stats, far),
        ]
        + [(p, far) for p in parts],
        [((length, d), BF16, far), ((length, d), BF16, far), (vector, F32, whole(vector))],
        scratch=[
            pltpu.VMEM((chunks, TILE, d), BF16), pltpu.VMEM((chunks, TILE, d), BF16),
            rows_of(2 * pieces), rows_of(2 * pieces), rows_of(2 * pieces),
            rows_of(pieces), rows_of(pieces), pltpu.VMEM((pieces, PIECE, PAIR), F32),
            pltpu.VMEM((8, d), F32), pltpu.VMEM((count, *vector), F32), pltpu.VMEM(vector, F32),
            pltpu.VMEM((size, *vector), F32),
            sems((7, max(pieces, size, count))), sems((pieces,)), sems((chunks,)), sems((chunks,)),
        ]
        + [sems((2 * pieces,))] * 9,
        collective=5,
        flops=200e9,
        mib=62,
    )


def output_rows(a, b, x, small):
    total = a[...].astype(F32) + b[...].astype(F32)
    biases = small[2:3] + small[3:4]
    return (x[...].astype(F32) + total + biases).astype(BF16)


def grad_rows(a, b, x, stats, g, small):
    u = (a[...].astype(F32) + b[...].astype(F32)) * small[0:1]
    mean, inverse = stats[:, 0:1], stats[:, 1:2]
    scaled = (x[...].astype(F32) - mean) * inverse
    back_u = inverse * (
        u
        - jnp.mean(u, axis=-1, keepdims=True)
        - scaled * jnp.mean(u * scaled, axis=-1, keepdims=True)
    )
    return (g[...].astype(F32) + back_u).astype(BF16)


PIECE = TILE // 2


def line_kernel(
    gq, gk, gv, pre, x_block, stats_block, wq, wu, small, extra, x_all, g_all, stats_all, *refs
):
    chunks = len(refs) - 28
    parts, refs = refs[:chunks], refs[chunks:]
    output, grad, vectors = refs[:3]
    held, came, own, lines, across, x_own, g_own, stats_own, sums, by_dp, mine, by_tensor = refs[3:15]
    (
        load_sem, part_sem, peer_send, peer_recv, in_send, in_recv, mid_send, mid_recv, out_send, out_recv,
        fin_send, fin_recv, keep_sem,
    ) = refs[15:28]
    i = pl.program_id(0)
    pieces = 2 * chunks
    d = came.shape[2]
    row, me = lax.axis_index("dp"), lax.axis_index("tensor")
    count, size = by_dp.shape[0], by_tensor.shape[0]
    core = lax.rem(me, 2)
    chip = me // 2
    peer = me + 1 - 2 * core
    beside = 2 * (chip + 1 - 2 * lax.rem(chip, 2)) + core
    facing = 2 * (3 - chip) + core
    middle = (chip == 1) | (chip == 2)
    end = jnp.logical_not(middle)
    mesh = pl.DeviceIdType.MESH
    barrier = pltpu.get_barrier_semaphore()

    def remote(source, target, send_sem, recv_sem, device, axis="tensor"):
        return pltpu.make_async_remote_copy(
            src_ref=source, dst_ref=target, send_sem=send_sem, recv_sem=recv_sem,
            device_id={axis: device}, device_id_type=mesh,
        )

    def place(p):
        start = place_of(p // 2, core) * TILE + lax.rem(p, 2) * PIECE
        return pl.ds(pl.multiple_of(start, PIECE), PIECE)

    def peer_copy(c):
        return remote(held.at[c], came.at[c], peer_send.at[c], peer_recv.at[c], peer)

    def in_copy(p):
        return remote(own.at[p], lines.at[p], in_send.at[p], in_recv.at[p], beside)

    def mid_copy(p):
        return remote(own.at[p], across.at[p], mid_send.at[p], mid_recv.at[p], facing)

    def out_copy(p):
        return remote(lines.at[p], lines.at[p], out_send.at[p], out_recv.at[p], beside)

    def fin_copy(p, result, q):
        return remote(lines.at[p], result.at[place(q)], fin_send.at[p], fin_recv.at[p], peer)

    def keep_copy(p, result, q):
        return pltpu.make_async_copy(lines.at[p], result.at[place(q)], keep_sem.at[p])

    def loads(p):
        return [
            pltpu.make_async_copy(array.at[place(p)], here.at[p], load_sem.at[n, p])
            for n, (array, here) in enumerate(((x_all, x_own), (g_all, g_own), (stats_all, stats_own)))
        ]

    def part_copy(c, r):
        p = 2 * c + r
        return pltpu.make_async_copy(
            parts[c].at[pl.ds(r * PIECE, PIECE)], own.at[p], part_sem.at[p]
        )

    def dp_copy(n):
        device = lax.rem(row + n, count)
        wide = d // count
        source = sums.at[:, pl.ds(pl.multiple_of(device * wide, 128), wide)]
        return remote(source, by_dp.at[n], load_sem.at[3, n], load_sem.at[4, n], device, "dp")

    def tensor_copy(n):
        device = lax.rem(me + n, size)
        return remote(mine, by_tensor.at[n], load_sem.at[5, n], load_sem.at[6, n], device)

    def of(p, action):
        @pl.when(p < pieces)
        def _():
            action(p, output, p)

        @pl.when(p >= pieces)
        def _():
            action(p, grad, p - pieces)

    def hand_over(p, result, q):
        fin_copy(p, result, q).start()
        keep_copy(p, result, q).start()

    def take_in(p):
        in_copy(p).wait_recv()
        own[p] = (own[p].astype(F32) + lines[p].astype(F32)).astype(BF16)
        mid_copy(p).start()

    def finish(p):
        mid_copy(p).wait_recv()

        @pl.when(p < pieces)
        def _():
            for load in loads(p):
                load.wait()
            lines[p] = output_rows(own[p], across[p], x_own[p], small[...])

        @pl.when(p >= pieces)
        def _():
            q = p - pieces
            lines[p] = grad_rows(own[p], across[p], x_own[q], stats_own[q], g_own[q], small[...])

        out_copy(p).start()
        of(p, hand_over)

    def each(action, first=0, last=2 * pieces):
        lax.fori_loop(first, last, lambda p, _: (action(p), 0)[1], 0)

    @pl.when(i == 0)
    def _():
        for n in range(1, count):
            pl.semaphore_signal(
                barrier, inc=1, device_id={"dp": lax.rem(row + n, count)}, device_id_type=mesh
            )
        for n in range(1, size):
            pl.semaphore_signal(
                barrier, inc=1, device_id={"tensor": lax.rem(me + n, size)}, device_id_type=mesh
            )
        for c in range(chunks):
            for r in range(2):
                part_copy(c, r).start()
        sums[...] = extra[...]
        pl.semaphore_wait(barrier, count + size - 2)
        for c in range(chunks):
            for r in range(2):
                part_copy(c, r).wait()

    @pl.when((i == 0) & end)
    def _():
        each(lambda p: in_copy(p).start(), 0, pieces)

    @pl.when((i == 0) & middle)
    def _():
        each(lambda p: [load.start() for load in loads(p)], 0, pieces)

    ours = lax.rem(i, 2)
    half = i // 2
    to = pl.ds(pieces + 2 * half, 2)
    for cut in range(0, d, 2 * TILE):
        cut = slice(cut, cut + 2 * TILE)
        total = nt(pre[...], wu[cut])
        for c, g in enumerate((gq, gk, gv)):
            total = total + nt(g[...], wq[c, cut])
        scaled = (x_block[:, cut].astype(F32) - stats_block[:, 0:1]) * stats_block[:, 1:2]
        sums[0:1, cut] += jnp.sum(total * scaled, axis=0, keepdims=True)
        sums[1:2, cut] += jnp.sum(total, axis=0, keepdims=True)
        total = total.astype(BF16)

        @pl.when(ours == 0)
        def _():
            held[half, :, cut] = total

        @pl.when(ours == 1)
        def _():
            own[to, :, cut] = total.reshape(2, PIECE, 2 * TILE)

    @pl.when(ours == 0)
    def _():
        peer_copy(half).start()

    @pl.when(ours == 1)
    def _():
        peer_copy(half).wait_recv()
        total = own[to].astype(F32) + came[half].reshape(2, PIECE, d).astype(F32)
        own[to] = total.astype(BF16)

    @pl.when((ours == 1) & end)
    def _():
        in_copy(pieces + 2 * half).start()
        in_copy(pieces + 2 * half + 1).start()

    early = 4
    begin = pieces - early

    @pl.when((i >= begin) & middle)
    def _():
        take_in(i - begin)

    @pl.when((i > begin) & middle)
    def _():
        finish(i - begin - 1)

    @pl.when(i == pieces - 1)
    def _():
        for n in range(1, count):
            dp_copy(n).start()

    def both(p, _):
        take_in(p)
        finish(p - 1)
        return 0

    def pass_on(p):
        out_copy(p).wait_recv()
        of(p, hand_over)

    some = early + 2

    @pl.when((i == pieces - 1) & middle)
    def _():
        lax.fori_loop(early, some, both, 0)

    @pl.when((i == pieces - 1) & end)
    def _():
        each(pass_on, 0, some)

    @pl.when(i == pieces - 1)
    def _():
        wide = d // count
        total = sums[:, pl.ds(pl.multiple_of(row * wide, 128), wide)]
        for n in range(1, count):
            dp_copy(n).wait()
            total = total + by_dp[n]
        mine[...] = total
        for n in range(1, size):
            tensor_copy(n).start()

    @pl.when((i == pieces - 1) & middle)
    def _():
        lax.fori_loop(some, 2 * pieces, both, 0)
        finish(2 * pieces - 1)
        each(lambda p: (mid_copy(p).wait_send(), out_copy(p).wait_send()))

    @pl.when((i == pieces - 1) & end)
    def _():
        each(pass_on, some)
        each(lambda p: in_copy(p).wait_send())

    @pl.when(i == pieces - 1)
    def _():
        total = mine[...]
        for n in range(1, size):
            tensor_copy(n).wait()
            total = total + by_tensor[n]
        vectors[...] = jnp.concatenate([total[:2], mine[2:]])
        for c in range(chunks):
            peer_copy(c).wait_send()
        each(lambda p: of(p, lambda *a: (fin_copy(*a).wait(), keep_copy(*a).wait())))


def line_sums(chain, parts, size, count, gq, gk, gv, pre, x, stats, wq, wu, small, extra, g):
    length, d = x.shape
    width, units = wq.shape[2], wu.shape[1]
    chunks = len(parts)
    pieces = 2 * chunks

    def block(n):
        def index(i):
            core = lax.rem(lax.axis_index("tensor"), 2)
            mine = lax.rem(i, 2)
            return (place_of(i // 2, lax.rem(core + 1 + mine, 2)), 0)

        return pl.BlockSpec((TILE, n), index)

    def once(shape):
        zeros = (0,) * len(shape)
        return pl.BlockSpec(shape, lambda *i: zeros, pipeline_mode=pl.Buffered(1))

    far = pl.BlockSpec(memory_space=pltpu.HBM)
    rows_of = lambda n: pltpu.VMEM((n, PIECE, d), BF16)
    sems = pltpu.SemaphoreType.DMA
    vector = (8, d // count)
    return chain(
        line_kernel,
        "line_sums",
        pieces,
        [(a, block(width)) for a in (gq, gk, gv)]
        + [
            (pre, block(units)), (x, block(d)), (stats, block(PAIR)), (wq, once(wq.shape)),
            (wu, once(wu.shape)), (small, once(small.shape)), (extra, once(extra.shape)),
            (x, far), (g, far), (stats, far),
        ]
        + [(p, far) for p in parts],
        [((length, d), BF16, far), ((length, d), BF16, far), (vector, F32, whole(vector))],
        scratch=[
            pltpu.VMEM((chunks, TILE, d), BF16), pltpu.VMEM((chunks, TILE, d), BF16),
            rows_of(2 * pieces), rows_of(2 * pieces), rows_of(2 * pieces),
            rows_of(pieces), rows_of(pieces), pltpu.VMEM((pieces, PIECE, PAIR), F32),
            pltpu.VMEM((8, d), F32), pltpu.VMEM((count, *vector), F32), pltpu.VMEM(vector, F32),
            pltpu.VMEM((size, *vector), F32),
            sems((7, max(pieces, size, count))), sems((pieces,)), sems((chunks,)), sems((chunks,)),
        ]
        + [sems((2 * pieces,))] * 9,
        collective=5,
        flops=200e9,
        mib=62,
    )


LAG = 3


def flow(chain, size, core, chunk, total, closing, results, key, length):
    chips = size // 2
    chip = lax.axis_index("tensor") // 2
    distance = jnp.where(chip < chips // 2, chips // 2 - 1 - chip, chip - chips // 2)
    for s in range(chips // 2 - 1):
        came = along(total, [(s, s + 1), (chips - 1 - s, chips - 2 - s)])
        yield
        total = plus(chain, total, came)
    a, b = chips // 2 - 1, chips // 2
    came = along(total, [(a, b), (b, a)])
    yield
    value = closing(chunk, total, came)
    for s in range(chips // 2 - 1):
        a, b = chips // 2 - 1 - s, chips // 2 + s
        came = along(value, [(a, a - 1), (b, b + 1)])
        yield
        value = choose(chain, (distance == s + 1).astype(jnp.int32)[None], value, came)
    peer = swap_cores(value, size)
    yield
    results[key] = assemble(chain, core, chunk, length, value, peer, results.get(key))


def on_device(
    size,
    inputs,
    segment_ids,
    norm_gain,
    norm_bias,
    qkv_weight,
    qkv_bias,
    out_weight,
    out_bias,
    up_weight,
    up_bias,
    down_weight,
    down_bias,
    cotangent,
):
    x, g, segment_row = inputs[0], cotangent[0], segment_ids[0]
    length, d = x.shape
    width, units = qkv_weight.shape[2], up_weight.shape[1]
    count = lax.axis_size("dp")
    core = (lax.axis_index("tensor") % 2).astype(jnp.int32)[None]

    start = jnp.sum((segment_row[None, :] < segment_row[:, None]).astype(jnp.int32), axis=1)
    small = jnp.stack([norm_gain, norm_bias, out_bias, down_bias] + [norm_gain] * 4).astype(F32)
    wq = qkv_weight.transpose(1, 0, 2)

    chain = Chain()
    normed, stats, q, k, v, hidden, slope, cos_wide, sin_wide = first(
        chain, x, small, wq, qkv_bias, up_weight, up_bias, start
    )
    mixed, log = attend(chain, start, q, k, v)
    parts = branch(chain, CHUNKS, mixed, hidden, out_weight, down_weight)

    pre, gm, delta, g_sums, up_sums = back(chain, g, slope, mixed, out_weight, down_weight)
    scatter = lambda a: lax.psum_scatter(a, "dp", scatter_dimension=1, tiled=True)
    near = scatter(weight_grad(chain, "weight_grad_g", [hidden, mixed], g))
    tiles = length // TILE
    *packed, qkv_sums, _ = attend_back(
        chain, 0, tiles, start, log, delta, q, k, v, gm, cos_wide, sin_wide, [log]
    )
    far = scatter(weight_grad(chain, "weight_grad_n", [pre, *packed], normed))

    by_share = lambda a: a.reshape(-1, count, HD // count).swapaxes(0, 1).reshape(count, -1)
    part = d // count
    narrow = jnp.concatenate([by_share(up_sums[0]), by_share(qkv_sums[:3])], axis=1)
    narrow = jnp.pad(narrow, ((0, 0), (0, part - narrow.shape[1]))).reshape(1, d)
    results = {}
    if size == 8:
        extra = jnp.concatenate([jnp.zeros((2, d), F32), g_sums[:1], narrow, jnp.zeros((4, d), F32)])
        results["output"], results["grad"], vectors = line_sums(
            chain, parts, size, count, *packed, pre, x, stats, wq, up_weight, small, extra, g
        )
    else:

        def summed(parts, closing, own, key):
            finish = lambda chunk, a, b: close(chain, closing, core, chunk, a, b, own, small)
            flows = [
                flow(chain, size, core, c, parts[c], finish, results, key, length)
                for c in range(CHUNKS)
            ]
            while flows:
                flows = [f for f in flows if next(f, flows) is None]

        summed(parts, output_rows, [x], "output")
        norm_sums, *parts = normed_back(chain, CHUNKS, *packed, pre, x, stats, wq, up_weight)
        summed(parts, grad_rows, [x, stats, g], "grad")
        vectors = jnp.concatenate([norm_sums[:2], g_sums[:1], narrow]).reshape(4, count, part)
        vectors = vectors.swapaxes(0, 1).reshape(count, -1, 128)
        vectors = add_vectors(chain, vectors, size, count).reshape(4, part)
    up_b_share = vectors[3, : units // count].reshape(-1, HD // count)
    qkv_b_share = vectors[3, units // count : (units + 3 * width) // count].reshape(3, -1, HD // count)
    down_share, out_share = widen(chain, near, [(units, part), (width, part)], (False, False))
    up_share, qkv_share = widen(chain, far, [(part, units), (3, part, width)], (True, True))

    return (
        results["output"][None],
        results["grad"][None],
        vectors[0],
        vectors[1],
        qkv_share.transpose(1, 0, 2),
        qkv_b_share,
        out_share,
        vectors[2],
        up_share,
        up_b_share,
        down_share,
        vectors[2],
    )


def solution(mesh):
    placed = (
        P("dp", None, None),
        P("dp", None),
        P(),
        P(),
        P(None, None, "tensor"),
        P(None, "tensor"),
        P("tensor", None),
        P(),
        P(None, "tensor"),
        P("tensor"),
        P("tensor", None),
        P(),
        P("dp", None, None),
    )
    return jax.shard_map(
        partial(on_device, mesh.shape["tensor"]),
        mesh=mesh,
        in_specs=placed,
        out_specs=(
            P("dp", None, None),
            P("dp", None, None),
            P("dp"),
            P("dp"),
            P("dp", None, "tensor"),
            P(None, "tensor", "dp"),
            P("tensor", "dp"),
            P("dp"),
            P("dp", "tensor"),
            P("tensor", "dp"),
            P("tensor", "dp"),
            P("dp"),
        ),
        check_vma=False,
    )
```

```python
from functools import partial

import jax
import jax.numpy as jnp
from jax import lax
from jax.experimental import pallas as pl
from jax.experimental.pallas import tpu as pltpu
from jax.sharding import PartitionSpec as P

HD = 64
ROT = 32
PAIR = 2 * HD
TILE = 256
CHUNKS = 4
NEG = -1e30
MIB = 1 << 20
F32 = jnp.float32
BF16 = jnp.bfloat16


class Chain:
    def __init__(self):
        self.link = jnp.zeros((8, 128), F32)

    def __call__(
        self, kernel, name, grid, ins, outs, scalars=(), scratch=(), alias=(), mib=58, flops=1, collective=None
    ):
        taken, given = len(scalars) + len(ins), len(outs)

        def body(*refs):
            kernel(*refs[:taken], *refs[taken + 1 : taken + 1 + given], *refs[taken + 2 + given :])

        anywhere = pl.BlockSpec(memory_space=pltpu.HBM)
        results = pl.pallas_call(
            body,
            grid_spec=pltpu.PrefetchScalarGridSpec(
                num_scalar_prefetch=len(scalars),
                grid=(grid,),
                in_specs=[spec for _, spec in ins] + [anywhere],
                out_specs=[spec for _, _, spec in outs] + [anywhere],
                scratch_shapes=list(scratch),
            ),
            out_shape=[jax.ShapeDtypeStruct(shape, dtype) for shape, dtype, _ in outs]
            + [jax.ShapeDtypeStruct(self.link.shape, F32)],
            input_output_aliases={taken: given, **{len(scalars) + i: o for i, o in alias}},
            compiler_params=pltpu.CompilerParams(
                dimension_semantics=("arbitrary",), vmem_limit_bytes=mib * MIB,
                collective_id=collective, has_side_effects=collective is not None,
            ),
            cost_estimate=pl.CostEstimate(flops=int(flops), bytes_accessed=1, transcendentals=0),
            name=name,
        )(*scalars, *[array for array, _ in ins], self.link)
        self.link = results[-1]
        return results[:-1]


def whole(shape):
    zeros = (0,) * len(shape)
    return pl.BlockSpec(shape, lambda *i: zeros)


def rows(n, height=TILE):
    return pl.BlockSpec((height, n), lambda i, *s: (i, 0))


def nn(a, b):
    return lax.dot_general(a, b, (((1,), (0,)), ((), ())), preferred_element_type=F32)


def nt(a, b):
    return lax.dot_general(a, b, (((1,), (1,)), ((), ())), preferred_element_type=F32)


def tn(a, b):
    return lax.dot_general(a, b, (((0,), (0,)), ((), ())), preferred_element_type=F32)


def rotated(x, cos_wide, sin_wide):
    lane = lax.broadcasted_iota(jnp.int32, x.shape, 1) % HD
    half = ROT // 2
    other = jnp.where(
        lane < half, pltpu.roll(x, PAIR - half, 1), pltpu.roll(x, half, 1)
    )
    return x * cos_wide + other * sin_wide


def row_stats(x):
    mean = jnp.mean(x, axis=-1, keepdims=True)
    centered = x - mean
    inverse = lax.rsqrt(jnp.mean(centered * centered, axis=-1, keepdims=True) + 1e-05)
    return centered * inverse, mean, inverse


def gelu_both(u):
    c = 0.7978845608028654
    u2 = u * u
    gate = 0.5 + 0.5 * jnp.tanh(u * (c + (c * 0.044715) * u2))
    value = u * gate
    slope = gate + value * (1.0 - gate) * (2.0 * c + (6.0 * c * 0.044715) * u2)
    return value, slope


def first_kernel(
    x0_ref, x1_ref, x2_ref, small_ref, wq_ref, bq_ref, wu_ref, bu_ref, start_ref, freq_ref,
    normed_ref, stats_ref, q_ref, k_ref, v_ref, hidden_ref, slope_ref, cos_ref, sin_ref,
    even, odd, even_stats,
):
    s = pl.program_id(0)
    gain, shift = small_ref[0:1], small_ref[1:2]
    lane = lax.broadcasted_iota(jnp.int32, (TILE, PAIR), 1)

    def norm(x):
        scaled, mean, inverse = row_stats(x.astype(F32))
        return (scaled * gain + shift).astype(BF16), jnp.where(lane == 0, mean, inverse)

    @pl.when(s == 0)
    def _():
        even[...], even_stats[...] = norm(x0_ref[...])

    half = ROT // 2
    unit = lax.broadcasted_iota(jnp.int32, (half, PAIR), 1) % HD
    index = lax.broadcasted_iota(jnp.int32, (half, PAIR), 0)
    first_half = (unit == index).astype(F32)
    second_half = (unit == index + half).astype(F32)
    bias = bq_ref[...].astype(F32)

    def spread(a, b):
        return lax.dot_general(
            a, b, (((0,), (0,)), ((), ())), precision=lax.Precision.HIGHEST,
            preferred_element_type=F32,
        )

    def project(t, normed):
        here = slice(t * TILE, (t + 1) * TILE)
        place = lax.broadcasted_iota(jnp.int32, (1, TILE), 1) + (2 * s + t) * TILE
        angle = freq_ref[...] * (place - start_ref[:, here]).astype(F32)
        cos_wide = spread(jnp.cos(angle), first_half + second_half)
        cos_wide = jnp.where(lane % HD < ROT, cos_wide, 1.0)
        sin_wide = spread(jnp.sin(angle), second_half - first_half)
        cos_ref[here], sin_ref[here] = cos_wide, sin_wide
        for c, out in enumerate((q_ref, k_ref, v_ref)):
            packed = nn(normed, wq_ref[c]) + bias[c : c + 1]
            if c == 2:
                out[here] = packed.astype(BF16)
            else:
                for p in range(packed.shape[1] // PAIR):
                    cut = slice(p * PAIR, (p + 1) * PAIR)
                    turned = rotated(packed[:, cut], cos_wide, sin_wide).astype(BF16)
                    out[here, cut] = turned * (HD**-0.5) if c == 0 else turned
        units = wu_ref.shape[1]
        for n in range(0, units, TILE):
            cut = slice(n, n + TILE)
            value, slope = gelu_both(nn(normed, wu_ref[:, cut]) + bu_ref[:, cut])
            hidden_ref[here, cut] = value.astype(BF16)
            slope_ref[here, cut] = slope.astype(BF16)

    normed = even[...]
    normed_ref[:TILE] = normed
    stats_ref[:TILE] = even_stats[...]
    after, after_stats = norm(x1_ref[...])
    odd[...] = after
    normed_ref[TILE:] = after
    stats_ref[TILE:] = after_stats
    project(0, normed)
    even[...], even_stats[...] = norm(x2_ref[...])
    project(1, odd[...])


def first(chain, x, small, wq, bq, wu, bu, start):
    length, d = x.shape
    width, units = wq.shape[2], wu.shape[1]
    tiles = length // TILE
    freq = 10000.0 ** (-jnp.arange(ROT // 2, dtype=F32) * 2.0 / ROT)
    at = lambda f: pl.BlockSpec((TILE, d), lambda s: (f(s), 0))
    big = lambda n: rows(n, 2 * TILE)
    return chain(
        first_kernel,
        "first",
        tiles // 2,
        [
            (x, at(lambda s: 0)),
            (x, at(lambda s: 2 * s + 1)),
            (x, at(lambda s: jnp.minimum(2 * s + 2, tiles - 1))),
            (small, whole(small.shape)), (wq, whole(wq.shape)), (bq, whole(bq.shape)),
            (wu, whole(wu.shape)), (bu[None].astype(F32), whole((1, units))),
            (start[None], pl.BlockSpec((1, 2 * TILE), lambda s: (0, s))),
            (jnp.broadcast_to(freq[:, None], (ROT // 2, TILE)), whole((ROT // 2, TILE))),
        ],
        [((length, d), BF16, big(d)), ((length, PAIR), F32, big(PAIR))]
        + [((length, n), BF16, big(n)) for n in (width, width, width, units, units)]
        + [((length, PAIR), F32, big(PAIR))] * 2,
        scratch=[pltpu.VMEM((TILE, d), BF16)] * 2 + [pltpu.VMEM((TILE, PAIR), F32)],
    )


def halves(x):
    left = lax.broadcasted_iota(jnp.int32, x.shape, 1) < HD
    zero = jnp.zeros(x.shape, x.dtype)
    return [jnp.where(left, x, zero), jnp.where(left, zero, x)]


def pair_cuts(width):
    return [slice(p, p + PAIR) for p in range(0, width, PAIR)]


def attend_kernel(start_sref, start_ref, q_ref, k_ref, v_ref, mixed_ref, log_ref):
    i = pl.program_id(0)
    cuts = pair_cuts(q_ref.shape[1])
    heads = range(2 * len(cuts))
    key_row = lax.broadcasted_iota(jnp.int32, (TILE, TILE), 0)
    query = lax.broadcasted_iota(jnp.int32, (TILE, TILE), 1) + i * TILE
    start = start_ref[...]
    queries = [q for cut in cuts for q in halves(q_ref[:, cut])]

    def step(j, carry):
        tops, totals, sums = carry
        there = pl.ds(pl.multiple_of(j * TILE, TILE), TILE)
        place = key_row + j * TILE
        allowed = (place >= start) & (place <= query)
        k = [k_ref[there, cut] for cut in cuts]
        v = [v_ref[there, cut] for cut in cuts]
        s = [nt(k[h // 2], queries[h]) for h in heads]
        s = [jnp.where(allowed, a, NEG) for a in s]
        top = [jnp.maximum(tops[h], jnp.max(s[h], axis=0, keepdims=True)) for h in heads]
        alpha = [jnp.exp(tops[h] - top[h]) for h in heads]
        w = [jnp.exp(s[h] - top[h]) for h in heads]
        totals = [totals[h] * alpha[h] + jnp.sum(w[h], axis=0, keepdims=True) for h in heads]
        w = [a.astype(BF16) for a in w]
        add = [tn(v[h // 2], w[h])[h % 2 * HD : (h % 2 + 1) * HD] for h in heads]
        sums = [sums[h] * alpha[h] + add[h] for h in heads]
        return tuple(top), tuple(totals), tuple(sums)

    empty = (
        tuple(jnp.full((1, TILE), NEG, F32) for _ in heads),
        tuple(jnp.zeros((1, TILE), F32) for _ in heads),
        tuple(jnp.zeros((HD, TILE), F32) for _ in heads),
    )
    low = start_sref[i * TILE] // TILE
    tops, totals, sums = lax.fori_loop(low, i + 1, step, empty)
    log_ref[...] = jnp.zeros_like(log_ref)
    for h in heads:
        log_ref[h : h + 1] = tops[h] + jnp.log(totals[h])
    mixed_ref[...] = jnp.concatenate([sums[h] * (1.0 / totals[h]) for h in heads]).T.astype(BF16)


def attend(chain, start, q, k, v):
    length, width = q.shape
    full = whole((length, width))
    return chain(
        attend_kernel,
        "attend",
        length // TILE,
        [
            (start[None], pl.BlockSpec((1, TILE), lambda i, *s: (0, i))),
            (q, rows(width)), (k, full), (v, full),
        ],
        [
            ((length, width), BF16, rows(width)),
            ((8, length), F32, pl.BlockSpec((8, TILE), lambda i, *s: (0, i))),
        ],
        scalars=(start,),
    )


def attend_back_kernel(
    begin, start_sref, start_ref, log_ref, delta_ref, q_ref, k_ref, v_ref, g_ref, cos_ref, sin_ref,
    totals_in, *refs,
):
    gq_ref, gk_ref, gv_ref, bias_ref, totals = refs[-5:]
    j = pl.program_id(0) + begin
    length, width = q_ref.shape
    cuts = pair_cuts(width)
    heads = range(2 * len(cuts))
    here = pl.ds(pl.multiple_of(j * TILE, TILE), TILE)

    @pl.when(pl.program_id(0) == 0)
    def _():
        totals[...] = totals_in[...] if begin else jnp.zeros_like(totals)
        bias_ref[...] = jnp.zeros_like(bias_ref)

    place = j * TILE + lax.broadcasted_iota(jnp.int32, (TILE, TILE), 0)
    query = lax.broadcasted_iota(jnp.int32, (TILE, TILE), 1)
    keys = [k_ref[here, cut] for cut in cuts]
    split = [half for k in keys for half in halves(k)]
    values = [v_ref[here, cut] for cut in cuts]

    def step(i, carry):
        gk, gv = carry
        there = pl.ds(pl.multiple_of(i * TILE, TILE), TILE)
        allowed = (place >= start_ref[:, there]) & (place <= query + i * TILE)
        qs = [half for cut in cuts for half in halves(q_ref[there, cut])]
        gs = [half for cut in cuts for half in halves(g_ref[there, cut])]
        s = [nt(keys[h // 2], qs[h]) for h in heads]
        gp = [nt(values[h // 2], gs[h]) for h in heads]
        w = [jnp.exp(jnp.where(allowed, s[h] - log_ref[h : h + 1, there], NEG)) for h in heads]
        ds = [(w[h] * (gp[h] - delta_ref[h : h + 1, there])).astype(BF16) for h in heads]
        w = [a.astype(BF16) for a in w]
        both = lambda f: tuple(f(h) + f(h + 1) for h in heads[::2])
        gv = [a + b for a, b in zip(gv, both(lambda h: nn(w[h], gs[h])))]
        gk = [a + b for a, b in zip(gk, both(lambda h: nn(ds[h], qs[h])))]
        for cut, gq in zip(cuts, both(lambda h: tn(ds[h], split[h]))):
            totals[there, cut] += gq
        return tuple(gk), tuple(gv)

    high = sum((start_sref[b * TILE] < (j + 1) * TILE).astype(jnp.int32) for b in range(length // TILE))
    empty = tuple(jnp.zeros((TILE, PAIR), F32) for _ in cuts)
    gks, gvs = lax.fori_loop(j, high, step, (empty, empty))
    cos_wide, sin_wide = cos_ref[...], -sin_ref[...]
    for cut, gk, gv in zip(cuts, gks, gvs):
        gq = rotated(totals[here, cut] * (HD**-0.5), cos_wide, sin_wide).astype(BF16)
        gk = rotated(gk, cos_wide, sin_wide).astype(BF16)
        for c, (g, out) in enumerate(((gq, gq_ref), (gk, gk_ref), (gv.astype(BF16), gv_ref))):
            out[:, cut] = g
            bias_ref[c : c + 1, cut] += jnp.sum(g.astype(F32), axis=0, keepdims=True)


def attend_back(chain, begin, end, start, log, delta, q, k, v, g, cos_wide, sin_wide, before):
    length, width = q.shape
    full = whole((length, width))
    shifted = lambda n: pl.BlockSpec((TILE, n), lambda i, *s: (i + begin, 0))
    anywhere = pl.BlockSpec(memory_space=pl.ANY)
    so_far = before[:3] if begin else []
    return chain(
        partial(attend_back_kernel, begin),
        f"attend_back_{begin}",
        end - begin,
        [
            (start[None], whole((1, length))), (log, whole((8, length))), (delta, whole((8, length))),
            (q, full), (k, full), (v, full), (g, full), (cos_wide, shifted(PAIR)), (sin_wide, shifted(PAIR)),
            (before[-1], full if begin else anywhere),
        ]
        + [(a, anywhere) for a in so_far],
        [((length, width), BF16, shifted(width))] * 3
        + [((8, width), F32, whole((8, width))), ((length, width), F32, full)],
        scalars=(start,),
        alias=tuple((10 + n, n) for n in range(len(so_far))),
    )


def place_of(chunk, core):
    return 4 * (chunk // 2) + 2 * core + chunk % 2


def own_rows(chunks, half, skip=0):
    def spec(n):
        def index(i):
            core = lax.rem(lax.axis_index("tensor"), 2)
            steps = chunks // 2
            return (skip + 2 * lax.rem(i, steps) + jnp.where(i < steps, 1 - core, core), 0)

        return pl.BlockSpec((2 * half, n), index)

    return spec


def paired(product, chunks, ins, *refs):
    given, extra, sums, held, came, send_sem, recv_sem = (
        refs[:ins], refs[ins : len(refs) - chunks - 4], refs[-chunks - 4 : -4], *refs[-4:]
    )
    i = pl.program_id(0)
    steps = chunks // 2
    half, d = sums[0].shape
    me = lax.axis_index("tensor")
    peer = me + 1 - 2 * lax.rem(me, 2)
    barrier = pltpu.get_barrier_semaphore()

    def copy(n):
        return pltpu.make_async_remote_copy(
            src_ref=held.at[n], dst_ref=came.at[n], send_sem=send_sem.at[n], recv_sem=recv_sem.at[n],
            device_id={"tensor": peer}, device_id_type=pl.DeviceIdType.MESH,
        )

    @pl.when(i == 0)
    def _():
        pl.semaphore_signal(
            barrier, inc=1, device_id={"tensor": peer}, device_id_type=pl.DeviceIdType.MESH
        )
        for e in extra:
            e[...] = jnp.zeros_like(e)

    for cut in range(0, d, 2 * TILE):
        cut = slice(cut, cut + 2 * TILE)
        total = product(cut, given, extra).astype(BF16)
        held[pl.ds(2 * i, 2), :, cut] = total.reshape(2, half, 2 * TILE)

    @pl.when(i == 0)
    def _():
        pl.semaphore_wait(barrier, 1)

    for n in range(steps):

        @pl.when(i == n)
        def _(n=n):
            copy(2 * n).start()
            copy(2 * n + 1).start()

        @pl.when(i == steps + n)
        def _(n=n):
            for c in (2 * n, 2 * n + 1):
                copy(c).wait()
                total = held[chunks + c].astype(F32) + came[c].astype(F32)
                sums[c][...] = total.astype(BF16)


def pair_call(chain, product, name, collective, chunks, half, d, ins, extra):
    return chain(
        partial(paired, product, chunks, len(ins)),
        name,
        chunks,
        ins,
        extra + [((half, d), BF16, whole((half, d)))] * chunks,
        scratch=[pltpu.VMEM((2 * chunks, half, d), BF16), pltpu.VMEM((chunks, half, d), BF16)]
        + [pltpu.SemaphoreType.DMA((chunks,))] * 2,
        collective=collective,
    )


def branch_kernel(mixed, hidden, wo, wd, out):
    for cut in range(0, out.shape[1], 2 * TILE):
        cut = slice(cut, cut + 2 * TILE)
        out[:, cut] = (nn(mixed[...], wo[:, cut]) + nn(hidden[...], wd[:, cut])).astype(BF16)


def branch(chain, length, mixed, hidden, wo, wd):
    d = wo.shape[1]
    big = lambda n: rows(n, 2 * TILE)
    return chain(
        branch_kernel,
        "branch",
        length // (2 * TILE),
        [
            (mixed, big(mixed.shape[1])), (hidden, big(hidden.shape[1])),
            (wo, whole(wo.shape)), (wd, whole(wd.shape)),
        ],
        [((length, d), BF16, big(d))],
    )[0]


def branch_product(cut, given, extra):
    mixed, hidden, wo, wd = given
    return nn(mixed[...], wo[:, cut]) + nn(hidden[...], wd[:, cut])


def branch_rest(chain, chunks, skip, mixed, hidden, wo, wd):
    length, d = mixed.shape[0], wo.shape[1]
    half = length // (2 * (chunks + skip))
    spec = own_rows(chunks, half, skip)
    ins = [
        (mixed, spec(mixed.shape[1])), (hidden, spec(hidden.shape[1])),
        (wo, whole(wo.shape)), (wd, whole(wd.shape)),
    ]
    return pair_call(chain, branch_product, "branch_rest", 1, chunks, half, d, ins, [])


def last_kernel(
    steps, summed, x, small, rest, grad, down_in, out_in, up_in, q_in, k_in, v_in,
    output, input_grad, down, out, up, qkv,
):
    i = pl.program_id(0)
    input_grad[...] = grad[...]
    down[...] = down_in[...].astype(F32)
    out[...] = out_in[...].astype(F32)
    up[...] = up_in[...].astype(F32).T
    for c, part in enumerate((q_in, k_in, v_in)):
        qkv[c] = part[...].astype(F32).T

    @pl.when(i < steps)
    def _():
        output[...] = output_rows(summed, x[...], None, small)

    @pl.when(i >= steps)
    def _():
        output[...] = rest[...]


def last(chain, summed, x, small, rest, grad, near, far, width, units):
    length, d = x.shape
    part = near.shape[1]
    lower = summed.shape[0]
    grid = 4
    high = length // grid
    steps = lower // high
    tall, slim, thin = units // grid, width // grid, part // grid
    block = rows(d, high)
    low = pl.BlockSpec((high, d), lambda i: (jnp.minimum(i, steps - 1), 0))
    upper = pl.BlockSpec((high, d), lambda i: (jnp.maximum(i - steps, 0), 0))
    third = lambda c: pl.BlockSpec((width, thin), lambda i: (units // width + c, i))
    return chain(
        partial(last_kernel, steps), "last", grid,
        [
            (summed, low), (x, low), (small, whole(small.shape)), (rest, upper), (grad, block),
            (near, rows(part, tall)),
            (near, pl.BlockSpec((slim, part), lambda i: (units // slim + i, 0))),
            (far, rows(part, tall)), (far, third(0)), (far, third(1)), (far, third(2)),
        ],
        [
            ((length, d), BF16, block), ((length, d), BF16, block),
            ((units, part), F32, rows(part, tall)), ((width, part), F32, rows(part, slim)),
            ((part, units), F32, pl.BlockSpec((part, tall), lambda i: (0, i))),
            ((3, part, width), F32, pl.BlockSpec((3, thin, width), lambda i: (0, i, 0))),
        ],
    )


def output_rows(a, x, b, small):
    total = a[...].astype(F32)
    if b is not None:
        total = total + b[...].astype(F32)
    return (x.astype(F32) + total + small[2:3] + small[3:4]).astype(BF16)


def close_kernel(summed, x, small, grad, output, input_grad):
    output[...] = output_rows(summed, x[...], None, small)
    input_grad[...] = grad[...]


def close_both(chain, summed, x, small, grad):
    length, d = x.shape
    block = rows(d, 2 * TILE)
    return chain(
        close_kernel, "close_both", length // (2 * TILE),
        [(summed, block), (x, block), (small, whole(small.shape)), (grad, block)],
        [((length, d), BF16, block)] * 2,
    )


def back_kernel(g_ref, slope_ref, mixed_ref, wo_ref, wd_ref, pre_ref, gm_ref, delta_ref, sums_ref, up_ref):
    @pl.when(pl.program_id(0) == 0)
    def _():
        sums_ref[...] = jnp.zeros_like(sums_ref)
        up_ref[...] = jnp.zeros_like(up_ref)

    g = g_ref[...]
    for n in range(0, wd_ref.shape[0], 2 * TILE):
        cut = slice(n, n + 2 * TILE)
        pre = (nt(g, wd_ref[cut]) * slope_ref[:, cut].astype(F32)).astype(BF16)
        pre_ref[:, cut] = pre
        up_ref[0:1, cut] += jnp.sum(pre.astype(F32), axis=0, keepdims=True)
    gm = nt(g, wo_ref[...]).astype(BF16)
    gm_ref[...] = gm
    product = gm.astype(F32) * mixed_ref[...].astype(F32)
    coarse = product.astype(BF16)
    fine = (product - coarse.astype(F32)).astype(BF16)
    width = gm.shape[1]
    pick = (
        lax.broadcasted_iota(jnp.int32, (8, width), 1) // HD
        == lax.broadcasted_iota(jnp.int32, (8, width), 0)
    ).astype(BF16)
    delta_ref[...] = nt(pick, coarse) + nt(pick, fine)
    sums_ref[0:1] += jnp.sum(g.astype(F32), axis=0, keepdims=True)


def back(chain, g, slope, mixed, wo, wd):
    length, d = g.shape
    width, units = wo.shape[0], wd.shape[0]
    big = lambda n: rows(n, 2 * TILE)
    return chain(
        back_kernel,
        "back",
        length // (2 * TILE),
        [
            (g, big(d)), (slope, big(units)), (mixed, big(width)),
            (wo, whole(wo.shape)), (wd, whole(wd.shape)),
        ],
        [
            ((length, units), BF16, big(units)), ((length, width), BF16, big(width)),
            ((8, length), F32, pl.BlockSpec((8, 2 * TILE), lambda i, *s: (0, i))),
            ((8, d), F32, whole((8, d))), ((8, units), F32, whole((8, units))),
        ],
    )


def normed_back_product(cut, given, extra):
    gq, gk, gv, pre, x, stats, wq, wu = given
    (sums,) = extra
    total = nt(pre[...], wu[cut])
    for c, g in enumerate((gq, gk, gv)):
        total = total + nt(g[...], wq[c, cut])
    scaled = (x[:, cut].astype(F32) - stats[:, 0:1]) * stats[:, 1:2]
    sums[0:1, cut] += jnp.sum(total * scaled, axis=0, keepdims=True)
    sums[1:2, cut] += jnp.sum(total, axis=0, keepdims=True)
    return total


def normed_back(chain, chunks, gq, gk, gv, pre, x, stats, wq, wu):
    length, d = x.shape
    width, units = wq.shape[2], wu.shape[1]
    half = length // (2 * chunks)
    spec = own_rows(chunks, half)
    ins = [(a, spec(width)) for a in (gq, gk, gv)] + [
        (pre, spec(units)), (x, spec(d)), (stats, spec(PAIR)),
        (wq, whole(wq.shape)), (wu, whole(wu.shape)),
    ]
    return pair_call(
        chain, normed_back_product, "normed_back", 2, chunks, half, d, ins,
        [((8, d), F32, whole((8, d)))],
    )


def weight_grad_kernel(counts, *refs):
    *lefts, right, out = refs
    i = pl.program_id(0)
    done = 0
    for left, count in zip(lefts, counts):

        @pl.when((i >= done) & (i < done + count))
        def _(left=left):
            out[...] = tn(left[...], right[...]).astype(BF16)

        done += count


def weight_grad(chain, name, lefts, right):
    length, d = right.shape
    wide = min(TILE, *[a.shape[1] for a in lefts])
    counts = tuple(a.shape[1] // wide for a in lefts)
    ins, done = [], 0
    for a, count in zip(lefts, counts):
        place = lambda i, done=done, count=count: jnp.clip(i - done, 0, count - 1)
        ins.append((a, pl.BlockSpec((length, wide), lambda i, f=place: (0, f(i)))))
        done += count
    return chain(
        partial(weight_grad_kernel, counts),
        name,
        done,
        ins + [(right, whole(right.shape))],
        [((done * wide, d), BF16, rows(d, wide))],
    )[0]


def vectors_kernel(size, count, vectors, total, came, part, wide, sems):
    row, me = lax.axis_index("dp"), lax.axis_index("tensor")
    barrier = pltpu.get_barrier_semaphore()
    mesh = pl.DeviceIdType.MESH
    half = part.shape[0] // 2

    def by_row(n):
        peer = lax.rem(row + n, count)
        return pltpu.make_async_remote_copy(
            src_ref=vectors.at[peer], dst_ref=came.at[n], send_sem=sems.at[0, n],
            recv_sem=sems.at[1, n], device_id={"dp": peer}, device_id_type=mesh,
        )

    def by_column(n):
        peer = lax.rem(me + n, size)
        return pltpu.make_async_remote_copy(
            src_ref=part.at[pl.ds(0, half)], dst_ref=wide.at[n], send_sem=sems.at[2, n],
            recv_sem=sems.at[3, n], device_id={"tensor": peer}, device_id_type=mesh,
        )

    for n in range(1, count):
        pl.semaphore_signal(
            barrier, inc=1, device_id={"dp": lax.rem(row + n, count)}, device_id_type=mesh
        )
    for n in range(1, size):
        pl.semaphore_signal(
            barrier, inc=1, device_id={"tensor": lax.rem(me + n, size)}, device_id_type=mesh
        )
    pl.semaphore_wait(barrier, count + size - 2)
    for n in range(1, count):
        by_row(n).start()
    mine = vectors[row]
    for n in range(1, count):
        by_row(n).wait()
        mine = mine + came[n]
    part[...] = mine
    for n in range(1, size):
        by_column(n).start()
    upper = mine[:half]
    for n in range(1, size):
        by_column(n).wait()
        upper = upper + wide[n]
    total[:half] = upper
    total[half:] = mine[half:]


def add_vectors(chain, vectors, size, count):
    small = vectors.shape[1:]
    return chain(
        partial(vectors_kernel, size, count), "add_vectors", 1, [(vectors, whole(vectors.shape))],
        [(small, F32, whole(small))],
        scratch=[
            pltpu.VMEM((count, *small), F32), pltpu.VMEM(small, F32),
            pltpu.VMEM((size, small[0] // 2, small[1]), F32),
            pltpu.SemaphoreType.DMA((4, max(size, count))),
        ],
        collective=6,
    )[0]


def widen_kernel(turned, share_ref, *outs):
    at = 0
    for out, turn in zip(outs, turned):
        if len(out.shape) == 3:
            for c in range(out.shape[0]):
                out[c] = share_ref[at : at + out.shape[2]].astype(F32).T
                at += out.shape[2]
        elif turn:
            out[...] = share_ref[at : at + out.shape[1]].astype(F32).T
            at += out.shape[1]
        else:
            out[...] = share_ref[at : at + out.shape[0]].astype(F32)
            at += out.shape[0]


def widen(chain, share, shapes, turned):
    return chain(
        partial(widen_kernel, turned), "widen", 1, [(share, whole(share.shape))],
        [(shape, F32, whole(shape)) for shape in shapes], mib=32,
    )


def add_kernel(a_ref, b_ref, out_ref):
    out_ref[...] = (a_ref[...].astype(F32) + b_ref[...].astype(F32)).astype(out_ref.dtype)


def plus(chain, a, b):
    block = whole(a.shape)
    return chain(
        add_kernel, "plus", 1, [(a, block), (b, block)], [(a.shape, a.dtype, block)], mib=16
    )[0]


def choose_kernel(flag_ref, a_ref, b_ref, out_ref):
    out_ref[...] = jnp.where(flag_ref[0] > 0, b_ref[...], a_ref[...])


def choose(chain, flag, a, b):
    height, d = a.shape
    block = rows(d, height // 2)
    return chain(
        choose_kernel, "choose", 2, [(a, block), (b, block)], [(a.shape, BF16, block)],
        scalars=(flag,),
    )[0]


def assemble_kernel(core_ref, a_ref, b_ref, *rest):
    rest[-1][...] = jnp.where(core_ref[0] == pl.program_id(0), a_ref[...], b_ref[...])


def assemble(chain, core, chunk, length, a, b, so_far):
    height, d = a.shape
    block = whole((height, d))
    anywhere = pl.BlockSpec(memory_space=pl.ANY)
    return chain(
        assemble_kernel, "assemble", 2,
        [(a, block), (b, block)] + ([] if so_far is None else [(so_far, anywhere)]),
        [((length, d), BF16, pl.BlockSpec((height, d), lambda i, *s: (place_of(chunk, i), 0)))],
        scalars=(core,), alias=() if so_far is None else ((2, 0),), mib=16,
    )[0]


def close_chunk_kernel(closing, core_ref, *refs):
    refs[-1][...] = closing(*refs[:-1])


def close_chunk(chain, closing, core, chunk, a, b, own, small):
    height, d = a.shape
    part = height // 2
    block = rows(d, part)

    def mine(n):
        return pl.BlockSpec((part, n), lambda i, core: (2 * place_of(chunk, core[0]) + i, 0))

    return chain(
        partial(close_chunk_kernel, closing), "close", 2,
        [(a, block), (b, block)] + [(o, mine(o.shape[1])) for o in own] + [(small, whole(small.shape))],
        [(a.shape, BF16, block)],
        scalars=(core,),
    )[0]


def swap_cores(value, size):
    return lax.ppermute(value, "tensor", [(i, i ^ 1) for i in range(size)])


def along(value, hops):
    return lax.ppermute(
        value, "tensor", [(2 * a + c, 2 * b + c) for a, b in hops for c in (0, 1)]
    )


def grad_rows(a, b, x, stats, g, small):
    u = (a[...].astype(F32) + b[...].astype(F32)) * small[0:1]
    mean, inverse = stats[:, 0:1], stats[:, 1:2]
    scaled = (x[...].astype(F32) - mean) * inverse
    back_u = inverse * (
        u
        - jnp.mean(u, axis=-1, keepdims=True)
        - scaled * jnp.mean(u * scaled, axis=-1, keepdims=True)
    )
    return (g[...].astype(F32) + back_u).astype(BF16)


PIECE = TILE // 2


def line_kernel(
    first, gq, gk, gv, pre, x_block, stats_block, wq, wu, small, extra, x_all, g_all, stats_all, *refs
):
    parts, refs = refs[: first // 2], refs[first // 2 :]
    output, grad, vectors = refs[:3]
    held, came, own, lines, across, x_own, g_own, stats_own, sums, by_dp, mine, by_tensor = refs[3:15]
    (
        load_sem, peer_send, peer_recv, in_send, in_recv, mid_send, mid_recv, out_send, out_recv,
        fin_send, fin_recv, keep_sem,
    ) = refs[15:]
    chunks = came.shape[0]
    i = pl.program_id(0)
    pieces = 2 * chunks
    d = came.shape[2]
    row, me = lax.axis_index("dp"), lax.axis_index("tensor")
    count, size = by_dp.shape[0], by_tensor.shape[0]
    core = lax.rem(me, 2)
    chip = me // 2
    peer = me + 1 - 2 * core
    beside = 2 * (chip + 1 - 2 * lax.rem(chip, 2)) + core
    facing = 2 * (3 - chip) + core
    middle = (chip == 1) | (chip == 2)
    end = jnp.logical_not(middle)
    mesh = pl.DeviceIdType.MESH
    barrier = pltpu.get_barrier_semaphore()

    def remote(source, target, send_sem, recv_sem, device, axis="tensor"):
        return pltpu.make_async_remote_copy(
            src_ref=source, dst_ref=target, send_sem=send_sem, recv_sem=recv_sem,
            device_id={axis: device}, device_id_type=mesh,
        )

    shift = pieces - first
    every = pieces + first

    def place(p, before=0):
        start = place_of(p // 2, core) * TILE + lax.rem(p, 2) * PIECE - before
        return pl.ds(pl.multiple_of(start, PIECE), PIECE)

    def peer_copy(c):
        return remote(held.at[c], came.at[c], peer_send.at[c], peer_recv.at[c], peer)

    def in_copy(p):
        return remote(own.at[p], lines.at[p], in_send.at[p], in_recv.at[p], beside)

    def mid_copy(p):
        return remote(own.at[p], across.at[p], mid_send.at[p], mid_recv.at[p], facing)

    def out_copy(p):
        return remote(lines.at[p], lines.at[p], out_send.at[p], out_recv.at[p], beside)

    def fin_copy(p, target):
        return remote(lines.at[p], target, fin_send.at[p], fin_recv.at[p], peer)

    def keep_copy(p, target):
        return pltpu.make_async_copy(lines.at[p], target, keep_sem.at[p])

    def part_copy(p):
        return pltpu.make_async_copy(
            parts[p // 2].at[pl.ds(p % 2 * PIECE, PIECE)], own.at[p], keep_sem.at[p]
        )

    def of(p, action):
        @pl.when(p < first)
        def _():
            action(p, output.at[place(p + shift, shift * 2 * PIECE)])

        @pl.when(p >= first)
        def _():
            action(p, grad.at[place(p - first)])

    def loads(p):
        return [
            pltpu.make_async_copy(array.at[place(p)], here.at[p], load_sem.at[n, p])
            for n, (array, here) in enumerate(((x_all, x_own), (g_all, g_own), (stats_all, stats_own)))
        ]

    def dp_copy(n):
        device = lax.rem(row + n, count)
        wide = d // count
        source = sums.at[:, pl.ds(pl.multiple_of(device * wide, 128), wide)]
        return remote(source, by_dp.at[n], load_sem.at[3, n], load_sem.at[4, n], device, "dp")

    def tensor_copy(n):
        device = lax.rem(me + n, size)
        return remote(mine, by_tensor.at[n], load_sem.at[5, n], load_sem.at[6, n], device)

    def hand_over(p, target):
        fin_copy(p, target).start()
        keep_copy(p, target).start()

    def take_in(p):
        in_copy(p).wait_recv()
        own[p] = (own[p].astype(F32) + lines[p].astype(F32)).astype(BF16)
        mid_copy(p).start()

    def finish(p):
        mid_copy(p).wait_recv()

        @pl.when(p < first)
        def _():
            q = p + shift
            lines[p] = output_rows(own[p], x_own[q], across[p], small[...])

        @pl.when(p >= first)
        def _():
            q = p - first
            lines[p] = grad_rows(own[p], across[p], x_own[q], stats_own[q], g_own[q], small[...])

        out_copy(p).start()
        of(p, hand_over)

    def each(action, begin=0, stop=every):
        lax.fori_loop(begin, stop, lambda p, _: (action(p), 0)[1], 0)

    @pl.when(i == 0)
    def _():
        for n in range(1, count):
            pl.semaphore_signal(
                barrier, inc=1, device_id={"dp": lax.rem(row + n, count)}, device_id_type=mesh
            )
        for n in range(1, size):
            pl.semaphore_signal(
                barrier, inc=1, device_id={"tensor": lax.rem(me + n, size)}, device_id_type=mesh
            )
        sums[...] = extra[...]
        for p in range(first):
            part_copy(p).start()
        pl.semaphore_wait(barrier, count + size - 2)
        for p in range(first):
            part_copy(p).wait()

    @pl.when((i == 0) & end)
    def _():
        each(lambda p: in_copy(p).start(), 0, first)

    @pl.when((i == 0) & middle)
    def _():
        each(lambda p: [load.start() for load in loads(p)], 0, pieces)
        each(lambda p: [load.wait() for load in loads(p)], 0, pieces)

    ours = lax.rem(i, 2)
    half = i // 2
    to = pl.ds(first + 2 * half, 2)
    for cut in range(0, d, 2 * TILE):
        cut = slice(cut, cut + 2 * TILE)
        total = nt(pre[...], wu[cut])
        for c, g in enumerate((gq, gk, gv)):
            total = total + nt(g[...], wq[c, cut])
        scaled = (x_block[:, cut].astype(F32) - stats_block[:, 0:1]) * stats_block[:, 1:2]
        sums[0:1, cut] += jnp.sum(total * scaled, axis=0, keepdims=True)
        sums[1:2, cut] += jnp.sum(total, axis=0, keepdims=True)
        total = total.astype(BF16)

        @pl.when(ours == 0)
        def _():
            held[half, :, cut] = total

        @pl.when(ours == 1)
        def _():
            own[to, :, cut] = total.reshape(2, PIECE, 2 * TILE)

    @pl.when(ours == 0)
    def _():
        peer_copy(half).start()

    @pl.when(ours == 1)
    def _():
        peer_copy(half).wait_recv()
        total = own[to].astype(F32) + came[half].reshape(2, PIECE, d).astype(F32)
        own[to] = total.astype(BF16)

    @pl.when((ours == 1) & end)
    def _():
        in_copy(first + 2 * half).start()
        in_copy(first + 2 * half + 1).start()

    early = 4
    begin = pieces - early

    @pl.when((i >= begin) & middle)
    def _():
        take_in(i - begin)

    @pl.when((i > begin) & middle)
    def _():
        finish(i - begin - 1)

    @pl.when(i == pieces - 1)
    def _():
        for n in range(1, count):
            dp_copy(n).start()

    def both(p, _):
        take_in(p)
        finish(p - 1)
        return 0

    def pass_on(p):
        out_copy(p).wait_recv()
        of(p, hand_over)

    some = early + 2

    @pl.when((i == pieces - 1) & middle)
    def _():
        lax.fori_loop(early, some, both, 0)

    @pl.when((i == pieces - 1) & end)
    def _():
        each(pass_on, 0, some)

    @pl.when(i == pieces - 1)
    def _():
        wide = d // count
        total = sums[:, pl.ds(pl.multiple_of(row * wide, 128), wide)]
        for n in range(1, count):
            dp_copy(n).wait()
            total = total + by_dp[n]
        mine[...] = total
        for n in range(1, size):
            tensor_copy(n).start()

    @pl.when((i == pieces - 1) & middle)
    def _():
        lax.fori_loop(some, every, both, 0)
        finish(every - 1)
        each(lambda p: (mid_copy(p).wait_send(), out_copy(p).wait_send()))

    @pl.when((i == pieces - 1) & end)
    def _():
        each(pass_on, some)
        each(lambda p: in_copy(p).wait_send())

    @pl.when(i == pieces - 1)
    def _():
        total = mine[...]
        for n in range(1, size):
            tensor_copy(n).wait()
            total = total + by_tensor[n]
        vectors[...] = jnp.concatenate([total[:2], mine[2:]])
        for c in range(chunks):
            peer_copy(c).wait_send()
        each(lambda p: of(p, lambda *a: (fin_copy(*a).wait(), keep_copy(*a).wait())))


def line_back(chain, parts, chunks, size, count, gq, gk, gv, pre, x, stats, wq, wu, small, extra, g):
    length, d = x.shape
    width, units = wq.shape[2], wu.shape[1]
    pieces, first = 2 * chunks, 2 * len(parts)

    def block(n):
        def index(i):
            core = lax.rem(lax.axis_index("tensor"), 2)
            mine = lax.rem(i, 2)
            return (place_of(i // 2, lax.rem(core + 1 + mine, 2)), 0)

        return pl.BlockSpec((TILE, n), index)

    def once(shape):
        zeros = (0,) * len(shape)
        return pl.BlockSpec(shape, lambda *i: zeros, pipeline_mode=pl.Buffered(1))

    far = pl.BlockSpec(memory_space=pltpu.HBM)
    rows_of = lambda n: pltpu.VMEM((n, PIECE, d), BF16)
    sems = pltpu.SemaphoreType.DMA
    vector = (8, d // count)
    return chain(
        partial(line_kernel, first),
        "line_back",
        pieces,
        [(a, block(width)) for a in (gq, gk, gv)]
        + [
            (pre, block(units)), (x, block(d)), (stats, block(PAIR)), (wq, once(wq.shape)),
            (wu, once(wu.shape)), (small, once(small.shape)), (extra, once(extra.shape)),
            (x, far), (g, far), (stats, far),
        ]
        + [(p, far) for p in parts],
        [
            ((first * 2 * PIECE, d), BF16, far), ((length, d), BF16, far),
            (vector, F32, whole(vector)),
        ],
        scratch=[
            pltpu.VMEM((chunks, TILE, d), BF16), pltpu.VMEM((chunks, TILE, d), BF16),
            rows_of(first + pieces), rows_of(first + pieces), rows_of(first + pieces),
            rows_of(pieces), rows_of(pieces),
            pltpu.VMEM((pieces, PIECE, PAIR), F32),
            pltpu.VMEM((8, d), F32), pltpu.VMEM((count, *vector), F32), pltpu.VMEM(vector, F32),
            pltpu.VMEM((size, *vector), F32),
            sems((7, max(pieces, size, count))), sems((chunks,)), sems((chunks,)),
        ]
        + [sems((first + pieces,))] * 9,
        collective=5,
        flops=200e9,
        mib=62,
    )


def flow(chain, size, core, chunk, total, closing, results, key, length):
    chips = size // 2
    chip = lax.axis_index("tensor") // 2
    distance = jnp.where(chip < chips // 2, chips // 2 - 1 - chip, chip - chips // 2)
    for s in range(chips // 2 - 1):
        came = along(total, [(s, s + 1), (chips - 1 - s, chips - 2 - s)])
        yield
        total = plus(chain, total, came)
    a, b = chips // 2 - 1, chips // 2
    came = along(total, [(a, b), (b, a)])
    yield
    value = closing(chunk, total, came)
    for s in range(chips // 2 - 1):
        a, b = chips // 2 - 1 - s, chips // 2 + s
        came = along(value, [(a, a - 1), (b, b + 1)])
        yield
        value = choose(chain, (distance == s + 1).astype(jnp.int32)[None], value, came)
    peer = swap_cores(value, size)
    yield
    results[key] = assemble(chain, core, chunk, length, value, peer, results.get(key))


def on_device(
    size,
    inputs,
    segment_ids,
    norm_gain,
    norm_bias,
    qkv_weight,
    qkv_bias,
    out_weight,
    out_bias,
    up_weight,
    up_bias,
    down_weight,
    down_bias,
    cotangent,
):
    x, g, segment_row = inputs[0], cotangent[0], segment_ids[0]
    length, d = x.shape
    width, units = qkv_weight.shape[2], up_weight.shape[1]
    count = lax.axis_size("dp")
    core = (lax.axis_index("tensor") % 2).astype(jnp.int32)[None]

    start = jnp.sum((segment_row[None, :] < segment_row[:, None]).astype(jnp.int32), axis=1)
    small = jnp.stack([norm_gain, norm_bias, out_bias, down_bias] + [norm_gain] * 4).astype(F32)
    wq = qkv_weight.transpose(1, 0, 2)

    chain = Chain()
    normed, stats, q, k, v, hidden, slope, cos_wide, sin_wide = first(
        chain, x, small, wq, qkv_bias, up_weight, up_bias, start
    )
    mixed, log = attend(chain, start, q, k, v)
    rest = 2 if size == 8 else 0
    lower = length - rest * (length // CHUNKS)
    weights = (mixed, hidden, out_weight, down_weight)
    summed = lax.psum(branch(chain, lower, *weights), "tensor")
    parts = branch_rest(chain, rest, CHUNKS - rest, *weights) if rest else []

    pre, gm, delta, g_sums, up_sums = back(chain, g, slope, mixed, out_weight, down_weight)
    scatter = lambda a: lax.psum_scatter(a, "dp", scatter_dimension=1, tiled=True)
    near = scatter(weight_grad(chain, "weight_grad_g", [hidden, mixed], g))
    tiles = length // TILE
    *packed, qkv_sums, _ = attend_back(
        chain, 0, tiles, start, log, delta, q, k, v, gm, cos_wide, sin_wide, [log]
    )
    far = scatter(weight_grad(chain, "weight_grad_n", [pre, *packed], normed))

    by_share = lambda a: a.reshape(-1, count, HD // count).swapaxes(0, 1).reshape(count, -1)
    part = d // count
    narrow = jnp.concatenate([by_share(up_sums[0]), by_share(qkv_sums[:3])], axis=1)
    narrow = jnp.pad(narrow, ((0, 0), (0, part - narrow.shape[1]))).reshape(1, d)
    if size == 8:
        extra = jnp.concatenate([jnp.zeros((2, d), F32), g_sums[:1], narrow, jnp.zeros((4, d), F32)])
        upper, grad, vectors = line_back(
            chain, parts, CHUNKS, size, count, *packed, pre, x, stats, wq, up_weight, small, extra, g
        )
    else:

        results = {}

        def line(parts, closing, own, key):
            finish = lambda chunk, a, b: close_chunk(chain, closing, core, chunk, a, b, own, small)
            flows = [
                flow(chain, size, core, c, parts[c], finish, results, key, length)
                for c in range(CHUNKS)
            ]
            while flows:
                flows = [f for f in flows if next(f, flows) is None]

        norm_sums, *parts = normed_back(chain, CHUNKS, *packed, pre, x, stats, wq, up_weight)
        line(parts, grad_rows, [x, stats, g], "grad")
        vectors = jnp.concatenate([norm_sums[:2], g_sums[:1], narrow]).reshape(4, count, part)
        vectors = vectors.swapaxes(0, 1).reshape(count, -1, 128)
        vectors = add_vectors(chain, vectors, size, count).reshape(4, part)
    if size == 8:
        output, input_grad, down_share, out_share, up_share, qkv_share = last(
            chain, summed, x, small, upper, grad, near, far, width, units
        )
    else:
        output, input_grad = close_both(chain, summed, x, small, results["grad"])
        shapes = [(units, part), (width, part)]
        down_share, out_share = widen(chain, near, shapes, (False, False))
        shapes = [(part, units), (3, part, width)]
        up_share, qkv_share = widen(chain, far, shapes, (True, True))
    up_b_share = vectors[3, : units // count].reshape(-1, HD // count)
    qkv_b_share = vectors[3, units // count : (units + 3 * width) // count].reshape(3, -1, HD // count)

    return (
        output[None],
        input_grad[None],
        vectors[0],
        vectors[1],
        qkv_share.transpose(1, 0, 2),
        qkv_b_share,
        out_share,
        vectors[2],
        up_share,
        up_b_share,
        down_share,
        vectors[2],
    )


def solution(mesh):
    placed = (
        P("dp", None, None),
        P("dp", None),
        P(),
        P(),
        P(None, None, "tensor"),
        P(None, "tensor"),
        P("tensor", None),
        P(),
        P(None, "tensor"),
        P("tensor"),
        P("tensor", None),
        P(),
        P("dp", None, None),
    )
    return jax.shard_map(
        partial(on_device, mesh.shape["tensor"]),
        mesh=mesh,
        in_specs=placed,
        out_specs=(
            P("dp", None, None),
            P("dp", None, None),
            P("dp"),
            P("dp"),
            P("dp", None, "tensor"),
            P(None, "tensor", "dp"),
            P("tensor", "dp"),
            P("dp"),
            P("dp", "tensor"),
            P("tensor", "dp"),
            P("tensor", "dp"),
            P("dp"),
        ),
        check_vma=False,
    )
```

```python
from functools import partial

import jax
import jax.numpy as jnp
from jax import lax
from jax.experimental import pallas as pl
from jax.experimental.pallas import tpu as pltpu
from jax.sharding import PartitionSpec as P

HD = 64
ROT = 32
PAIR = 2 * HD
TILE = 256
CHUNKS = 4
NEG = -1e30
MIB = 1 << 20
F32 = jnp.float32
BF16 = jnp.bfloat16


class Chain:
    def __init__(self):
        self.link = jnp.zeros((8, 128), F32)

    def __call__(
        self, kernel, name, grid, ins, outs, scalars=(), scratch=(), alias=(), mib=58, flops=1, collective=None
    ):
        taken, given = len(scalars) + len(ins), len(outs)

        def body(*refs):
            kernel(*refs[:taken], *refs[taken + 1 : taken + 1 + given], *refs[taken + 2 + given :])

        anywhere = pl.BlockSpec(memory_space=pltpu.HBM)
        results = pl.pallas_call(
            body,
            grid_spec=pltpu.PrefetchScalarGridSpec(
                num_scalar_prefetch=len(scalars),
                grid=(grid,),
                in_specs=[spec for _, spec in ins] + [anywhere],
                out_specs=[spec for _, _, spec in outs] + [anywhere],
                scratch_shapes=list(scratch),
            ),
            out_shape=[jax.ShapeDtypeStruct(shape, dtype) for shape, dtype, _ in outs]
            + [jax.ShapeDtypeStruct(self.link.shape, F32)],
            input_output_aliases={taken: given, **{len(scalars) + i: o for i, o in alias}},
            compiler_params=pltpu.CompilerParams(
                dimension_semantics=("arbitrary",), vmem_limit_bytes=mib * MIB,
                collective_id=collective, has_side_effects=collective is not None,
            ),
            cost_estimate=pl.CostEstimate(flops=int(flops), bytes_accessed=1, transcendentals=0),
            name=name,
        )(*scalars, *[array for array, _ in ins], self.link)
        self.link = results[-1]
        return results[:-1]


def whole(shape):
    zeros = (0,) * len(shape)
    return pl.BlockSpec(shape, lambda *i: zeros)


def rows(n, height=TILE):
    return pl.BlockSpec((height, n), lambda i, *s: (i, 0))


def nn(a, b):
    return lax.dot_general(a, b, (((1,), (0,)), ((), ())), preferred_element_type=F32)


def nt(a, b):
    return lax.dot_general(a, b, (((1,), (1,)), ((), ())), preferred_element_type=F32)


def tn(a, b):
    return lax.dot_general(a, b, (((0,), (0,)), ((), ())), preferred_element_type=F32)


def rotated(x, cos_wide, sin_wide):
    lane = lax.broadcasted_iota(jnp.int32, x.shape, 1) % HD
    half = ROT // 2
    other = jnp.where(
        lane < half, pltpu.roll(x, PAIR - half, 1), pltpu.roll(x, half, 1)
    )
    return x * cos_wide + other * sin_wide


def row_stats(x):
    mean = jnp.mean(x, axis=-1, keepdims=True)
    centered = x - mean
    inverse = lax.rsqrt(jnp.mean(centered * centered, axis=-1, keepdims=True) + 1e-05)
    return centered * inverse, mean, inverse


def gelu_both(u):
    c = 0.7978845608028654
    u2 = u * u
    gate = 0.5 + 0.5 * jnp.tanh(u * (c + (c * 0.044715) * u2))
    value = u * gate
    slope = gate + value * (1.0 - gate) * (2.0 * c + (6.0 * c * 0.044715) * u2)
    return value, slope


def first_kernel(
    x0_ref, x1_ref, x2_ref, small_ref, wq_ref, bq_ref, wu_ref, bu_ref, start_ref, freq_ref,
    normed_ref, stats_ref, q_ref, k_ref, v_ref, hidden_ref, slope_ref, cos_ref, sin_ref,
    even, odd, even_stats,
):
    s = pl.program_id(0)
    gain, shift = small_ref[0:1], small_ref[1:2]
    lane = lax.broadcasted_iota(jnp.int32, (TILE, PAIR), 1)

    def norm(x):
        scaled, mean, inverse = row_stats(x.astype(F32))
        return (scaled * gain + shift).astype(BF16), jnp.where(lane == 0, mean, inverse)

    @pl.when(s == 0)
    def _():
        even[...], even_stats[...] = norm(x0_ref[...])

    half = ROT // 2
    unit = lax.broadcasted_iota(jnp.int32, (half, PAIR), 1) % HD
    index = lax.broadcasted_iota(jnp.int32, (half, PAIR), 0)
    first_half = (unit == index).astype(F32)
    second_half = (unit == index + half).astype(F32)
    bias = bq_ref[...].astype(F32)

    def spread(a, b):
        return lax.dot_general(
            a, b, (((0,), (0,)), ((), ())), precision=lax.Precision.HIGHEST,
            preferred_element_type=F32,
        )

    def project(t, normed):
        here = slice(t * TILE, (t + 1) * TILE)
        place = lax.broadcasted_iota(jnp.int32, (1, TILE), 1) + (2 * s + t) * TILE
        angle = freq_ref[...] * (place - start_ref[:, here]).astype(F32)
        cos_wide = spread(jnp.cos(angle), first_half + second_half)
        cos_wide = jnp.where(lane % HD < ROT, cos_wide, 1.0)
        sin_wide = spread(jnp.sin(angle), second_half - first_half)
        cos_ref[here], sin_ref[here] = cos_wide, sin_wide
        for c, out in enumerate((q_ref, k_ref, v_ref)):
            packed = nn(normed, wq_ref[c]) + bias[c : c + 1]
            if c == 2:
                out[here] = packed.astype(BF16)
            else:
                for p in range(packed.shape[1] // PAIR):
                    cut = slice(p * PAIR, (p + 1) * PAIR)
                    turned = rotated(packed[:, cut], cos_wide, sin_wide).astype(BF16)
                    out[here, cut] = turned * (HD**-0.5) if c == 0 else turned
        units = wu_ref.shape[1]
        for n in range(0, units, TILE):
            cut = slice(n, n + TILE)
            value, slope = gelu_both(nn(normed, wu_ref[:, cut]) + bu_ref[:, cut])
            hidden_ref[here, cut] = value.astype(BF16)
            slope_ref[here, cut] = slope.astype(BF16)

    normed = even[...]
    normed_ref[:TILE] = normed
    stats_ref[:TILE] = even_stats[...]
    after, after_stats = norm(x1_ref[...])
    odd[...] = after
    normed_ref[TILE:] = after
    stats_ref[TILE:] = after_stats
    project(0, normed)
    even[...], even_stats[...] = norm(x2_ref[...])
    project(1, odd[...])


def first(chain, x, small, wq, bq, wu, bu, start):
    length, d = x.shape
    width, units = wq.shape[2], wu.shape[1]
    tiles = length // TILE
    freq = 10000.0 ** (-jnp.arange(ROT // 2, dtype=F32) * 2.0 / ROT)
    at = lambda f: pl.BlockSpec((TILE, d), lambda s: (f(s), 0))
    big = lambda n: rows(n, 2 * TILE)
    return chain(
        first_kernel,
        "first",
        tiles // 2,
        [
            (x, at(lambda s: 0)),
            (x, at(lambda s: 2 * s + 1)),
            (x, at(lambda s: jnp.minimum(2 * s + 2, tiles - 1))),
            (small, whole(small.shape)), (wq, whole(wq.shape)), (bq, whole(bq.shape)),
            (wu, whole(wu.shape)), (bu[None].astype(F32), whole((1, units))),
            (start[None], pl.BlockSpec((1, 2 * TILE), lambda s: (0, s))),
            (jnp.broadcast_to(freq[:, None], (ROT // 2, TILE)), whole((ROT // 2, TILE))),
        ],
        [((length, d), BF16, big(d)), ((length, PAIR), F32, big(PAIR))]
        + [((length, n), BF16, big(n)) for n in (width, width, width, units, units)]
        + [((length, PAIR), F32, big(PAIR))] * 2,
        scratch=[pltpu.VMEM((TILE, d), BF16)] * 2 + [pltpu.VMEM((TILE, PAIR), F32)],
        mib=40,
        flops=35e9,
    )


def halves(x):
    left = lax.broadcasted_iota(jnp.int32, x.shape, 1) < HD
    zero = jnp.zeros(x.shape, x.dtype)
    return [jnp.where(left, x, zero), jnp.where(left, zero, x)]


def pair_cuts(width):
    return [slice(p, p + PAIR) for p in range(0, width, PAIR)]


def attend_kernel(start_sref, start_ref, q_ref, k_ref, v_ref, mixed_ref, log_ref):
    i = pl.program_id(0)
    cuts = pair_cuts(q_ref.shape[1])
    heads = range(2 * len(cuts))
    key_row = lax.broadcasted_iota(jnp.int32, (TILE, TILE), 0)
    query = lax.broadcasted_iota(jnp.int32, (TILE, TILE), 1) + i * TILE
    start = start_ref[...]
    queries = [q for cut in cuts for q in halves(q_ref[:, cut])]

    def step(j, carry):
        tops, totals, sums = carry
        there = pl.ds(pl.multiple_of(j * TILE, TILE), TILE)
        place = key_row + j * TILE
        allowed = (place >= start) & (place <= query)
        k = [k_ref[there, cut] for cut in cuts]
        v = [v_ref[there, cut] for cut in cuts]
        s = [nt(k[h // 2], queries[h]) for h in heads]
        s = [jnp.where(allowed, a, NEG) for a in s]
        top = [jnp.maximum(tops[h], jnp.max(s[h], axis=0, keepdims=True)) for h in heads]
        alpha = [jnp.exp(tops[h] - top[h]) for h in heads]
        w = [jnp.exp(s[h] - top[h]) for h in heads]
        totals = [totals[h] * alpha[h] + jnp.sum(w[h], axis=0, keepdims=True) for h in heads]
        w = [a.astype(BF16) for a in w]
        add = [tn(v[h // 2], w[h])[h % 2 * HD : (h % 2 + 1) * HD] for h in heads]
        sums = [sums[h] * alpha[h] + add[h] for h in heads]
        return tuple(top), tuple(totals), tuple(sums)

    empty = (
        tuple(jnp.full((1, TILE), NEG, F32) for _ in heads),
        tuple(jnp.zeros((1, TILE), F32) for _ in heads),
        tuple(jnp.zeros((HD, TILE), F32) for _ in heads),
    )
    low = start_sref[i * TILE] // TILE
    tops, totals, sums = lax.fori_loop(low, i + 1, step, empty)
    log_ref[...] = jnp.zeros_like(log_ref)
    for h in heads:
        log_ref[h : h + 1] = tops[h] + jnp.log(totals[h])
    mixed_ref[...] = jnp.concatenate([sums[h] * (1.0 / totals[h]) for h in heads]).T.astype(BF16)


def attend(chain, start, q, k, v):
    length, width = q.shape
    full = whole((length, width))
    return chain(
        attend_kernel,
        "attend",
        length // TILE,
        [
            (start[None], pl.BlockSpec((1, TILE), lambda i, *s: (0, i))),
            (q, rows(width)), (k, full), (v, full),
        ],
        [
            ((length, width), BF16, rows(width)),
            ((8, length), F32, pl.BlockSpec((8, TILE), lambda i, *s: (0, i))),
        ],
        scalars=(start,),
        mib=24,
        flops=19e9,
    )


def attend_back_kernel(
    begin, start_sref, start_ref, log_ref, delta_ref, q_ref, k_ref, v_ref, g_ref, cos_ref, sin_ref,
    totals_in, *refs,
):
    gq_ref, gk_ref, gv_ref, bias_ref, totals = refs[-5:]
    j = pl.program_id(0) + begin
    length, width = q_ref.shape
    cuts = pair_cuts(width)
    heads = range(2 * len(cuts))
    here = pl.ds(pl.multiple_of(j * TILE, TILE), TILE)

    @pl.when(pl.program_id(0) == 0)
    def _():
        totals[...] = totals_in[...] if begin else jnp.zeros_like(totals)
        bias_ref[...] = jnp.zeros_like(bias_ref)

    place = j * TILE + lax.broadcasted_iota(jnp.int32, (TILE, TILE), 0)
    query = lax.broadcasted_iota(jnp.int32, (TILE, TILE), 1)
    keys = [k_ref[here, cut] for cut in cuts]
    split = [half for k in keys for half in halves(k)]
    values = [v_ref[here, cut] for cut in cuts]

    def step(i, carry):
        gk, gv = carry
        there = pl.ds(pl.multiple_of(i * TILE, TILE), TILE)
        allowed = (place >= start_ref[:, there]) & (place <= query + i * TILE)
        qs = [half for cut in cuts for half in halves(q_ref[there, cut])]
        gs = [half for cut in cuts for half in halves(g_ref[there, cut])]
        s = [nt(keys[h // 2], qs[h]) for h in heads]
        gp = [nt(values[h // 2], gs[h]) for h in heads]
        w = [jnp.exp(jnp.where(allowed, s[h] - log_ref[h : h + 1, there], NEG)) for h in heads]
        ds = [(w[h] * (gp[h] - delta_ref[h : h + 1, there])).astype(BF16) for h in heads]
        w = [a.astype(BF16) for a in w]
        both = lambda f: tuple(f(h) + f(h + 1) for h in heads[::2])
        gv = [a + b for a, b in zip(gv, both(lambda h: nn(w[h], gs[h])))]
        gk = [a + b for a, b in zip(gk, both(lambda h: nn(ds[h], qs[h])))]
        for cut, gq in zip(cuts, both(lambda h: tn(ds[h], split[h]))):
            totals[there, cut] += gq
        return tuple(gk), tuple(gv)

    high = sum((start_sref[b * TILE] < (j + 1) * TILE).astype(jnp.int32) for b in range(length // TILE))
    empty = tuple(jnp.zeros((TILE, PAIR), F32) for _ in cuts)
    gks, gvs = lax.fori_loop(j, high, step, (empty, empty))
    cos_wide, sin_wide = cos_ref[...], -sin_ref[...]
    for cut, gk, gv in zip(cuts, gks, gvs):
        gq = rotated(totals[here, cut] * (HD**-0.5), cos_wide, sin_wide).astype(BF16)
        gk = rotated(gk, cos_wide, sin_wide).astype(BF16)
        for c, (g, out) in enumerate(((gq, gq_ref), (gk, gk_ref), (gv.astype(BF16), gv_ref))):
            out[:, cut] = g
            bias_ref[c : c + 1, cut] += jnp.sum(g.astype(F32), axis=0, keepdims=True)


def attend_back(chain, begin, end, start, log, delta, q, k, v, g, cos_wide, sin_wide, before):
    length, width = q.shape
    full = whole((length, width))
    shifted = lambda n: pl.BlockSpec((TILE, n), lambda i, *s: (i + begin, 0))
    anywhere = pl.BlockSpec(memory_space=pl.ANY)
    so_far = before[:3] if begin else []
    return chain(
        partial(attend_back_kernel, begin),
        f"attend_back_{begin}",
        end - begin,
        [
            (start[None], whole((1, length))), (log, whole((8, length))), (delta, whole((8, length))),
            (q, full), (k, full), (v, full), (g, full), (cos_wide, shifted(PAIR)), (sin_wide, shifted(PAIR)),
            (before[-1], full if begin else anywhere),
        ]
        + [(a, anywhere) for a in so_far],
        [((length, width), BF16, shifted(width))] * 3
        + [((8, width), F32, whole((8, width))), ((length, width), F32, full)],
        scalars=(start,),
        alias=tuple((10 + n, n) for n in range(len(so_far))),
        flops=31e9,
    )


def place_of(chunk, core):
    return 4 * (chunk // 2) + 2 * core + chunk % 2


def own_rows(chunks, half, skip=0):
    def spec(n):
        def index(i):
            core = lax.rem(lax.axis_index("tensor"), 2)
            steps = chunks // 2
            return (skip + 2 * lax.rem(i, steps) + jnp.where(i < steps, 1 - core, core), 0)

        return pl.BlockSpec((2 * half, n), index)

    return spec


def paired(product, chunks, ins, *refs):
    given, extra, sums, held, came, send_sem, recv_sem = (
        refs[:ins], refs[ins : len(refs) - chunks - 4], refs[-chunks - 4 : -4], *refs[-4:]
    )
    i = pl.program_id(0)
    steps = chunks // 2
    half, d = sums[0].shape
    me = lax.axis_index("tensor")
    peer = me + 1 - 2 * lax.rem(me, 2)
    barrier = pltpu.get_barrier_semaphore()

    def copy(n):
        return pltpu.make_async_remote_copy(
            src_ref=held.at[n], dst_ref=came.at[n], send_sem=send_sem.at[n], recv_sem=recv_sem.at[n],
            device_id={"tensor": peer}, device_id_type=pl.DeviceIdType.MESH,
        )

    @pl.when(i == 0)
    def _():
        pl.semaphore_signal(
            barrier, inc=1, device_id={"tensor": peer}, device_id_type=pl.DeviceIdType.MESH
        )
        for e in extra:
            e[...] = jnp.zeros_like(e)

    for cut in range(0, d, 2 * TILE):
        cut = slice(cut, cut + 2 * TILE)
        total = product(cut, given, extra).astype(BF16)
        held[pl.ds(2 * i, 2), :, cut] = total.reshape(2, half, 2 * TILE)

    @pl.when(i == 0)
    def _():
        pl.semaphore_wait(barrier, 1)

    for n in range(steps):

        @pl.when(i == n)
        def _(n=n):
            copy(2 * n).start()
            copy(2 * n + 1).start()

        @pl.when(i == steps + n)
        def _(n=n):
            for c in (2 * n, 2 * n + 1):
                copy(c).wait()
                total = held[chunks + c].astype(F32) + came[c].astype(F32)
                sums[c][...] = total.astype(BF16)


def pair_call(chain, product, name, collective, chunks, half, d, ins, extra):
    return chain(
        partial(paired, product, chunks, len(ins)),
        name,
        chunks,
        ins,
        extra + [((half, d), BF16, whole((half, d)))] * chunks,
        scratch=[pltpu.VMEM((2 * chunks, half, d), BF16), pltpu.VMEM((chunks, half, d), BF16)]
        + [pltpu.SemaphoreType.DMA((chunks,))] * 2,
        flops=13e9,
        collective=collective,
    )


def branch_kernel(mixed, hidden, wo, wd, out):
    for cut in range(0, out.shape[1], 2 * TILE):
        cut = slice(cut, cut + 2 * TILE)
        out[:, cut] = (nn(mixed[...], wo[:, cut]) + nn(hidden[...], wd[:, cut])).astype(BF16)


def branch(chain, length, mixed, hidden, wo, wd):
    d = wo.shape[1]
    big = lambda n: rows(n, 2 * TILE)
    return chain(
        branch_kernel,
        "branch",
        length // (2 * TILE),
        [
            (mixed, big(mixed.shape[1])), (hidden, big(hidden.shape[1])),
            (wo, whole(wo.shape)), (wd, whole(wd.shape)),
        ],
        [((length, d), BF16, big(d))],
        mib=30,
        flops=7e9,
    )[0]


def branch_product(cut, given, extra):
    mixed, hidden, wo, wd = given
    return nn(mixed[...], wo[:, cut]) + nn(hidden[...], wd[:, cut])


def branch_rest(chain, chunks, skip, mixed, hidden, wo, wd):
    length, d = mixed.shape[0], wo.shape[1]
    half = length // (2 * (chunks + skip))
    spec = own_rows(chunks, half, skip)
    ins = [
        (mixed, spec(mixed.shape[1])), (hidden, spec(hidden.shape[1])),
        (wo, whole(wo.shape)), (wd, whole(wd.shape)),
    ]
    return pair_call(chain, branch_product, "branch_rest", 1, chunks, half, d, ins, [])


def last_kernel(
    steps, summed, x, small, rest, grad, down_in, out_in, up_in, q_in, k_in, v_in,
    output, input_grad, down, out, up, qkv,
):
    i = pl.program_id(0)
    input_grad[...] = grad[...]
    down[...] = down_in[...].astype(F32)
    out[...] = out_in[...].astype(F32)
    up[...] = up_in[...].astype(F32).T
    for c, part in enumerate((q_in, k_in, v_in)):
        qkv[c] = part[...].astype(F32).T

    @pl.when(i < steps)
    def _():
        output[...] = output_rows(summed, x[...], None, small)

    @pl.when(i >= steps)
    def _():
        output[...] = rest[...]


def last(chain, summed, x, small, rest, grad, near, far, width, units):
    length, d = x.shape
    part = near.shape[1]
    lower = summed.shape[0]
    grid = 4
    high = length // grid
    steps = lower // high
    tall, slim, thin = units // grid, width // grid, part // grid
    block = rows(d, high)
    low = pl.BlockSpec((high, d), lambda i: (jnp.minimum(i, steps - 1), 0))
    upper = pl.BlockSpec((high, d), lambda i: (jnp.maximum(i - steps, 0), 0))
    third = lambda c: pl.BlockSpec((width, thin), lambda i: (units // width + c, i))
    return chain(
        partial(last_kernel, steps), "last", grid,
        [
            (summed, low), (x, low), (small, whole(small.shape)), (rest, upper), (grad, block),
            (near, rows(part, tall)),
            (near, pl.BlockSpec((slim, part), lambda i: (units // slim + i, 0))),
            (far, rows(part, tall)), (far, third(0)), (far, third(1)), (far, third(2)),
        ],
        [
            ((length, d), BF16, block), ((length, d), BF16, block),
            ((units, part), F32, rows(part, tall)), ((width, part), F32, rows(part, slim)),
            ((part, units), F32, pl.BlockSpec((part, tall), lambda i: (0, i))),
            ((3, part, width), F32, pl.BlockSpec((3, thin, width), lambda i: (0, i, 0))),
        ],
    )


def output_rows(a, x, b, small):
    total = a[...].astype(F32)
    if b is not None:
        total = total + b[...].astype(F32)
    return (x.astype(F32) + total + small[2:3] + small[3:4]).astype(BF16)


def close_kernel(summed, x, small, grad, output, input_grad):
    output[...] = output_rows(summed, x[...], None, small)
    input_grad[...] = grad[...]


def close_both(chain, summed, x, small, grad):
    length, d = x.shape
    block = rows(d, 2 * TILE)
    return chain(
        close_kernel, "close_both", length // (2 * TILE),
        [(summed, block), (x, block), (small, whole(small.shape)), (grad, block)],
        [((length, d), BF16, block)] * 2,
    )


def back_kernel(g_ref, slope_ref, mixed_ref, wo_ref, wd_ref, pre_ref, gm_ref, delta_ref, sums_ref, up_ref):
    @pl.when(pl.program_id(0) == 0)
    def _():
        sums_ref[...] = jnp.zeros_like(sums_ref)
        up_ref[...] = jnp.zeros_like(up_ref)

    g = g_ref[...]
    for n in range(0, wd_ref.shape[0], 2 * TILE):
        cut = slice(n, n + 2 * TILE)
        pre = (nt(g, wd_ref[cut]) * slope_ref[:, cut].astype(F32)).astype(BF16)
        pre_ref[:, cut] = pre
        up_ref[0:1, cut] += jnp.sum(pre.astype(F32), axis=0, keepdims=True)
    gm = nt(g, wo_ref[...]).astype(BF16)
    gm_ref[...] = gm
    product = gm.astype(F32) * mixed_ref[...].astype(F32)
    coarse = product.astype(BF16)
    fine = (product - coarse.astype(F32)).astype(BF16)
    width = gm.shape[1]
    pick = (
        lax.broadcasted_iota(jnp.int32, (8, width), 1) // HD
        == lax.broadcasted_iota(jnp.int32, (8, width), 0)
    ).astype(BF16)
    delta_ref[...] = nt(pick, coarse) + nt(pick, fine)
    sums_ref[0:1] += jnp.sum(g.astype(F32), axis=0, keepdims=True)


def back(chain, g, slope, mixed, wo, wd):
    length, d = g.shape
    width, units = wo.shape[0], wd.shape[0]
    big = lambda n: rows(n, 2 * TILE)
    return chain(
        back_kernel,
        "back",
        length // (2 * TILE),
        [
            (g, big(d)), (slope, big(units)), (mixed, big(width)),
            (wo, whole(wo.shape)), (wd, whole(wd.shape)),
        ],
        [
            ((length, units), BF16, big(units)), ((length, width), BF16, big(width)),
            ((8, length), F32, pl.BlockSpec((8, 2 * TILE), lambda i, *s: (0, i))),
            ((8, d), F32, whole((8, d))), ((8, units), F32, whole((8, units))),
        ],
        flops=15e9,
    )


def normed_back_product(cut, given, extra):
    gq, gk, gv, pre, x, stats, wq, wu = given
    (sums,) = extra
    total = nt(pre[...], wu[cut])
    for c, g in enumerate((gq, gk, gv)):
        total = total + nt(g[...], wq[c, cut])
    scaled = (x[:, cut].astype(F32) - stats[:, 0:1]) * stats[:, 1:2]
    sums[0:1, cut] += jnp.sum(total * scaled, axis=0, keepdims=True)
    sums[1:2, cut] += jnp.sum(total, axis=0, keepdims=True)
    return total


def normed_back(chain, chunks, gq, gk, gv, pre, x, stats, wq, wu):
    length, d = x.shape
    width, units = wq.shape[2], wu.shape[1]
    half = length // (2 * chunks)
    spec = own_rows(chunks, half)
    ins = [(a, spec(width)) for a in (gq, gk, gv)] + [
        (pre, spec(units)), (x, spec(d)), (stats, spec(PAIR)),
        (wq, whole(wq.shape)), (wu, whole(wu.shape)),
    ]
    return pair_call(
        chain, normed_back_product, "normed_back", 2, chunks, half, d, ins,
        [((8, d), F32, whole((8, d)))],
    )


def weight_grad_kernel(counts, *refs):
    *lefts, right, out = refs
    i = pl.program_id(0)
    done = 0
    for left, count in zip(lefts, counts):

        @pl.when((i >= done) & (i < done + count))
        def _(left=left):
            out[...] = tn(left[...], right[...]).astype(BF16)

        done += count


def weight_grad(chain, name, lefts, right):
    length, d = right.shape
    wide = min(TILE, *[a.shape[1] for a in lefts])
    counts = tuple(a.shape[1] // wide for a in lefts)
    ins, done = [], 0
    for a, count in zip(lefts, counts):
        place = lambda i, done=done, count=count: jnp.clip(i - done, 0, count - 1)
        ins.append((a, pl.BlockSpec((length, wide), lambda i, f=place: (0, f(i)))))
        done += count
    return chain(
        partial(weight_grad_kernel, counts),
        name,
        done,
        ins + [(right, whole(right.shape))],
        [((done * wide, d), BF16, rows(d, wide))],
        flops=2 * length * d * done * wide,
    )[0]


def vectors_kernel(size, count, vectors, total, came, part, wide, sems):
    row, me = lax.axis_index("dp"), lax.axis_index("tensor")
    barrier = pltpu.get_barrier_semaphore()
    mesh = pl.DeviceIdType.MESH
    half = part.shape[0] // 2

    def by_row(n):
        peer = lax.rem(row + n, count)
        return pltpu.make_async_remote_copy(
            src_ref=vectors.at[peer], dst_ref=came.at[n], send_sem=sems.at[0, n],
            recv_sem=sems.at[1, n], device_id={"dp": peer}, device_id_type=mesh,
        )

    def by_column(n):
        peer = lax.rem(me + n, size)
        return pltpu.make_async_remote_copy(
            src_ref=part.at[pl.ds(0, half)], dst_ref=wide.at[n], send_sem=sems.at[2, n],
            recv_sem=sems.at[3, n], device_id={"tensor": peer}, device_id_type=mesh,
        )

    for n in range(1, count):
        pl.semaphore_signal(
            barrier, inc=1, device_id={"dp": lax.rem(row + n, count)}, device_id_type=mesh
        )
    for n in range(1, size):
        pl.semaphore_signal(
            barrier, inc=1, device_id={"tensor": lax.rem(me + n, size)}, device_id_type=mesh
        )
    pl.semaphore_wait(barrier, count + size - 2)
    for n in range(1, count):
        by_row(n).start()
    mine = vectors[row]
    for n in range(1, count):
        by_row(n).wait()
        mine = mine + came[n]
    part[...] = mine
    for n in range(1, size):
        by_column(n).start()
    upper = mine[:half]
    for n in range(1, size):
        by_column(n).wait()
        upper = upper + wide[n]
    total[:half] = upper
    total[half:] = mine[half:]


def add_vectors(chain, vectors, size, count):
    small = vectors.shape[1:]
    return chain(
        partial(vectors_kernel, size, count), "add_vectors", 1, [(vectors, whole(vectors.shape))],
        [(small, F32, whole(small))],
        scratch=[
            pltpu.VMEM((count, *small), F32), pltpu.VMEM(small, F32),
            pltpu.VMEM((size, small[0] // 2, small[1]), F32),
            pltpu.SemaphoreType.DMA((4, max(size, count))),
        ],
        collective=6,
    )[0]


def widen_kernel(turned, share_ref, *outs):
    at = 0
    for out, turn in zip(outs, turned):
        if len(out.shape) == 3:
            for c in range(out.shape[0]):
                out[c] = share_ref[at : at + out.shape[2]].astype(F32).T
                at += out.shape[2]
        elif turn:
            out[...] = share_ref[at : at + out.shape[1]].astype(F32).T
            at += out.shape[1]
        else:
            out[...] = share_ref[at : at + out.shape[0]].astype(F32)
            at += out.shape[0]


def widen(chain, share, shapes, turned):
    return chain(
        partial(widen_kernel, turned), "widen", 1, [(share, whole(share.shape))],
        [(shape, F32, whole(shape)) for shape in shapes], mib=32,
    )


def add_kernel(a_ref, b_ref, out_ref):
    out_ref[...] = (a_ref[...].astype(F32) + b_ref[...].astype(F32)).astype(out_ref.dtype)


def plus(chain, a, b):
    block = whole(a.shape)
    return chain(
        add_kernel, "plus", 1, [(a, block), (b, block)], [(a.shape, a.dtype, block)], mib=16
    )[0]


def choose_kernel(flag_ref, a_ref, b_ref, out_ref):
    out_ref[...] = jnp.where(flag_ref[0] > 0, b_ref[...], a_ref[...])


def choose(chain, flag, a, b):
    height, d = a.shape
    block = rows(d, height // 2)
    return chain(
        choose_kernel, "choose", 2, [(a, block), (b, block)], [(a.shape, BF16, block)],
        scalars=(flag,),
    )[0]


def assemble_kernel(core_ref, a_ref, b_ref, *rest):
    rest[-1][...] = jnp.where(core_ref[0] == pl.program_id(0), a_ref[...], b_ref[...])


def assemble(chain, core, chunk, length, a, b, so_far):
    height, d = a.shape
    block = whole((height, d))
    anywhere = pl.BlockSpec(memory_space=pl.ANY)
    return chain(
        assemble_kernel, "assemble", 2,
        [(a, block), (b, block)] + ([] if so_far is None else [(so_far, anywhere)]),
        [((length, d), BF16, pl.BlockSpec((height, d), lambda i, *s: (place_of(chunk, i), 0)))],
        scalars=(core,), alias=() if so_far is None else ((2, 0),), mib=16,
    )[0]


def close_chunk_kernel(closing, core_ref, *refs):
    refs[-1][...] = closing(*refs[:-1])


def close_chunk(chain, closing, core, chunk, a, b, own, small):
    height, d = a.shape
    part = height // 2
    block = rows(d, part)

    def mine(n):
        return pl.BlockSpec((part, n), lambda i, core: (2 * place_of(chunk, core[0]) + i, 0))

    return chain(
        partial(close_chunk_kernel, closing), "close", 2,
        [(a, block), (b, block)] + [(o, mine(o.shape[1])) for o in own] + [(small, whole(small.shape))],
        [(a.shape, BF16, block)],
        scalars=(core,),
    )[0]


def swap_cores(value, size):
    return lax.ppermute(value, "tensor", [(i, i ^ 1) for i in range(size)])


def along(value, hops):
    return lax.ppermute(
        value, "tensor", [(2 * a + c, 2 * b + c) for a, b in hops for c in (0, 1)]
    )


def grad_rows(a, b, x, stats, g, small):
    u = (a[...].astype(F32) + b[...].astype(F32)) * small[0:1]
    mean, inverse = stats[:, 0:1], stats[:, 1:2]
    scaled = (x[...].astype(F32) - mean) * inverse
    back_u = inverse * (
        u
        - jnp.mean(u, axis=-1, keepdims=True)
        - scaled * jnp.mean(u * scaled, axis=-1, keepdims=True)
    )
    return (g[...].astype(F32) + back_u).astype(BF16)


SPLIT = 4
PIECE = TILE // SPLIT


def line_kernel(
    first, gq, gk, gv, pre, x_block, stats_block, wq, wu, small, extra, x_all, g_all, stats_all, *refs
):
    parts, refs = refs[: first // SPLIT], refs[first // SPLIT :]
    output, grad, vectors = refs[:3]
    held, came, own, lines, across, x_own, g_own, stats_own, sums, by_dp, mine, by_tensor = refs[3:15]
    (
        load_sem, peer_send, peer_recv, in_send, in_recv, mid_send, mid_recv, out_send, out_recv,
        fin_send, fin_recv, keep_sem,
    ) = refs[15:]
    chunks = came.shape[0]
    i = pl.program_id(0)
    steps, pieces = 2 * chunks, SPLIT * chunks
    d = came.shape[2]
    row, me = lax.axis_index("dp"), lax.axis_index("tensor")
    count, size = by_dp.shape[0], by_tensor.shape[0]
    core = lax.rem(me, 2)
    chip = me // 2
    peer = me + 1 - 2 * core
    beside = 2 * (chip + 1 - 2 * lax.rem(chip, 2)) + core
    facing = 2 * (3 - chip) + core
    middle = (chip == 1) | (chip == 2)
    end = jnp.logical_not(middle)
    mesh = pl.DeviceIdType.MESH
    barrier = pltpu.get_barrier_semaphore()

    def remote(source, target, send_sem, recv_sem, device, axis="tensor"):
        return pltpu.make_async_remote_copy(
            src_ref=source, dst_ref=target, send_sem=send_sem, recv_sem=recv_sem,
            device_id={axis: device}, device_id_type=mesh,
        )

    shift = pieces - first
    every = pieces + first

    def place(p, before=0):
        start = place_of(p // SPLIT, core) * TILE + lax.rem(p, SPLIT) * PIECE - before
        return pl.ds(pl.multiple_of(start, PIECE), PIECE)

    def peer_copy(c):
        return remote(held.at[c], came.at[c], peer_send.at[c], peer_recv.at[c], peer)

    def in_copy(p):
        return remote(own.at[p], lines.at[p], in_send.at[p], in_recv.at[p], beside)

    def mid_copy(p):
        return remote(own.at[p], across.at[p], mid_send.at[p], mid_recv.at[p], facing)

    def out_copy(p):
        return remote(lines.at[p], lines.at[p], out_send.at[p], out_recv.at[p], beside)

    def fin_copy(p, target):
        return remote(lines.at[p], target, fin_send.at[p], fin_recv.at[p], peer)

    def keep_copy(p, target):
        return pltpu.make_async_copy(lines.at[p], target, keep_sem.at[p])

    def part_copy(p):
        return pltpu.make_async_copy(
            parts[p // SPLIT].at[pl.ds(p % SPLIT * PIECE, PIECE)], own.at[p], keep_sem.at[p]
        )

    def of(p, action):
        @pl.when(p < first)
        def _():
            action(p, output.at[place(p + shift, shift * 2 * PIECE)])

        @pl.when(p >= first)
        def _():
            action(p, grad.at[place(p - first)])

    def loads(p):
        return [
            pltpu.make_async_copy(array.at[place(p)], here.at[p], load_sem.at[n, p])
            for n, (array, here) in enumerate(((x_all, x_own), (g_all, g_own), (stats_all, stats_own)))
        ]

    def dp_copy(n):
        device = lax.rem(row + n, count)
        wide = d // count
        source = sums.at[:, pl.ds(pl.multiple_of(device * wide, 128), wide)]
        return remote(source, by_dp.at[n], load_sem.at[3, n], load_sem.at[4, n], device, "dp")

    def tensor_copy(n):
        device = lax.rem(me + n, size)
        return remote(mine, by_tensor.at[n], load_sem.at[5, n], load_sem.at[6, n], device)

    def hand_over(p, target):
        fin_copy(p, target).start()
        keep_copy(p, target).start()

    def take_in(p):
        in_copy(p).wait_recv()
        own[p] = (own[p].astype(F32) + lines[p].astype(F32)).astype(BF16)
        mid_copy(p).start()

    def finish(p):
        mid_copy(p).wait_recv()

        @pl.when(p < first)
        def _():
            q = p + shift
            lines[p] = output_rows(own[p], x_own[q], across[p], small[...])

        @pl.when(p >= first)
        def _():
            q = p - first
            lines[p] = grad_rows(own[p], across[p], x_own[q], stats_own[q], g_own[q], small[...])

        out_copy(p).start()
        of(p, hand_over)

    def each(action, begin=0, stop=every):
        lax.fori_loop(begin, stop, lambda p, _: (action(p), 0)[1], 0)

    @pl.when(i == 0)
    def _():
        for n in range(1, count):
            pl.semaphore_signal(
                barrier, inc=1, device_id={"dp": lax.rem(row + n, count)}, device_id_type=mesh
            )
        for n in range(1, size):
            pl.semaphore_signal(
                barrier, inc=1, device_id={"tensor": lax.rem(me + n, size)}, device_id_type=mesh
            )
        sums[...] = extra[...]
        for p in range(first):
            part_copy(p).start()
        pl.semaphore_wait(barrier, count + size - 2)
        for p in range(first):
            part_copy(p).wait()

    @pl.when((i == 0) & end)
    def _():
        each(lambda p: in_copy(p).start(), 0, first)

    @pl.when((i == 0) & middle)
    def _():
        each(lambda p: [load.start() for load in loads(p)], 0, pieces)
        each(lambda p: [load.wait() for load in loads(p)], 0, pieces)

    ours = lax.rem(i, 2)
    half = i // 2
    to = pl.ds(first + SPLIT * half, SPLIT)
    for cut in range(0, d, 2 * TILE):
        cut = slice(cut, cut + 2 * TILE)
        total = nt(pre[...], wu[cut])
        for c, g in enumerate((gq, gk, gv)):
            total = total + nt(g[...], wq[c, cut])
        scaled = (x_block[:, cut].astype(F32) - stats_block[:, 0:1]) * stats_block[:, 1:2]
        sums[0:1, cut] += jnp.sum(total * scaled, axis=0, keepdims=True)
        sums[1:2, cut] += jnp.sum(total, axis=0, keepdims=True)
        total = total.astype(BF16)

        @pl.when(ours == 0)
        def _():
            held[half, :, cut] = total

        @pl.when(ours == 1)
        def _():
            own[to, :, cut] = total.reshape(SPLIT, PIECE, 2 * TILE)

    @pl.when(ours == 0)
    def _():
        peer_copy(half).start()

    @pl.when(ours == 1)
    def _():
        peer_copy(half).wait_recv()
        total = own[to].astype(F32) + came[half].reshape(SPLIT, PIECE, d).astype(F32)
        own[to] = total.astype(BF16)

    @pl.when((ours == 1) & end)
    def _():
        for r in range(SPLIT):
            in_copy(first + SPLIT * half + r).start()

    early = 6
    begin = steps - early

    @pl.when((i >= begin) & middle)
    def _():
        take_in(i - begin)

    @pl.when((i > begin) & middle)
    def _():
        finish(i - begin - 1)

    @pl.when(i == steps - 1)
    def _():
        for n in range(1, count):
            dp_copy(n).start()

    def both(p, _):
        take_in(p)
        finish(p - 1)
        return 0

    def pass_on(p):
        out_copy(p).wait_recv()
        of(p, hand_over)

    some = early + 2

    @pl.when((i == steps - 1) & middle)
    def _():
        lax.fori_loop(early, some, both, 0)

    @pl.when((i == steps - 1) & end)
    def _():
        each(pass_on, 0, some)

    @pl.when(i == steps - 1)
    def _():
        wide = d // count
        total = sums[:, pl.ds(pl.multiple_of(row * wide, 128), wide)]
        for n in range(1, count):
            dp_copy(n).wait()
            total = total + by_dp[n]
        mine[...] = total
        for n in range(1, size):
            tensor_copy(n).start()

    @pl.when((i == steps - 1) & middle)
    def _():
        lax.fori_loop(some, every, both, 0)
        finish(every - 1)
        each(lambda p: (mid_copy(p).wait_send(), out_copy(p).wait_send()))

    @pl.when((i == steps - 1) & end)
    def _():
        each(pass_on, some)
        each(lambda p: in_copy(p).wait_send())

    @pl.when(i == steps - 1)
    def _():
        total = mine[...]
        for n in range(1, size):
            tensor_copy(n).wait()
            total = total + by_tensor[n]
        vectors[...] = jnp.concatenate([total[:2], mine[2:]])
        for c in range(chunks):
            peer_copy(c).wait_send()
        each(lambda p: of(p, lambda *a: (fin_copy(*a).wait(), keep_copy(*a).wait())))


def line_back(chain, parts, chunks, size, count, gq, gk, gv, pre, x, stats, wq, wu, small, extra, g):
    length, d = x.shape
    width, units = wq.shape[2], wu.shape[1]
    pieces, first = SPLIT * chunks, SPLIT * len(parts)

    def block(n):
        def index(i):
            core = lax.rem(lax.axis_index("tensor"), 2)
            mine = lax.rem(i, 2)
            return (place_of(i // 2, lax.rem(core + 1 + mine, 2)), 0)

        return pl.BlockSpec((TILE, n), index)

    def once(shape):
        zeros = (0,) * len(shape)
        return pl.BlockSpec(shape, lambda *i: zeros, pipeline_mode=pl.Buffered(1))

    far = pl.BlockSpec(memory_space=pltpu.HBM)
    rows_of = lambda n: pltpu.VMEM((n, PIECE, d), BF16)
    sems = pltpu.SemaphoreType.DMA
    vector = (8, d // count)
    return chain(
        partial(line_kernel, first),
        "line_back",
        2 * chunks,
        [(a, block(width)) for a in (gq, gk, gv)]
        + [
            (pre, block(units)), (x, block(d)), (stats, block(PAIR)), (wq, once(wq.shape)),
            (wu, once(wu.shape)), (small, once(small.shape)), (extra, once(extra.shape)),
            (x, far), (g, far), (stats, far),
        ]
        + [(p, far) for p in parts],
        [
            ((first * 2 * PIECE, d), BF16, far), ((length, d), BF16, far),
            (vector, F32, whole(vector)),
        ],
        scratch=[
            pltpu.VMEM((chunks, TILE, d), BF16), pltpu.VMEM((chunks, TILE, d), BF16),
            rows_of(first + pieces), rows_of(first + pieces), rows_of(first + pieces),
            rows_of(pieces), rows_of(pieces),
            pltpu.VMEM((pieces, PIECE, PAIR), F32),
            pltpu.VMEM((8, d), F32), pltpu.VMEM((count, *vector), F32), pltpu.VMEM(vector, F32),
            pltpu.VMEM((size, *vector), F32),
            sems((7, max(pieces, size, count))), sems((chunks,)), sems((chunks,)),
        ]
        + [sems((first + pieces,))] * 9,
        collective=5,
        flops=200e9,
        mib=62,
    )


def flow(chain, size, core, chunk, total, closing, results, key, length):
    chips = size // 2
    chip = lax.axis_index("tensor") // 2
    distance = jnp.where(chip < chips // 2, chips // 2 - 1 - chip, chip - chips // 2)
    for s in range(chips // 2 - 1):
        came = along(total, [(s, s + 1), (chips - 1 - s, chips - 2 - s)])
        yield
        total = plus(chain, total, came)
    a, b = chips // 2 - 1, chips // 2
    came = along(total, [(a, b), (b, a)])
    yield
    value = closing(chunk, total, came)
    for s in range(chips // 2 - 1):
        a, b = chips // 2 - 1 - s, chips // 2 + s
        came = along(value, [(a, a - 1), (b, b + 1)])
        yield
        value = choose(chain, (distance == s + 1).astype(jnp.int32)[None], value, came)
    peer = swap_cores(value, size)
    yield
    results[key] = assemble(chain, core, chunk, length, value, peer, results.get(key))


def on_device(
    size,
    inputs,
    segment_ids,
    norm_gain,
    norm_bias,
    qkv_weight,
    qkv_bias,
    out_weight,
    out_bias,
    up_weight,
    up_bias,
    down_weight,
    down_bias,
    cotangent,
):
    x, g, segment_row = inputs[0], cotangent[0], segment_ids[0]
    length, d = x.shape
    width, units = qkv_weight.shape[2], up_weight.shape[1]
    count = lax.axis_size("dp")
    core = (lax.axis_index("tensor") % 2).astype(jnp.int32)[None]

    start = jnp.sum((segment_row[None, :] < segment_row[:, None]).astype(jnp.int32), axis=1)
    small = jnp.stack([norm_gain, norm_bias, out_bias, down_bias] + [norm_gain] * 4).astype(F32)
    wq = qkv_weight.transpose(1, 0, 2)

    chain = Chain()
    normed, stats, q, k, v, hidden, slope, cos_wide, sin_wide = first(
        chain, x, small, wq, qkv_bias, up_weight, up_bias, start
    )
    mixed, log = attend(chain, start, q, k, v)
    rest = 2 if size == 8 else 0
    lower = length - rest * (length // CHUNKS)
    weights = (mixed, hidden, out_weight, down_weight)
    summed = lax.psum(branch(chain, lower, *weights), "tensor")
    parts = branch_rest(chain, rest, CHUNKS - rest, *weights) if rest else []

    pre, gm, delta, g_sums, up_sums = back(chain, g, slope, mixed, out_weight, down_weight)
    scatter = lambda a: lax.psum_scatter(a, "dp", scatter_dimension=1, tiled=True)
    near = scatter(weight_grad(chain, "weight_grad_g", [hidden, mixed], g))
    tiles = length // TILE
    *packed, qkv_sums, _ = attend_back(
        chain, 0, tiles, start, log, delta, q, k, v, gm, cos_wide, sin_wide, [log]
    )
    far = scatter(weight_grad(chain, "weight_grad_n", [pre, *packed], normed))

    by_share = lambda a: a.reshape(-1, count, HD // count).swapaxes(0, 1).reshape(count, -1)
    part = d // count
    narrow = jnp.concatenate([by_share(up_sums[0]), by_share(qkv_sums[:3])], axis=1)
    narrow = jnp.pad(narrow, ((0, 0), (0, part - narrow.shape[1]))).reshape(1, d)
    if size == 8:
        extra = jnp.concatenate([jnp.zeros((2, d), F32), g_sums[:1], narrow, jnp.zeros((4, d), F32)])
        upper, grad, vectors = line_back(
            chain, parts, CHUNKS, size, count, *packed, pre, x, stats, wq, up_weight, small, extra, g
        )
    else:

        results = {}

        def line(parts, closing, own, key):
            finish = lambda chunk, a, b: close_chunk(chain, closing, core, chunk, a, b, own, small)
            flows = [
                flow(chain, size, core, c, parts[c], finish, results, key, length)
                for c in range(CHUNKS)
            ]
            while flows:
                flows = [f for f in flows if next(f, flows) is None]

        norm_sums, *parts = normed_back(chain, CHUNKS, *packed, pre, x, stats, wq, up_weight)
        line(parts, grad_rows, [x, stats, g], "grad")
        vectors = jnp.concatenate([norm_sums[:2], g_sums[:1], narrow]).reshape(4, count, part)
        vectors = vectors.swapaxes(0, 1).reshape(count, -1, 128)
        vectors = add_vectors(chain, vectors, size, count).reshape(4, part)
    if size == 8:
        output, input_grad, down_share, out_share, up_share, qkv_share = last(
            chain, summed, x, small, upper, grad, near, far, width, units
        )
    else:
        output, input_grad = close_both(chain, summed, x, small, results["grad"])
        shapes = [(units, part), (width, part)]
        down_share, out_share = widen(chain, near, shapes, (False, False))
        shapes = [(part, units), (3, part, width)]
        up_share, qkv_share = widen(chain, far, shapes, (True, True))
    up_b_share = vectors[3, : units // count].reshape(-1, HD // count)
    qkv_b_share = vectors[3, units // count : (units + 3 * width) // count].reshape(3, -1, HD // count)

    return (
        output[None],
        input_grad[None],
        vectors[0],
        vectors[1],
        qkv_share.transpose(1, 0, 2),
        qkv_b_share,
        out_share,
        vectors[2],
        up_share,
        up_b_share,
        down_share,
        vectors[2],
    )


def solution(mesh):
    placed = (
        P("dp", None, None),
        P("dp", None),
        P(),
        P(),
        P(None, None, "tensor"),
        P(None, "tensor"),
        P("tensor", None),
        P(),
        P(None, "tensor"),
        P("tensor"),
        P("tensor", None),
        P(),
        P("dp", None, None),
    )
    return jax.shard_map(
        partial(on_device, mesh.shape["tensor"]),
        mesh=mesh,
        in_specs=placed,
        out_specs=(
            P("dp", None, None),
            P("dp", None, None),
            P("dp"),
            P("dp"),
            P("dp", None, "tensor"),
            P(None, "tensor", "dp"),
            P("tensor", "dp"),
            P("dp"),
            P("dp", "tensor"),
            P("tensor", "dp"),
            P("tensor", "dp"),
            P("dp"),
        ),
        check_vma=False,
    )
```

```python
from functools import partial

import jax
import jax.numpy as jnp
from jax import lax
from jax.experimental import pallas as pl
from jax.experimental.pallas import tpu as pltpu
from jax.sharding import PartitionSpec as P

HD = 64
ROT = 32
PAIR = 2 * HD
TILE = 256
CHUNKS = 4
NEG = -1e30
MIB = 1 << 20
F32 = jnp.float32
BF16 = jnp.bfloat16


class Chain:
    def __init__(self):
        self.link = jnp.zeros((8, 128), F32)

    def __call__(
        self, kernel, name, grid, ins, outs, scalars=(), scratch=(), alias=(), mib=58, flops=1, collective=None
    ):
        taken, given = len(scalars) + len(ins), len(outs)

        def body(*refs):
            kernel(*refs[:taken], *refs[taken + 1 : taken + 1 + given], *refs[taken + 2 + given :])

        anywhere = pl.BlockSpec(memory_space=pltpu.HBM)
        results = pl.pallas_call(
            body,
            grid_spec=pltpu.PrefetchScalarGridSpec(
                num_scalar_prefetch=len(scalars),
                grid=(grid,),
                in_specs=[spec for _, spec in ins] + [anywhere],
                out_specs=[spec for _, _, spec in outs] + [anywhere],
                scratch_shapes=list(scratch),
            ),
            out_shape=[jax.ShapeDtypeStruct(shape, dtype) for shape, dtype, _ in outs]
            + [jax.ShapeDtypeStruct(self.link.shape, F32)],
            input_output_aliases={taken: given, **{len(scalars) + i: o for i, o in alias}},
            compiler_params=pltpu.CompilerParams(
                dimension_semantics=("arbitrary",), vmem_limit_bytes=mib * MIB,
                collective_id=collective, has_side_effects=collective is not None,
            ),
            cost_estimate=pl.CostEstimate(flops=int(flops), bytes_accessed=1, transcendentals=0),
            name=name,
        )(*scalars, *[array for array, _ in ins], self.link)
        self.link = results[-1]
        return results[:-1]


def whole(shape):
    zeros = (0,) * len(shape)
    return pl.BlockSpec(shape, lambda *i: zeros)


def rows(n, height=TILE):
    return pl.BlockSpec((height, n), lambda i, *s: (i, 0))


def nn(a, b):
    return lax.dot_general(a, b, (((1,), (0,)), ((), ())), preferred_element_type=F32)


def nt(a, b):
    return lax.dot_general(a, b, (((1,), (1,)), ((), ())), preferred_element_type=F32)


def tn(a, b):
    return lax.dot_general(a, b, (((0,), (0,)), ((), ())), preferred_element_type=F32)


def rotated(x, cos_wide, sin_wide):
    lane = lax.broadcasted_iota(jnp.int32, x.shape, 1) % HD
    half = ROT // 2
    other = jnp.where(
        lane < half, pltpu.roll(x, PAIR - half, 1), pltpu.roll(x, half, 1)
    )
    return x * cos_wide + other * sin_wide


def row_stats(x):
    mean = jnp.mean(x, axis=-1, keepdims=True)
    centered = x - mean
    inverse = lax.rsqrt(jnp.mean(centered * centered, axis=-1, keepdims=True) + 1e-05)
    return centered * inverse, mean, inverse


def gelu_both(u):
    c = 0.7978845608028654
    u2 = u * u
    gate = 0.5 + 0.5 * jnp.tanh(u * (c + (c * 0.044715) * u2))
    value = u * gate
    slope = gate + value * (1.0 - gate) * (2.0 * c + (6.0 * c * 0.044715) * u2)
    return value, slope


def first_kernel(
    x0_ref, x1_ref, x2_ref, small_ref, wq_ref, bq_ref, wu_ref, bu_ref, start_ref, freq_ref,
    normed_ref, stats_ref, q_ref, k_ref, v_ref, hidden_ref, slope_ref, cos_ref, sin_ref,
    even, odd, even_stats,
):
    s = pl.program_id(0)
    gain, shift = small_ref[0:1], small_ref[1:2]
    lane = lax.broadcasted_iota(jnp.int32, (TILE, PAIR), 1)

    def norm(x):
        scaled, mean, inverse = row_stats(x.astype(F32))
        return (scaled * gain + shift).astype(BF16), jnp.where(lane == 0, mean, inverse)

    @pl.when(s == 0)
    def _():
        even[...], even_stats[...] = norm(x0_ref[...])

    half = ROT // 2
    unit = lax.broadcasted_iota(jnp.int32, (half, PAIR), 1) % HD
    index = lax.broadcasted_iota(jnp.int32, (half, PAIR), 0)
    first_half = (unit == index).astype(F32)
    second_half = (unit == index + half).astype(F32)
    bias = bq_ref[...].astype(F32)

    def spread(a, b):
        return lax.dot_general(
            a, b, (((0,), (0,)), ((), ())), precision=lax.Precision.HIGHEST,
            preferred_element_type=F32,
        )

    def project(t, normed):
        here = slice(t * TILE, (t + 1) * TILE)
        place = lax.broadcasted_iota(jnp.int32, (1, TILE), 1) + (2 * s + t) * TILE
        angle = freq_ref[...] * (place - start_ref[:, here]).astype(F32)
        cos_wide = spread(jnp.cos(angle), first_half + second_half)
        cos_wide = jnp.where(lane % HD < ROT, cos_wide, 1.0)
        sin_wide = spread(jnp.sin(angle), second_half - first_half)
        cos_ref[here], sin_ref[here] = cos_wide, sin_wide
        for c, out in enumerate((q_ref, k_ref, v_ref)):
            packed = nn(normed, wq_ref[c]) + bias[c : c + 1]
            if c == 2:
                out[here] = packed.astype(BF16)
            else:
                for p in range(packed.shape[1] // PAIR):
                    cut = slice(p * PAIR, (p + 1) * PAIR)
                    turned = rotated(packed[:, cut], cos_wide, sin_wide).astype(BF16)
                    out[here, cut] = turned * (HD**-0.5) if c == 0 else turned
        units = wu_ref.shape[1]
        for n in range(0, units, TILE):
            cut = slice(n, n + TILE)
            value, slope = gelu_both(nn(normed, wu_ref[:, cut]) + bu_ref[:, cut])
            hidden_ref[here, cut] = value.astype(BF16)
            slope_ref[here, cut] = slope.astype(BF16)

    normed = even[...]
    normed_ref[:TILE] = normed
    stats_ref[:TILE] = even_stats[...]
    after, after_stats = norm(x1_ref[...])
    odd[...] = after
    normed_ref[TILE:] = after
    stats_ref[TILE:] = after_stats
    project(0, normed)
    even[...], even_stats[...] = norm(x2_ref[...])
    project(1, odd[...])


def first(chain, x, small, wq, bq, wu, bu, start):
    length, d = x.shape
    width, units = wq.shape[2], wu.shape[1]
    tiles = length // TILE
    freq = 10000.0 ** (-jnp.arange(ROT // 2, dtype=F32) * 2.0 / ROT)
    at = lambda f: pl.BlockSpec((TILE, d), lambda s: (f(s), 0))
    big = lambda n: rows(n, 2 * TILE)
    return chain(
        first_kernel,
        "first",
        tiles // 2,
        [
            (x, at(lambda s: 0)),
            (x, at(lambda s: 2 * s + 1)),
            (x, at(lambda s: jnp.minimum(2 * s + 2, tiles - 1))),
            (small, whole(small.shape)), (wq, whole(wq.shape)), (bq, whole(bq.shape)),
            (wu, whole(wu.shape)), (bu[None].astype(F32), whole((1, units))),
            (start[None], pl.BlockSpec((1, 2 * TILE), lambda s: (0, s))),
            (jnp.broadcast_to(freq[:, None], (ROT // 2, TILE)), whole((ROT // 2, TILE))),
        ],
        [((length, d), BF16, big(d)), ((length, PAIR), F32, big(PAIR))]
        + [((length, n), BF16, big(n)) for n in (width, width, width, units, units)]
        + [((length, PAIR), F32, big(PAIR))] * 2,
        scratch=[pltpu.VMEM((TILE, d), BF16)] * 2 + [pltpu.VMEM((TILE, PAIR), F32)],
        mib=40,
        flops=35e9,
    )


def halves(x):
    left = lax.broadcasted_iota(jnp.int32, x.shape, 1) < HD
    zero = jnp.zeros(x.shape, x.dtype)
    return [jnp.where(left, x, zero), jnp.where(left, zero, x)]


def pair_cuts(width):
    return [slice(p, p + PAIR) for p in range(0, width, PAIR)]


def attend_kernel(start_sref, start_ref, q_ref, k_ref, v_ref, mixed_ref, log_ref):
    i = pl.program_id(0)
    cuts = pair_cuts(q_ref.shape[1])
    heads = range(2 * len(cuts))
    key_row = lax.broadcasted_iota(jnp.int32, (TILE, TILE), 0)
    query = lax.broadcasted_iota(jnp.int32, (TILE, TILE), 1) + i * TILE
    start = start_ref[...]
    queries = [q for cut in cuts for q in halves(q_ref[:, cut])]

    def step(j, carry):
        tops, totals, sums = carry
        there = pl.ds(pl.multiple_of(j * TILE, TILE), TILE)
        place = key_row + j * TILE
        allowed = (place >= start) & (place <= query)
        k = [k_ref[there, cut] for cut in cuts]
        v = [v_ref[there, cut] for cut in cuts]
        s = [nt(k[h // 2], queries[h]) for h in heads]
        s = [jnp.where(allowed, a, NEG) for a in s]
        top = [jnp.maximum(tops[h], jnp.max(s[h], axis=0, keepdims=True)) for h in heads]
        alpha = [jnp.exp(tops[h] - top[h]) for h in heads]
        w = [jnp.exp(s[h] - top[h]) for h in heads]
        totals = [totals[h] * alpha[h] + jnp.sum(w[h], axis=0, keepdims=True) for h in heads]
        w = [a.astype(BF16) for a in w]
        add = [tn(v[h // 2], w[h])[h % 2 * HD : (h % 2 + 1) * HD] for h in heads]
        sums = [sums[h] * alpha[h] + add[h] for h in heads]
        return tuple(top), tuple(totals), tuple(sums)

    empty = (
        tuple(jnp.full((1, TILE), NEG, F32) for _ in heads),
        tuple(jnp.zeros((1, TILE), F32) for _ in heads),
        tuple(jnp.zeros((HD, TILE), F32) for _ in heads),
    )
    low = start_sref[i * TILE] // TILE
    tops, totals, sums = lax.fori_loop(low, i + 1, step, empty)
    log_ref[...] = jnp.zeros_like(log_ref)
    for h in heads:
        log_ref[h : h + 1] = tops[h] + jnp.log(totals[h])
    mixed_ref[...] = jnp.concatenate([sums[h] * (1.0 / totals[h]) for h in heads]).T.astype(BF16)


def attend(chain, start, q, k, v):
    length, width = q.shape
    full = whole((length, width))
    return chain(
        attend_kernel,
        "attend",
        length // TILE,
        [
            (start[None], pl.BlockSpec((1, TILE), lambda i, *s: (0, i))),
            (q, rows(width)), (k, full), (v, full),
        ],
        [
            ((length, width), BF16, rows(width)),
            ((8, length), F32, pl.BlockSpec((8, TILE), lambda i, *s: (0, i))),
        ],
        scalars=(start,),
        mib=24,
        flops=19e9,
    )


def attend_back_kernel(
    begin, start_sref, start_ref, log_ref, delta_ref, q_ref, k_ref, v_ref, g_ref, cos_ref, sin_ref,
    totals_in, *refs,
):
    gq_ref, gk_ref, gv_ref, bias_ref, totals = refs[-5:]
    j = pl.program_id(0) + begin
    length, width = q_ref.shape
    cuts = pair_cuts(width)
    heads = range(2 * len(cuts))
    here = pl.ds(pl.multiple_of(j * TILE, TILE), TILE)

    @pl.when(pl.program_id(0) == 0)
    def _():
        totals[...] = totals_in[...] if begin else jnp.zeros_like(totals)
        bias_ref[...] = jnp.zeros_like(bias_ref)

    place = j * TILE + lax.broadcasted_iota(jnp.int32, (TILE, TILE), 0)
    query = lax.broadcasted_iota(jnp.int32, (TILE, TILE), 1)
    keys = [k_ref[here, cut] for cut in cuts]
    split = [half for k in keys for half in halves(k)]
    values = [v_ref[here, cut] for cut in cuts]

    def step(i, carry):
        gk, gv = carry
        there = pl.ds(pl.multiple_of(i * TILE, TILE), TILE)
        allowed = (place >= start_ref[:, there]) & (place <= query + i * TILE)
        qs = [half for cut in cuts for half in halves(q_ref[there, cut])]
        gs = [half for cut in cuts for half in halves(g_ref[there, cut])]
        s = [nt(keys[h // 2], qs[h]) for h in heads]
        gp = [nt(values[h // 2], gs[h]) for h in heads]
        w = [jnp.exp(jnp.where(allowed, s[h] - log_ref[h : h + 1, there], NEG)) for h in heads]
        ds = [(w[h] * (gp[h] - delta_ref[h : h + 1, there])).astype(BF16) for h in heads]
        w = [a.astype(BF16) for a in w]
        both = lambda f: tuple(f(h) + f(h + 1) for h in heads[::2])
        gv = [a + b for a, b in zip(gv, both(lambda h: nn(w[h], gs[h])))]
        gk = [a + b for a, b in zip(gk, both(lambda h: nn(ds[h], qs[h])))]
        for cut, gq in zip(cuts, both(lambda h: tn(ds[h], split[h]))):
            totals[there, cut] += gq
        return tuple(gk), tuple(gv)

    high = sum((start_sref[b * TILE] < (j + 1) * TILE).astype(jnp.int32) for b in range(length // TILE))
    empty = tuple(jnp.zeros((TILE, PAIR), F32) for _ in cuts)
    gks, gvs = lax.fori_loop(j, high, step, (empty, empty))
    cos_wide, sin_wide = cos_ref[...], -sin_ref[...]
    for cut, gk, gv in zip(cuts, gks, gvs):
        gq = rotated(totals[here, cut] * (HD**-0.5), cos_wide, sin_wide).astype(BF16)
        gk = rotated(gk, cos_wide, sin_wide).astype(BF16)
        for c, (g, out) in enumerate(((gq, gq_ref), (gk, gk_ref), (gv.astype(BF16), gv_ref))):
            out[:, cut] = g
            bias_ref[c : c + 1, cut] += jnp.sum(g.astype(F32), axis=0, keepdims=True)


def attend_back(chain, begin, end, start, log, delta, q, k, v, g, cos_wide, sin_wide, before):
    length, width = q.shape
    full = whole((length, width))
    shifted = lambda n: pl.BlockSpec((TILE, n), lambda i, *s: (i + begin, 0))
    anywhere = pl.BlockSpec(memory_space=pl.ANY)
    so_far = before[:3] if begin else []
    return chain(
        partial(attend_back_kernel, begin),
        f"attend_back_{begin}",
        end - begin,
        [
            (start[None], whole((1, length))), (log, whole((8, length))), (delta, whole((8, length))),
            (q, full), (k, full), (v, full), (g, full), (cos_wide, shifted(PAIR)), (sin_wide, shifted(PAIR)),
            (before[-1], full if begin else anywhere),
        ]
        + [(a, anywhere) for a in so_far],
        [((length, width), BF16, shifted(width))] * 3
        + [((8, width), F32, whole((8, width))), ((length, width), F32, full)],
        scalars=(start,),
        alias=tuple((10 + n, n) for n in range(len(so_far))),
        flops=31e9,
    )


def place_of(chunk, core):
    return 4 * (chunk // 2) + 2 * core + chunk % 2


def own_rows(chunks, half, skip=0):
    def spec(n):
        def index(i):
            core = lax.rem(lax.axis_index("tensor"), 2)
            steps = chunks // 2
            return (skip + 2 * lax.rem(i, steps) + jnp.where(i < steps, 1 - core, core), 0)

        return pl.BlockSpec((2 * half, n), index)

    return spec


def paired(product, chunks, ins, *refs):
    given, extra, sums, held, came, send_sem, recv_sem = (
        refs[:ins], refs[ins : len(refs) - chunks - 4], refs[-chunks - 4 : -4], *refs[-4:]
    )
    i = pl.program_id(0)
    steps = chunks // 2
    half, d = sums[0].shape
    me = lax.axis_index("tensor")
    peer = me + 1 - 2 * lax.rem(me, 2)
    barrier = pltpu.get_barrier_semaphore()

    def copy(n):
        return pltpu.make_async_remote_copy(
            src_ref=held.at[n], dst_ref=came.at[n], send_sem=send_sem.at[n], recv_sem=recv_sem.at[n],
            device_id={"tensor": peer}, device_id_type=pl.DeviceIdType.MESH,
        )

    @pl.when(i == 0)
    def _():
        pl.semaphore_signal(
            barrier, inc=1, device_id={"tensor": peer}, device_id_type=pl.DeviceIdType.MESH
        )
        for e in extra:
            e[...] = jnp.zeros_like(e)

    for cut in range(0, d, 2 * TILE):
        cut = slice(cut, cut + 2 * TILE)
        total = product(cut, given, extra).astype(BF16)
        held[pl.ds(2 * i, 2), :, cut] = total.reshape(2, half, 2 * TILE)

    @pl.when(i == 0)
    def _():
        pl.semaphore_wait(barrier, 1)

    for n in range(steps):

        @pl.when(i == n)
        def _(n=n):
            copy(2 * n).start()
            copy(2 * n + 1).start()

        @pl.when(i == steps + n)
        def _(n=n):
            for c in (2 * n, 2 * n + 1):
                copy(c).wait()
                total = held[chunks + c].astype(F32) + came[c].astype(F32)
                sums[c][...] = total.astype(BF16)


def pair_call(chain, product, name, collective, chunks, half, d, ins, extra):
    return chain(
        partial(paired, product, chunks, len(ins)),
        name,
        chunks,
        ins,
        extra + [((half, d), BF16, whole((half, d)))] * chunks,
        scratch=[pltpu.VMEM((2 * chunks, half, d), BF16), pltpu.VMEM((chunks, half, d), BF16)]
        + [pltpu.SemaphoreType.DMA((chunks,))] * 2,
        flops=13e9,
        collective=collective,
    )


def branch_kernel(mixed, hidden, wo, wd, out):
    for cut in range(0, out.shape[1], 2 * TILE):
        cut = slice(cut, cut + 2 * TILE)
        out[:, cut] = (nn(mixed[...], wo[:, cut]) + nn(hidden[...], wd[:, cut])).astype(BF16)


def branch(chain, length, mixed, hidden, wo, wd):
    d = wo.shape[1]
    big = lambda n: rows(n, 2 * TILE)
    return chain(
        branch_kernel,
        "branch",
        length // (2 * TILE),
        [
            (mixed, big(mixed.shape[1])), (hidden, big(hidden.shape[1])),
            (wo, whole(wo.shape)), (wd, whole(wd.shape)),
        ],
        [((length, d), BF16, big(d))],
        mib=30,
        flops=7e9,
    )[0]


def branch_product(cut, given, extra):
    mixed, hidden, wo, wd = given
    return nn(mixed[...], wo[:, cut]) + nn(hidden[...], wd[:, cut])


def branch_rest(chain, chunks, skip, mixed, hidden, wo, wd):
    length, d = mixed.shape[0], wo.shape[1]
    half = length // (2 * (chunks + skip))
    spec = own_rows(chunks, half, skip)
    ins = [
        (mixed, spec(mixed.shape[1])), (hidden, spec(hidden.shape[1])),
        (wo, whole(wo.shape)), (wd, whole(wd.shape)),
    ]
    return pair_call(chain, branch_product, "branch_rest", 1, chunks, half, d, ins, [])


def last_kernel(
    steps, summed, x, small, rest, grad, down_in, out_in, up_in, q_in, k_in, v_in,
    output, input_grad, down, out, up, qkv,
):
    i = pl.program_id(0)
    input_grad[...] = grad[...]
    down[...] = down_in[...].astype(F32)
    out[...] = out_in[...].astype(F32)
    up[...] = up_in[...].astype(F32).T
    for c, part in enumerate((q_in, k_in, v_in)):
        qkv[c] = part[...].astype(F32).T

    @pl.when(i < steps)
    def _():
        output[...] = output_rows(summed, x[...], None, small)

    @pl.when(i >= steps)
    def _():
        output[...] = rest[...]


def last(chain, summed, x, small, rest, grad, near, far, width, units):
    length, d = x.shape
    part = near.shape[1]
    lower = summed.shape[0]
    grid = 4
    high = length // grid
    steps = lower // high
    tall, slim, thin = units // grid, width // grid, part // grid
    block = rows(d, high)
    low = pl.BlockSpec((high, d), lambda i: (jnp.minimum(i, steps - 1), 0))
    upper = pl.BlockSpec((high, d), lambda i: (jnp.maximum(i - steps, 0), 0))
    third = lambda c: pl.BlockSpec((width, thin), lambda i: (units // width + c, i))
    return chain(
        partial(last_kernel, steps), "last", grid,
        [
            (summed, low), (x, low), (small, whole(small.shape)), (rest, upper), (grad, block),
            (near, rows(part, tall)),
            (near, pl.BlockSpec((slim, part), lambda i: (units // slim + i, 0))),
            (far, rows(part, tall)), (far, third(0)), (far, third(1)), (far, third(2)),
        ],
        [
            ((length, d), BF16, block), ((length, d), BF16, block),
            ((units, part), F32, rows(part, tall)), ((width, part), F32, rows(part, slim)),
            ((part, units), F32, pl.BlockSpec((part, tall), lambda i: (0, i))),
            ((3, part, width), F32, pl.BlockSpec((3, thin, width), lambda i: (0, i, 0))),
        ],
    )


def output_rows(a, x, b, small):
    total = a[...].astype(F32)
    if b is not None:
        total = total + b[...].astype(F32)
    return (x.astype(F32) + total + small[2:3] + small[3:4]).astype(BF16)


def close_kernel(summed, x, small, grad, output, input_grad):
    output[...] = output_rows(summed, x[...], None, small)
    input_grad[...] = grad[...]


def close_both(chain, summed, x, small, grad):
    length, d = x.shape
    block = rows(d, 2 * TILE)
    return chain(
        close_kernel, "close_both", length // (2 * TILE),
        [(summed, block), (x, block), (small, whole(small.shape)), (grad, block)],
        [((length, d), BF16, block)] * 2,
    )


def back_kernel(g_ref, slope_ref, mixed_ref, wo_ref, wd_ref, pre_ref, gm_ref, delta_ref, sums_ref, up_ref):
    @pl.when(pl.program_id(0) == 0)
    def _():
        sums_ref[...] = jnp.zeros_like(sums_ref)
        up_ref[...] = jnp.zeros_like(up_ref)

    g = g_ref[...]
    for n in range(0, wd_ref.shape[0], 2 * TILE):
        cut = slice(n, n + 2 * TILE)
        pre = (nt(g, wd_ref[cut]) * slope_ref[:, cut].astype(F32)).astype(BF16)
        pre_ref[:, cut] = pre
        up_ref[0:1, cut] += jnp.sum(pre.astype(F32), axis=0, keepdims=True)
    gm = nt(g, wo_ref[...]).astype(BF16)
    gm_ref[...] = gm
    product = gm.astype(F32) * mixed_ref[...].astype(F32)
    coarse = product.astype(BF16)
    fine = (product - coarse.astype(F32)).astype(BF16)
    width = gm.shape[1]
    pick = (
        lax.broadcasted_iota(jnp.int32, (8, width), 1) // HD
        == lax.broadcasted_iota(jnp.int32, (8, width), 0)
    ).astype(BF16)
    delta_ref[...] = nt(pick, coarse) + nt(pick, fine)
    sums_ref[0:1] += jnp.sum(g.astype(F32), axis=0, keepdims=True)


def back(chain, g, slope, mixed, wo, wd):
    length, d = g.shape
    width, units = wo.shape[0], wd.shape[0]
    big = lambda n: rows(n, 2 * TILE)
    return chain(
        back_kernel,
        "back",
        length // (2 * TILE),
        [
            (g, big(d)), (slope, big(units)), (mixed, big(width)),
            (wo, whole(wo.shape)), (wd, whole(wd.shape)),
        ],
        [
            ((length, units), BF16, big(units)), ((length, width), BF16, big(width)),
            ((8, length), F32, pl.BlockSpec((8, 2 * TILE), lambda i, *s: (0, i))),
            ((8, d), F32, whole((8, d))), ((8, units), F32, whole((8, units))),
        ],
        flops=15e9,
    )


def normed_back_product(cut, given, extra):
    gq, gk, gv, pre, x, stats, wq, wu = given
    (sums,) = extra
    total = nt(pre[...], wu[cut])
    for c, g in enumerate((gq, gk, gv)):
        total = total + nt(g[...], wq[c, cut])
    scaled = (x[:, cut].astype(F32) - stats[:, 0:1]) * stats[:, 1:2]
    sums[0:1, cut] += jnp.sum(total * scaled, axis=0, keepdims=True)
    sums[1:2, cut] += jnp.sum(total, axis=0, keepdims=True)
    return total


def normed_back(chain, chunks, gq, gk, gv, pre, x, stats, wq, wu):
    length, d = x.shape
    width, units = wq.shape[2], wu.shape[1]
    half = length // (2 * chunks)
    spec = own_rows(chunks, half)
    ins = [(a, spec(width)) for a in (gq, gk, gv)] + [
        (pre, spec(units)), (x, spec(d)), (stats, spec(PAIR)),
        (wq, whole(wq.shape)), (wu, whole(wu.shape)),
    ]
    return pair_call(
        chain, normed_back_product, "normed_back", 2, chunks, half, d, ins,
        [((8, d), F32, whole((8, d)))],
    )


def weight_grad_kernel(counts, *refs):
    *lefts, right, out = refs
    i = pl.program_id(0)
    done = 0
    for left, count in zip(lefts, counts):

        @pl.when((i >= done) & (i < done + count))
        def _(left=left):
            out[...] = tn(left[...], right[...]).astype(BF16)

        done += count


def weight_grad(chain, name, lefts, right):
    length, d = right.shape
    wide = min(TILE, *[a.shape[1] for a in lefts])
    counts = tuple(a.shape[1] // wide for a in lefts)
    ins, done = [], 0
    for a, count in zip(lefts, counts):
        place = lambda i, done=done, count=count: jnp.clip(i - done, 0, count - 1)
        ins.append((a, pl.BlockSpec((length, wide), lambda i, f=place: (0, f(i)))))
        done += count
    return chain(
        partial(weight_grad_kernel, counts),
        name,
        done,
        ins + [(right, whole(right.shape))],
        [((done * wide, d), BF16, rows(d, wide))],
        flops=2 * length * d * done * wide,
    )[0]


def vectors_kernel(size, count, vectors, total, came, part, wide, sems):
    row, me = lax.axis_index("dp"), lax.axis_index("tensor")
    barrier = pltpu.get_barrier_semaphore()
    mesh = pl.DeviceIdType.MESH
    half = part.shape[0] // 2

    def by_row(n):
        peer = lax.rem(row + n, count)
        return pltpu.make_async_remote_copy(
            src_ref=vectors.at[peer], dst_ref=came.at[n], send_sem=sems.at[0, n],
            recv_sem=sems.at[1, n], device_id={"dp": peer}, device_id_type=mesh,
        )

    def by_column(n):
        peer = lax.rem(me + n, size)
        return pltpu.make_async_remote_copy(
            src_ref=part.at[pl.ds(0, half)], dst_ref=wide.at[n], send_sem=sems.at[2, n],
            recv_sem=sems.at[3, n], device_id={"tensor": peer}, device_id_type=mesh,
        )

    for n in range(1, count):
        pl.semaphore_signal(
            barrier, inc=1, device_id={"dp": lax.rem(row + n, count)}, device_id_type=mesh
        )
    for n in range(1, size):
        pl.semaphore_signal(
            barrier, inc=1, device_id={"tensor": lax.rem(me + n, size)}, device_id_type=mesh
        )
    pl.semaphore_wait(barrier, count + size - 2)
    for n in range(1, count):
        by_row(n).start()
    mine = vectors[row]
    for n in range(1, count):
        by_row(n).wait()
        mine = mine + came[n]
    part[...] = mine
    for n in range(1, size):
        by_column(n).start()
    upper = mine[:half]
    for n in range(1, size):
        by_column(n).wait()
        upper = upper + wide[n]
    total[:half] = upper
    total[half:] = mine[half:]


def add_vectors(chain, vectors, size, count):
    small = vectors.shape[1:]
    return chain(
        partial(vectors_kernel, size, count), "add_vectors", 1, [(vectors, whole(vectors.shape))],
        [(small, F32, whole(small))],
        scratch=[
            pltpu.VMEM((count, *small), F32), pltpu.VMEM(small, F32),
            pltpu.VMEM((size, small[0] // 2, small[1]), F32),
            pltpu.SemaphoreType.DMA((4, max(size, count))),
        ],
        collective=6,
    )[0]


def widen_kernel(turned, share_ref, *outs):
    at = 0
    for out, turn in zip(outs, turned):
        if len(out.shape) == 3:
            for c in range(out.shape[0]):
                out[c] = share_ref[at : at + out.shape[2]].astype(F32).T
                at += out.shape[2]
        elif turn:
            out[...] = share_ref[at : at + out.shape[1]].astype(F32).T
            at += out.shape[1]
        else:
            out[...] = share_ref[at : at + out.shape[0]].astype(F32)
            at += out.shape[0]


def widen(chain, share, shapes, turned):
    return chain(
        partial(widen_kernel, turned), "widen", 1, [(share, whole(share.shape))],
        [(shape, F32, whole(shape)) for shape in shapes], mib=32,
    )


def add_kernel(a_ref, b_ref, out_ref):
    out_ref[...] = (a_ref[...].astype(F32) + b_ref[...].astype(F32)).astype(out_ref.dtype)


def plus(chain, a, b):
    block = whole(a.shape)
    return chain(
        add_kernel, "plus", 1, [(a, block), (b, block)], [(a.shape, a.dtype, block)], mib=16
    )[0]


def choose_kernel(flag_ref, a_ref, b_ref, out_ref):
    out_ref[...] = jnp.where(flag_ref[0] > 0, b_ref[...], a_ref[...])


def choose(chain, flag, a, b):
    height, d = a.shape
    block = rows(d, height // 2)
    return chain(
        choose_kernel, "choose", 2, [(a, block), (b, block)], [(a.shape, BF16, block)],
        scalars=(flag,),
    )[0]


def assemble_kernel(core_ref, a_ref, b_ref, *rest):
    rest[-1][...] = jnp.where(core_ref[0] == pl.program_id(0), a_ref[...], b_ref[...])


def assemble(chain, core, chunk, length, a, b, so_far):
    height, d = a.shape
    block = whole((height, d))
    anywhere = pl.BlockSpec(memory_space=pl.ANY)
    return chain(
        assemble_kernel, "assemble", 2,
        [(a, block), (b, block)] + ([] if so_far is None else [(so_far, anywhere)]),
        [((length, d), BF16, pl.BlockSpec((height, d), lambda i, *s: (place_of(chunk, i), 0)))],
        scalars=(core,), alias=() if so_far is None else ((2, 0),), mib=16,
    )[0]


def close_chunk_kernel(closing, core_ref, *refs):
    refs[-1][...] = closing(*refs[:-1])


def close_chunk(chain, closing, core, chunk, a, b, own, small):
    height, d = a.shape
    part = height // 2
    block = rows(d, part)

    def mine(n):
        return pl.BlockSpec((part, n), lambda i, core: (2 * place_of(chunk, core[0]) + i, 0))

    return chain(
        partial(close_chunk_kernel, closing), "close", 2,
        [(a, block), (b, block)] + [(o, mine(o.shape[1])) for o in own] + [(small, whole(small.shape))],
        [(a.shape, BF16, block)],
        scalars=(core,),
    )[0]


def swap_cores(value, size):
    return lax.ppermute(value, "tensor", [(i, i ^ 1) for i in range(size)])


def along(value, hops):
    return lax.ppermute(
        value, "tensor", [(2 * a + c, 2 * b + c) for a, b in hops for c in (0, 1)]
    )


def grad_rows(a, b, x, stats, g, small):
    u = (a[...].astype(F32) + b[...].astype(F32)) * small[0:1]
    mean, inverse = stats[:, 0:1], stats[:, 1:2]
    scaled = (x[...].astype(F32) - mean) * inverse
    back_u = inverse * (
        u
        - jnp.mean(u, axis=-1, keepdims=True)
        - scaled * jnp.mean(u * scaled, axis=-1, keepdims=True)
    )
    return (g[...].astype(F32) + back_u).astype(BF16)


SPLIT = 4
PIECE = TILE // SPLIT


def line_kernel(
    first, gq, gk, gv, pre, x_block, stats_block, wq, wu, small, extra, x_all, g_all, stats_all, *refs
):
    parts, refs = refs[: first // SPLIT], refs[first // SPLIT :]
    output, grad, vectors = refs[:3]
    held, came, own, lines, across, x_own, g_own, stats_own, sums, by_dp, mine, by_tensor = refs[3:15]
    (
        load_sem, peer_send, peer_recv, in_send, in_recv, mid_send, mid_recv, out_send, out_recv,
        fin_send, fin_recv, keep_sem,
    ) = refs[15:]
    chunks = came.shape[0]
    i = pl.program_id(0)
    steps, pieces = 2 * chunks, SPLIT * chunks
    d = came.shape[2]
    row, me = lax.axis_index("dp"), lax.axis_index("tensor")
    count, size = by_dp.shape[0], by_tensor.shape[0]
    core = lax.rem(me, 2)
    chip = me // 2
    peer = me + 1 - 2 * core
    beside = 2 * (chip + 1 - 2 * lax.rem(chip, 2)) + core
    facing = 2 * (3 - chip) + core
    middle = (chip == 1) | (chip == 2)
    end = jnp.logical_not(middle)
    mesh = pl.DeviceIdType.MESH
    barrier = pltpu.get_barrier_semaphore()

    def remote(source, target, send_sem, recv_sem, device, axis="tensor"):
        return pltpu.make_async_remote_copy(
            src_ref=source, dst_ref=target, send_sem=send_sem, recv_sem=recv_sem,
            device_id={axis: device}, device_id_type=mesh,
        )

    shift = pieces - first
    every = pieces + first

    def place(p, before=0):
        start = place_of(p // SPLIT, core) * TILE + lax.rem(p, SPLIT) * PIECE - before
        return pl.ds(pl.multiple_of(start, PIECE), PIECE)

    def peer_copy(c):
        return remote(held.at[c], came.at[c], peer_send.at[c], peer_recv.at[c], peer)

    def in_copy(p):
        return remote(own.at[p], lines.at[p], in_send.at[p], in_recv.at[p], beside)

    def mid_copy(p):
        return remote(own.at[p], across.at[p], mid_send.at[p], mid_recv.at[p], facing)

    def out_copy(p):
        return remote(lines.at[p], lines.at[p], out_send.at[p], out_recv.at[p], beside)

    def fin_copy(p, target):
        return remote(lines.at[p], target, fin_send.at[p], fin_recv.at[p], peer)

    def keep_copy(p, target):
        return pltpu.make_async_copy(lines.at[p], target, keep_sem.at[p])

    def part_copy(p):
        return pltpu.make_async_copy(
            parts[p // SPLIT].at[pl.ds(p % SPLIT * PIECE, PIECE)], own.at[p], keep_sem.at[p]
        )

    def of(p, action):
        @pl.when(p < first)
        def _():
            action(p, output.at[place(p + shift, shift * 2 * PIECE)])

        @pl.when(p >= first)
        def _():
            action(p, grad.at[place(p - first)])

    def loads(p):
        return [
            pltpu.make_async_copy(array.at[place(p)], here.at[p], load_sem.at[n, p])
            for n, (array, here) in enumerate(((x_all, x_own), (g_all, g_own), (stats_all, stats_own)))
        ]

    def dp_copy(n):
        device = lax.rem(row + n, count)
        wide = d // count
        source = sums.at[:, pl.ds(pl.multiple_of(device * wide, 128), wide)]
        return remote(source, by_dp.at[n], load_sem.at[3, n], load_sem.at[4, n], device, "dp")

    def tensor_copy(n):
        device = lax.rem(me + n, size)
        return remote(mine, by_tensor.at[n], load_sem.at[5, n], load_sem.at[6, n], device)

    def hand_over(p, target):
        fin_copy(p, target).start()
        keep_copy(p, target).start()

    def take_in(p):
        in_copy(p).wait_recv()
        own[p] = (own[p].astype(F32) + lines[p].astype(F32)).astype(BF16)
        mid_copy(p).start()

    def finish(p):
        mid_copy(p).wait_recv()

        @pl.when(p < first)
        def _():
            q = p + shift
            lines[p] = output_rows(own[p], x_own[q], across[p], small[...])

        @pl.when(p >= first)
        def _():
            q = p - first
            lines[p] = grad_rows(own[p], across[p], x_own[q], stats_own[q], g_own[q], small[...])

        out_copy(p).start()
        of(p, hand_over)

    def each(action, begin=0, stop=every):
        lax.fori_loop(begin, stop, lambda p, _: (action(p), 0)[1], 0)

    @pl.when(i == 0)
    def _():
        for n in range(1, count):
            pl.semaphore_signal(
                barrier, inc=1, device_id={"dp": lax.rem(row + n, count)}, device_id_type=mesh
            )
        for n in range(1, size):
            pl.semaphore_signal(
                barrier, inc=1, device_id={"tensor": lax.rem(me + n, size)}, device_id_type=mesh
            )
        sums[...] = extra[...]
        for p in range(first):
            part_copy(p).start()
        pl.semaphore_wait(barrier, count + size - 2)
        for p in range(first):
            part_copy(p).wait()

    @pl.when((i == 0) & end)
    def _():
        each(lambda p: in_copy(p).start(), 0, first)

    @pl.when((i == 0) & middle)
    def _():
        each(lambda p: [load.start() for load in loads(p)], 0, pieces)

    @pl.when((i == 1) & middle)
    def _():
        each(lambda p: [load.wait() for load in loads(p)], 0, pieces)

    ours = lax.rem(i, 2)
    half = i // 2
    to = pl.ds(first + SPLIT * half, SPLIT)
    for cut in range(0, d, 2 * TILE):
        cut = slice(cut, cut + 2 * TILE)
        total = nt(pre[...], wu[cut])
        for c, g in enumerate((gq, gk, gv)):
            total = total + nt(g[...], wq[c, cut])
        scaled = (x_block[:, cut].astype(F32) - stats_block[:, 0:1]) * stats_block[:, 1:2]
        sums[0:1, cut] += jnp.sum(total * scaled, axis=0, keepdims=True)
        sums[1:2, cut] += jnp.sum(total, axis=0, keepdims=True)
        total = total.astype(BF16)

        @pl.when(ours == 0)
        def _():
            held[half, :, cut] = total

        @pl.when(ours == 1)
        def _():
            own[to, :, cut] = total.reshape(SPLIT, PIECE, 2 * TILE)

    @pl.when(ours == 0)
    def _():
        peer_copy(half).start()

    @pl.when(ours == 1)
    def _():
        peer_copy(half).wait_recv()
        total = own[to].astype(F32) + came[half].reshape(SPLIT, PIECE, d).astype(F32)
        own[to] = total.astype(BF16)

    @pl.when((ours == 1) & end)
    def _():
        for r in range(SPLIT):
            in_copy(first + SPLIT * half + r).start()

    early = steps
    begin = steps - early

    @pl.when((i >= begin) & middle)
    def _():
        take_in(i - begin)

    @pl.when((i > begin) & middle)
    def _():
        finish(i - begin - 1)

    @pl.when(i == steps - 1)
    def _():
        for n in range(1, count):
            dp_copy(n).start()

    def both(p, _):
        take_in(p)
        finish(p - 1)
        return 0

    def pass_on(p):
        out_copy(p).wait_recv()
        of(p, hand_over)

    some = early + 2 * (every - early) // 3

    @pl.when((i == steps - 1) & middle)
    def _():
        lax.fori_loop(early, some, both, 0)

    @pl.when((i == steps - 1) & end)
    def _():
        each(pass_on, 0, some)

    @pl.when(i == steps - 1)
    def _():
        wide = d // count
        total = sums[:, pl.ds(pl.multiple_of(row * wide, 128), wide)]
        for n in range(1, count):
            dp_copy(n).wait()
            total = total + by_dp[n]
        mine[...] = total
        for n in range(1, size):
            tensor_copy(n).start()

    @pl.when((i == steps - 1) & middle)
    def _():
        lax.fori_loop(some, every, both, 0)
        finish(every - 1)
        each(lambda p: (mid_copy(p).wait_send(), out_copy(p).wait_send()))

    @pl.when((i == steps - 1) & end)
    def _():
        each(pass_on, some)
        each(lambda p: in_copy(p).wait_send())

    @pl.when(i == steps - 1)
    def _():
        total = mine[...]
        for n in range(1, size):
            tensor_copy(n).wait()
            total = total + by_tensor[n]
        vectors[...] = jnp.concatenate([total[:2], mine[2:]])
        for c in range(chunks):
            peer_copy(c).wait_send()
        each(lambda p: of(p, lambda *a: (fin_copy(*a).wait(), keep_copy(*a).wait())))


def line_back(chain, parts, chunks, size, count, gq, gk, gv, pre, x, stats, wq, wu, small, extra, g):
    length, d = x.shape
    width, units = wq.shape[2], wu.shape[1]
    pieces, first = SPLIT * chunks, SPLIT * len(parts)

    def block(n):
        def index(i):
            core = lax.rem(lax.axis_index("tensor"), 2)
            mine = lax.rem(i, 2)
            return (place_of(i // 2, lax.rem(core + 1 + mine, 2)), 0)

        return pl.BlockSpec((TILE, n), index)

    def once(shape):
        zeros = (0,) * len(shape)
        return pl.BlockSpec(shape, lambda *i: zeros, pipeline_mode=pl.Buffered(1))

    far = pl.BlockSpec(memory_space=pltpu.HBM)
    rows_of = lambda n: pltpu.VMEM((n, PIECE, d), BF16)
    sems = pltpu.SemaphoreType.DMA
    vector = (8, d // count)
    return chain(
        partial(line_kernel, first),
        "line_back",
        2 * chunks,
        [(a, block(width)) for a in (gq, gk, gv)]
        + [
            (pre, block(units)), (x, block(d)), (stats, block(PAIR)), (wq, once(wq.shape)),
            (wu, once(wu.shape)), (small, once(small.shape)), (extra, once(extra.shape)),
            (x, far), (g, far), (stats, far),
        ]
        + [(p, far) for p in parts],
        [
            ((first * 2 * PIECE, d), BF16, far), ((length, d), BF16, far),
            (vector, F32, whole(vector)),
        ],
        scratch=[
            pltpu.VMEM((chunks, TILE, d), BF16), pltpu.VMEM((chunks, TILE, d), BF16),
            rows_of(first + pieces), rows_of(first + pieces), rows_of(first + pieces),
            rows_of(pieces), rows_of(pieces),
            pltpu.VMEM((pieces, PIECE, PAIR), F32),
            pltpu.VMEM((8, d), F32), pltpu.VMEM((count, *vector), F32), pltpu.VMEM(vector, F32),
            pltpu.VMEM((size, *vector), F32),
            sems((7, max(pieces, size, count))), sems((chunks,)), sems((chunks,)),
        ]
        + [sems((first + pieces,))] * 9,
        collective=5,
        flops=200e9,
        mib=62,
    )


def flow(chain, size, core, chunk, total, closing, results, key, length):
    chips = size // 2
    chip = lax.axis_index("tensor") // 2
    distance = jnp.where(chip < chips // 2, chips // 2 - 1 - chip, chip - chips // 2)
    for s in range(chips // 2 - 1):
        came = along(total, [(s, s + 1), (chips - 1 - s, chips - 2 - s)])
        yield
        total = plus(chain, total, came)
    a, b = chips // 2 - 1, chips // 2
    came = along(total, [(a, b), (b, a)])
    yield
    value = closing(chunk, total, came)
    for s in range(chips // 2 - 1):
        a, b = chips // 2 - 1 - s, chips // 2 + s
        came = along(value, [(a, a - 1), (b, b + 1)])
        yield
        value = choose(chain, (distance == s + 1).astype(jnp.int32)[None], value, came)
    peer = swap_cores(value, size)
    yield
    results[key] = assemble(chain, core, chunk, length, value, peer, results.get(key))


def on_device(
    size,
    inputs,
    segment_ids,
    norm_gain,
    norm_bias,
    qkv_weight,
    qkv_bias,
    out_weight,
    out_bias,
    up_weight,
    up_bias,
    down_weight,
    down_bias,
    cotangent,
):
    x, g, segment_row = inputs[0], cotangent[0], segment_ids[0]
    length, d = x.shape
    width, units = qkv_weight.shape[2], up_weight.shape[1]
    count = lax.axis_size("dp")
    core = (lax.axis_index("tensor") % 2).astype(jnp.int32)[None]

    start = jnp.sum((segment_row[None, :] < segment_row[:, None]).astype(jnp.int32), axis=1)
    small = jnp.stack([norm_gain, norm_bias, out_bias, down_bias] + [norm_gain] * 4).astype(F32)
    wq = qkv_weight.transpose(1, 0, 2)

    chain = Chain()
    normed, stats, q, k, v, hidden, slope, cos_wide, sin_wide = first(
        chain, x, small, wq, qkv_bias, up_weight, up_bias, start
    )
    mixed, log = attend(chain, start, q, k, v)
    rest = 2 if size == 8 else 0
    lower = length - rest * (length // CHUNKS)
    weights = (mixed, hidden, out_weight, down_weight)
    summed = lax.psum(branch(chain, lower, *weights), "tensor")
    parts = branch_rest(chain, rest, CHUNKS - rest, *weights) if rest else []

    pre, gm, delta, g_sums, up_sums = back(chain, g, slope, mixed, out_weight, down_weight)
    scatter = lambda a: lax.psum_scatter(a, "dp", scatter_dimension=1, tiled=True)
    near = scatter(weight_grad(chain, "weight_grad_g", [hidden, mixed], g))
    tiles = length // TILE
    *packed, qkv_sums, _ = attend_back(
        chain, 0, tiles, start, log, delta, q, k, v, gm, cos_wide, sin_wide, [log]
    )
    far = scatter(weight_grad(chain, "weight_grad_n", [pre, *packed], normed))

    by_share = lambda a: a.reshape(-1, count, HD // count).swapaxes(0, 1).reshape(count, -1)
    part = d // count
    narrow = jnp.concatenate([by_share(up_sums[0]), by_share(qkv_sums[:3])], axis=1)
    narrow = jnp.pad(narrow, ((0, 0), (0, part - narrow.shape[1]))).reshape(1, d)
    if size == 8:
        extra = jnp.concatenate([jnp.zeros((2, d), F32), g_sums[:1], narrow, jnp.zeros((4, d), F32)])
        upper, grad, vectors = line_back(
            chain, parts, CHUNKS, size, count, *packed, pre, x, stats, wq, up_weight, small, extra, g
        )
    else:

        results = {}

        def line(parts, closing, own, key):
            finish = lambda chunk, a, b: close_chunk(chain, closing, core, chunk, a, b, own, small)
            flows = [
                flow(chain, size, core, c, parts[c], finish, results, key, length)
                for c in range(CHUNKS)
            ]
            while flows:
                flows = [f for f in flows if next(f, flows) is None]

        norm_sums, *parts = normed_back(chain, CHUNKS, *packed, pre, x, stats, wq, up_weight)
        line(parts, grad_rows, [x, stats, g], "grad")
        vectors = jnp.concatenate([norm_sums[:2], g_sums[:1], narrow]).reshape(4, count, part)
        vectors = vectors.swapaxes(0, 1).reshape(count, -1, 128)
        vectors = add_vectors(chain, vectors, size, count).reshape(4, part)
    if size == 8:
        output, input_grad, down_share, out_share, up_share, qkv_share = last(
            chain, summed, x, small, upper, grad, near, far, width, units
        )
    else:
        output, input_grad = close_both(chain, summed, x, small, results["grad"])
        shapes = [(units, part), (width, part)]
        down_share, out_share = widen(chain, near, shapes, (False, False))
        shapes = [(part, units), (3, part, width)]
        up_share, qkv_share = widen(chain, far, shapes, (True, True))
    up_b_share = vectors[3, : units // count].reshape(-1, HD // count)
    qkv_b_share = vectors[3, units // count : (units + 3 * width) // count].reshape(3, -1, HD // count)

    return (
        output[None],
        input_grad[None],
        vectors[0],
        vectors[1],
        qkv_share.transpose(1, 0, 2),
        qkv_b_share,
        out_share,
        vectors[2],
        up_share,
        up_b_share,
        down_share,
        vectors[2],
    )


def solution(mesh):
    placed = (
        P("dp", None, None),
        P("dp", None),
        P(),
        P(),
        P(None, None, "tensor"),
        P(None, "tensor"),
        P("tensor", None),
        P(),
        P(None, "tensor"),
        P("tensor"),
        P("tensor", None),
        P(),
        P("dp", None, None),
    )
    return jax.shard_map(
        partial(on_device, mesh.shape["tensor"]),
        mesh=mesh,
        in_specs=placed,
        out_specs=(
            P("dp", None, None),
            P("dp", None, None),
            P("dp"),
            P("dp"),
            P("dp", None, "tensor"),
            P(None, "tensor", "dp"),
            P("tensor", "dp"),
            P("dp"),
            P("dp", "tensor"),
            P("tensor", "dp"),
            P("tensor", "dp"),
            P("dp"),
        ),
        check_vma=False,
    )
```

```python
from functools import partial

import jax
import jax.numpy as jnp
from jax import lax
from jax.experimental import pallas as pl
from jax.experimental.pallas import tpu as pltpu
from jax.sharding import PartitionSpec as P

HD = 64
ROT = 32
PAIR = 2 * HD
TILE = 256
CHUNKS = 4
NEG = -1e30
MIB = 1 << 20
F32 = jnp.float32
BF16 = jnp.bfloat16


class Chain:
    def __init__(self):
        self.link = jnp.zeros((8, 128), F32)

    def __call__(
        self, kernel, name, grid, ins, outs, scalars=(), scratch=(), alias=(), mib=58, flops=1, collective=None
    ):
        taken, given = len(scalars) + len(ins), len(outs)

        def body(*refs):
            kernel(*refs[:taken], *refs[taken + 1 : taken + 1 + given], *refs[taken + 2 + given :])

        anywhere = pl.BlockSpec(memory_space=pltpu.HBM)
        results = pl.pallas_call(
            body,
            grid_spec=pltpu.PrefetchScalarGridSpec(
                num_scalar_prefetch=len(scalars),
                grid=(grid,),
                in_specs=[spec for _, spec in ins] + [anywhere],
                out_specs=[spec for _, _, spec in outs] + [anywhere],
                scratch_shapes=list(scratch),
            ),
            out_shape=[jax.ShapeDtypeStruct(shape, dtype) for shape, dtype, _ in outs]
            + [jax.ShapeDtypeStruct(self.link.shape, F32)],
            input_output_aliases={taken: given, **{len(scalars) + i: o for i, o in alias}},
            compiler_params=pltpu.CompilerParams(
                dimension_semantics=("arbitrary",), vmem_limit_bytes=mib * MIB,
                collective_id=collective, has_side_effects=collective is not None,
            ),
            cost_estimate=pl.CostEstimate(flops=int(flops), bytes_accessed=1, transcendentals=0),
            name=name,
        )(*scalars, *[array for array, _ in ins], self.link)
        self.link = results[-1]
        return results[:-1]


def whole(shape):
    zeros = (0,) * len(shape)
    return pl.BlockSpec(shape, lambda *i: zeros)


def rows(n, height=TILE):
    return pl.BlockSpec((height, n), lambda i, *s: (i, 0))


def nn(a, b):
    return lax.dot_general(a, b, (((1,), (0,)), ((), ())), preferred_element_type=F32)


def nt(a, b):
    return lax.dot_general(a, b, (((1,), (1,)), ((), ())), preferred_element_type=F32)


def tn(a, b):
    return lax.dot_general(a, b, (((0,), (0,)), ((), ())), preferred_element_type=F32)


def rotated(x, cos_wide, sin_wide):
    lane = lax.broadcasted_iota(jnp.int32, x.shape, 1) % HD
    half = ROT // 2
    other = jnp.where(
        lane < half, pltpu.roll(x, PAIR - half, 1), pltpu.roll(x, half, 1)
    )
    return x * cos_wide + other * sin_wide


def row_stats(x):
    mean = jnp.mean(x, axis=-1, keepdims=True)
    centered = x - mean
    inverse = lax.rsqrt(jnp.mean(centered * centered, axis=-1, keepdims=True) + 1e-05)
    return centered * inverse, mean, inverse


def gelu_both(u):
    c = 0.7978845608028654
    u2 = u * u
    gate = 0.5 + 0.5 * jnp.tanh(u * (c + (c * 0.044715) * u2))
    value = u * gate
    slope = gate + value * (1.0 - gate) * (2.0 * c + (6.0 * c * 0.044715) * u2)
    return value, slope


def first_kernel(
    x0_ref, x1_ref, x2_ref, small_ref, wq_ref, bq_ref, wu_ref, bu_ref, start_ref, freq_ref,
    normed_ref, stats_ref, q_ref, k_ref, v_ref, hidden_ref, slope_ref, cos_ref, sin_ref,
    even, odd, even_stats,
):
    s = pl.program_id(0)
    gain, shift = small_ref[0:1], small_ref[1:2]
    lane = lax.broadcasted_iota(jnp.int32, (TILE, PAIR), 1)

    def norm(x):
        scaled, mean, inverse = row_stats(x.astype(F32))
        return (scaled * gain + shift).astype(BF16), jnp.where(lane == 0, mean, inverse)

    @pl.when(s == 0)
    def _():
        even[...], even_stats[...] = norm(x0_ref[...])

    half = ROT // 2
    unit = lax.broadcasted_iota(jnp.int32, (half, PAIR), 1) % HD
    index = lax.broadcasted_iota(jnp.int32, (half, PAIR), 0)
    first_half = (unit == index).astype(F32)
    second_half = (unit == index + half).astype(F32)
    bias = bq_ref[...].astype(F32)

    def spread(a, b):
        return lax.dot_general(
            a, b, (((0,), (0,)), ((), ())), precision=lax.Precision.HIGHEST,
            preferred_element_type=F32,
        )

    def project(t, normed):
        here = slice(t * TILE, (t + 1) * TILE)
        place = lax.broadcasted_iota(jnp.int32, (1, TILE), 1) + (2 * s + t) * TILE
        angle = freq_ref[...] * (place - start_ref[:, here]).astype(F32)
        cos_wide = spread(jnp.cos(angle), first_half + second_half)
        cos_wide = jnp.where(lane % HD < ROT, cos_wide, 1.0)
        sin_wide = spread(jnp.sin(angle), second_half - first_half)
        cos_ref[here], sin_ref[here] = cos_wide, sin_wide
        for c, out in enumerate((q_ref, k_ref, v_ref)):
            packed = nn(normed, wq_ref[c]) + bias[c : c + 1]
            if c == 2:
                out[here] = packed.astype(BF16)
            else:
                for p in range(packed.shape[1] // PAIR):
                    cut = slice(p * PAIR, (p + 1) * PAIR)
                    turned = rotated(packed[:, cut], cos_wide, sin_wide).astype(BF16)
                    out[here, cut] = turned * (HD**-0.5) if c == 0 else turned
        units = wu_ref.shape[1]
        for n in range(0, units, TILE):
            cut = slice(n, n + TILE)
            value, slope = gelu_both(nn(normed, wu_ref[:, cut]) + bu_ref[:, cut])
            hidden_ref[here, cut] = value.astype(BF16)
            slope_ref[here, cut] = slope.astype(BF16)

    normed = even[...]
    normed_ref[:TILE] = normed
    stats_ref[:TILE] = even_stats[...]
    after, after_stats = norm(x1_ref[...])
    odd[...] = after
    normed_ref[TILE:] = after
    stats_ref[TILE:] = after_stats
    project(0, normed)
    even[...], even_stats[...] = norm(x2_ref[...])
    project(1, odd[...])


def first(chain, x, small, wq, bq, wu, bu, start):
    length, d = x.shape
    width, units = wq.shape[2], wu.shape[1]
    tiles = length // TILE
    freq = 10000.0 ** (-jnp.arange(ROT // 2, dtype=F32) * 2.0 / ROT)
    at = lambda f: pl.BlockSpec((TILE, d), lambda s: (f(s), 0))
    big = lambda n: rows(n, 2 * TILE)
    return chain(
        first_kernel,
        "first",
        tiles // 2,
        [
            (x, at(lambda s: 0)),
            (x, at(lambda s: 2 * s + 1)),
            (x, at(lambda s: jnp.minimum(2 * s + 2, tiles - 1))),
            (small, whole(small.shape)), (wq, whole(wq.shape)), (bq, whole(bq.shape)),
            (wu, whole(wu.shape)), (bu[None].astype(F32), whole((1, units))),
            (start[None], pl.BlockSpec((1, 2 * TILE), lambda s: (0, s))),
            (jnp.broadcast_to(freq[:, None], (ROT // 2, TILE)), whole((ROT // 2, TILE))),
        ],
        [((length, d), BF16, big(d)), ((length, PAIR), F32, big(PAIR))]
        + [((length, n), BF16, big(n)) for n in (width, width, width, units, units)]
        + [((length, PAIR), F32, big(PAIR))] * 2,
        scratch=[pltpu.VMEM((TILE, d), BF16)] * 2 + [pltpu.VMEM((TILE, PAIR), F32)],
        mib=40,
        flops=35e9,
    )


def halves(x):
    left = lax.broadcasted_iota(jnp.int32, x.shape, 1) < HD
    zero = jnp.zeros(x.shape, x.dtype)
    return [jnp.where(left, x, zero), jnp.where(left, zero, x)]


def pair_cuts(width):
    return [slice(p, p + PAIR) for p in range(0, width, PAIR)]


def attend_kernel(start_sref, start_ref, q_ref, k_ref, v_ref, mixed_ref, log_ref):
    i = pl.program_id(0)
    cuts = pair_cuts(q_ref.shape[1])
    heads = range(2 * len(cuts))
    key_row = lax.broadcasted_iota(jnp.int32, (TILE, TILE), 0)
    query = lax.broadcasted_iota(jnp.int32, (TILE, TILE), 1) + i * TILE
    start = start_ref[...]
    queries = [q for cut in cuts for q in halves(q_ref[:, cut])]

    def step(j, carry):
        tops, totals, sums = carry
        there = pl.ds(pl.multiple_of(j * TILE, TILE), TILE)
        place = key_row + j * TILE
        allowed = (place >= start) & (place <= query)
        k = [k_ref[there, cut] for cut in cuts]
        v = [v_ref[there, cut] for cut in cuts]
        s = [nt(k[h // 2], queries[h]) for h in heads]
        s = [jnp.where(allowed, a, NEG) for a in s]
        top = [jnp.maximum(tops[h], jnp.max(s[h], axis=0, keepdims=True)) for h in heads]
        alpha = [jnp.exp(tops[h] - top[h]) for h in heads]
        w = [jnp.exp(s[h] - top[h]) for h in heads]
        totals = [totals[h] * alpha[h] + jnp.sum(w[h], axis=0, keepdims=True) for h in heads]
        w = [a.astype(BF16) for a in w]
        add = [tn(v[h // 2], w[h])[h % 2 * HD : (h % 2 + 1) * HD] for h in heads]
        sums = [sums[h] * alpha[h] + add[h] for h in heads]
        return tuple(top), tuple(totals), tuple(sums)

    empty = (
        tuple(jnp.full((1, TILE), NEG, F32) for _ in heads),
        tuple(jnp.zeros((1, TILE), F32) for _ in heads),
        tuple(jnp.zeros((HD, TILE), F32) for _ in heads),
    )
    low = start_sref[i * TILE] // TILE
    tops, totals, sums = lax.fori_loop(low, i + 1, step, empty)
    log_ref[...] = jnp.zeros_like(log_ref)
    for h in heads:
        log_ref[h : h + 1] = tops[h] + jnp.log(totals[h])
    mixed_ref[...] = jnp.concatenate([sums[h] * (1.0 / totals[h]) for h in heads]).T.astype(BF16)


def attend(chain, start, q, k, v):
    length, width = q.shape
    full = whole((length, width))
    return chain(
        attend_kernel,
        "attend",
        length // TILE,
        [
            (start[None], pl.BlockSpec((1, TILE), lambda i, *s: (0, i))),
            (q, rows(width)), (k, full), (v, full),
        ],
        [
            ((length, width), BF16, rows(width)),
            ((8, length), F32, pl.BlockSpec((8, TILE), lambda i, *s: (0, i))),
        ],
        scalars=(start,),
        mib=24,
        flops=19e9,
    )


def attend_back_kernel(
    begin, start_sref, start_ref, log_ref, delta_ref, q_ref, k_ref, v_ref, g_ref, cos_ref, sin_ref,
    totals_in, *refs,
):
    gq_ref, gk_ref, gv_ref, bias_ref, totals = refs[-5:]
    j = pl.program_id(0) + begin
    length, width = q_ref.shape
    cuts = pair_cuts(width)
    heads = range(2 * len(cuts))
    here = pl.ds(pl.multiple_of(j * TILE, TILE), TILE)

    @pl.when(pl.program_id(0) == 0)
    def _():
        totals[...] = totals_in[...] if begin else jnp.zeros_like(totals)
        bias_ref[...] = jnp.zeros_like(bias_ref)

    place = j * TILE + lax.broadcasted_iota(jnp.int32, (TILE, TILE), 0)
    query = lax.broadcasted_iota(jnp.int32, (TILE, TILE), 1)
    keys = [k_ref[here, cut] for cut in cuts]
    split = [half for k in keys for half in halves(k)]
    values = [v_ref[here, cut] for cut in cuts]

    def step(i, carry):
        gk, gv = carry
        there = pl.ds(pl.multiple_of(i * TILE, TILE), TILE)
        allowed = (place >= start_ref[:, there]) & (place <= query + i * TILE)
        qs = [half for cut in cuts for half in halves(q_ref[there, cut])]
        gs = [half for cut in cuts for half in halves(g_ref[there, cut])]
        s = [nt(keys[h // 2], qs[h]) for h in heads]
        gp = [nt(values[h // 2], gs[h]) for h in heads]
        w = [jnp.exp(jnp.where(allowed, s[h] - log_ref[h : h + 1, there], NEG)) for h in heads]
        ds = [(w[h] * (gp[h] - delta_ref[h : h + 1, there])).astype(BF16) for h in heads]
        w = [a.astype(BF16) for a in w]
        both = lambda f: tuple(f(h) + f(h + 1) for h in heads[::2])
        gv = [a + b for a, b in zip(gv, both(lambda h: nn(w[h], gs[h])))]
        gk = [a + b for a, b in zip(gk, both(lambda h: nn(ds[h], qs[h])))]
        for cut, gq in zip(cuts, both(lambda h: tn(ds[h], split[h]))):
            totals[there, cut] += gq
        return tuple(gk), tuple(gv)

    high = sum((start_sref[b * TILE] < (j + 1) * TILE).astype(jnp.int32) for b in range(length // TILE))
    empty = tuple(jnp.zeros((TILE, PAIR), F32) for _ in cuts)
    gks, gvs = lax.fori_loop(j, high, step, (empty, empty))
    cos_wide, sin_wide = cos_ref[...], -sin_ref[...]
    for cut, gk, gv in zip(cuts, gks, gvs):
        gq = rotated(totals[here, cut] * (HD**-0.5), cos_wide, sin_wide).astype(BF16)
        gk = rotated(gk, cos_wide, sin_wide).astype(BF16)
        for c, (g, out) in enumerate(((gq, gq_ref), (gk, gk_ref), (gv.astype(BF16), gv_ref))):
            out[:, cut] = g
            bias_ref[c : c + 1, cut] += jnp.sum(g.astype(F32), axis=0, keepdims=True)


def attend_back(chain, begin, end, start, log, delta, q, k, v, g, cos_wide, sin_wide, before):
    length, width = q.shape
    full = whole((length, width))
    shifted = lambda n: pl.BlockSpec((TILE, n), lambda i, *s: (i + begin, 0))
    anywhere = pl.BlockSpec(memory_space=pl.ANY)
    so_far = before[:3] if begin else []
    return chain(
        partial(attend_back_kernel, begin),
        f"attend_back_{begin}",
        end - begin,
        [
            (start[None], whole((1, length))), (log, whole((8, length))), (delta, whole((8, length))),
            (q, full), (k, full), (v, full), (g, full), (cos_wide, shifted(PAIR)), (sin_wide, shifted(PAIR)),
            (before[-1], full if begin else anywhere),
        ]
        + [(a, anywhere) for a in so_far],
        [((length, width), BF16, shifted(width))] * 3
        + [((8, width), F32, whole((8, width))), ((length, width), F32, full)],
        scalars=(start,),
        alias=tuple((10 + n, n) for n in range(len(so_far))),
        flops=31e9,
    )


def place_of(chunk, core):
    return 4 * (chunk // 2) + 2 * core + chunk % 2


def own_rows(chunks, half, skip=0):
    def spec(n):
        def index(i):
            core = lax.rem(lax.axis_index("tensor"), 2)
            steps = chunks // 2
            return (skip + 2 * lax.rem(i, steps) + jnp.where(i < steps, 1 - core, core), 0)

        return pl.BlockSpec((2 * half, n), index)

    return spec


def paired(product, chunks, ins, *refs):
    given, extra, sums, held, came, send_sem, recv_sem = (
        refs[:ins], refs[ins : len(refs) - chunks - 4], refs[-chunks - 4 : -4], *refs[-4:]
    )
    i = pl.program_id(0)
    steps = chunks // 2
    half, d = sums[0].shape
    me = lax.axis_index("tensor")
    peer = me + 1 - 2 * lax.rem(me, 2)
    barrier = pltpu.get_barrier_semaphore()

    def copy(n):
        return pltpu.make_async_remote_copy(
            src_ref=held.at[n], dst_ref=came.at[n], send_sem=send_sem.at[n], recv_sem=recv_sem.at[n],
            device_id={"tensor": peer}, device_id_type=pl.DeviceIdType.MESH,
        )

    @pl.when(i == 0)
    def _():
        pl.semaphore_signal(
            barrier, inc=1, device_id={"tensor": peer}, device_id_type=pl.DeviceIdType.MESH
        )
        for e in extra:
            e[...] = jnp.zeros_like(e)

    for cut in range(0, d, 2 * TILE):
        cut = slice(cut, cut + 2 * TILE)
        total = product(cut, given, extra).astype(BF16)
        held[pl.ds(2 * i, 2), :, cut] = total.reshape(2, half, 2 * TILE)

    @pl.when(i == 0)
    def _():
        pl.semaphore_wait(barrier, 1)

    for n in range(steps):

        @pl.when(i == n)
        def _(n=n):
            copy(2 * n).start()
            copy(2 * n + 1).start()

        @pl.when(i == steps + n)
        def _(n=n):
            for c in (2 * n, 2 * n + 1):
                copy(c).wait()
                total = held[chunks + c].astype(F32) + came[c].astype(F32)
                sums[c][...] = total.astype(BF16)


def pair_call(chain, product, name, collective, chunks, half, d, ins, extra):
    return chain(
        partial(paired, product, chunks, len(ins)),
        name,
        chunks,
        ins,
        extra + [((half, d), BF16, whole((half, d)))] * chunks,
        scratch=[pltpu.VMEM((2 * chunks, half, d), BF16), pltpu.VMEM((chunks, half, d), BF16)]
        + [pltpu.SemaphoreType.DMA((chunks,))] * 2,
        flops=13e9,
        collective=collective,
    )


def branch_kernel(mixed, hidden, wo, wd, out):
    for cut in range(0, out.shape[1], 2 * TILE):
        cut = slice(cut, cut + 2 * TILE)
        out[:, cut] = (nn(mixed[...], wo[:, cut]) + nn(hidden[...], wd[:, cut])).astype(BF16)


def branch(chain, length, mixed, hidden, wo, wd):
    d = wo.shape[1]
    big = lambda n: rows(n, 2 * TILE)
    return chain(
        branch_kernel,
        "branch",
        length // (2 * TILE),
        [
            (mixed, big(mixed.shape[1])), (hidden, big(hidden.shape[1])),
            (wo, whole(wo.shape)), (wd, whole(wd.shape)),
        ],
        [((length, d), BF16, big(d))],
        mib=30,
        flops=7e9,
    )[0]


def branch_product(cut, given, extra):
    mixed, hidden, wo, wd = given
    return nn(mixed[...], wo[:, cut]) + nn(hidden[...], wd[:, cut])


def branch_rest(chain, chunks, skip, mixed, hidden, wo, wd):
    length, d = mixed.shape[0], wo.shape[1]
    half = length // (2 * (chunks + skip))
    spec = own_rows(chunks, half, skip)
    ins = [
        (mixed, spec(mixed.shape[1])), (hidden, spec(hidden.shape[1])),
        (wo, whole(wo.shape)), (wd, whole(wd.shape)),
    ]
    return pair_call(chain, branch_product, "branch_rest", 1, chunks, half, d, ins, [])


def last_kernel(
    steps, summed, x, small, rest, grad, down_in, out_in, up_in, q_in, k_in, v_in,
    output, input_grad, down, out, up, qkv,
):
    i = pl.program_id(0)
    input_grad[...] = grad[...]
    down[...] = down_in[...].astype(F32)
    out[...] = out_in[...].astype(F32)
    up[...] = up_in[...].astype(F32).T
    for c, part in enumerate((q_in, k_in, v_in)):
        qkv[c] = part[...].astype(F32).T

    @pl.when(i < steps)
    def _():
        output[...] = output_rows(summed, x[...], None, small)

    @pl.when(i >= steps)
    def _():
        output[...] = rest[...]


def last(chain, summed, x, small, rest, grad, near, far, width, units):
    length, d = x.shape
    part = near.shape[1]
    lower = summed.shape[0]
    grid = 8
    high = length // grid
    steps = lower // high
    tall, slim, thin = units // grid, width // grid, 2 * part // grid
    block = rows(d, high)
    low = pl.BlockSpec((high, d), lambda i: (jnp.minimum(i, steps - 1), 0))
    upper = pl.BlockSpec((high, d), lambda i: (jnp.maximum(i - steps, 0), 0))
    third = lambda c: pl.BlockSpec((width, thin), lambda i: (units // width + c, i // 2))
    return chain(
        partial(last_kernel, steps), "last", grid,
        [
            (summed, low), (x, low), (small, whole(small.shape)), (rest, upper), (grad, block),
            (near, rows(part, tall)),
            (near, pl.BlockSpec((slim, part), lambda i: (units // slim + i, 0))),
            (far, rows(part, tall)), (far, third(0)), (far, third(1)), (far, third(2)),
        ],
        [
            ((length, d), BF16, block), ((length, d), BF16, block),
            ((units, part), F32, rows(part, tall)), ((width, part), F32, rows(part, slim)),
            ((part, units), F32, pl.BlockSpec((part, tall), lambda i: (0, i))),
            ((3, part, width), F32, pl.BlockSpec((3, thin, width), lambda i: (0, i // 2, 0))),
        ],
    )


def output_rows(a, x, b, small):
    total = a[...].astype(F32)
    if b is not None:
        total = total + b[...].astype(F32)
    return (x.astype(F32) + total + small[2:3] + small[3:4]).astype(BF16)


def close_kernel(summed, x, small, grad, output, input_grad):
    output[...] = output_rows(summed, x[...], None, small)
    input_grad[...] = grad[...]


def close_both(chain, summed, x, small, grad):
    length, d = x.shape
    block = rows(d, 2 * TILE)
    return chain(
        close_kernel, "close_both", length // (2 * TILE),
        [(summed, block), (x, block), (small, whole(small.shape)), (grad, block)],
        [((length, d), BF16, block)] * 2,
    )


def back_kernel(g_ref, slope_ref, mixed_ref, wo_ref, wd_ref, pre_ref, gm_ref, delta_ref, sums_ref, up_ref):
    @pl.when(pl.program_id(0) == 0)
    def _():
        sums_ref[...] = jnp.zeros_like(sums_ref)
        up_ref[...] = jnp.zeros_like(up_ref)

    g = g_ref[...]
    for n in range(0, wd_ref.shape[0], 2 * TILE):
        cut = slice(n, n + 2 * TILE)
        pre = (nt(g, wd_ref[cut]) * slope_ref[:, cut].astype(F32)).astype(BF16)
        pre_ref[:, cut] = pre
        up_ref[0:1, cut] += jnp.sum(pre.astype(F32), axis=0, keepdims=True)
    gm = nt(g, wo_ref[...]).astype(BF16)
    gm_ref[...] = gm
    product = gm.astype(F32) * mixed_ref[...].astype(F32)
    coarse = product.astype(BF16)
    fine = (product - coarse.astype(F32)).astype(BF16)
    width = gm.shape[1]
    pick = (
        lax.broadcasted_iota(jnp.int32, (8, width), 1) // HD
        == lax.broadcasted_iota(jnp.int32, (8, width), 0)
    ).astype(BF16)
    delta_ref[...] = nt(pick, coarse) + nt(pick, fine)
    sums_ref[0:1] += jnp.sum(g.astype(F32), axis=0, keepdims=True)


def back(chain, g, slope, mixed, wo, wd):
    length, d = g.shape
    width, units = wo.shape[0], wd.shape[0]
    big = lambda n: rows(n, 2 * TILE)
    return chain(
        back_kernel,
        "back",
        length // (2 * TILE),
        [
            (g, big(d)), (slope, big(units)), (mixed, big(width)),
            (wo, whole(wo.shape)), (wd, whole(wd.shape)),
        ],
        [
            ((length, units), BF16, big(units)), ((length, width), BF16, big(width)),
            ((8, length), F32, pl.BlockSpec((8, 2 * TILE), lambda i, *s: (0, i))),
            ((8, d), F32, whole((8, d))), ((8, units), F32, whole((8, units))),
        ],
        flops=15e9,
    )


def normed_back_product(cut, given, extra):
    gq, gk, gv, pre, x, stats, wq, wu = given
    (sums,) = extra
    total = nt(pre[...], wu[cut])
    for c, g in enumerate((gq, gk, gv)):
        total = total + nt(g[...], wq[c, cut])
    scaled = (x[:, cut].astype(F32) - stats[:, 0:1]) * stats[:, 1:2]
    sums[0:1, cut] += jnp.sum(total * scaled, axis=0, keepdims=True)
    sums[1:2, cut] += jnp.sum(total, axis=0, keepdims=True)
    return total


def normed_back(chain, chunks, gq, gk, gv, pre, x, stats, wq, wu):
    length, d = x.shape
    width, units = wq.shape[2], wu.shape[1]
    half = length // (2 * chunks)
    spec = own_rows(chunks, half)
    ins = [(a, spec(width)) for a in (gq, gk, gv)] + [
        (pre, spec(units)), (x, spec(d)), (stats, spec(PAIR)),
        (wq, whole(wq.shape)), (wu, whole(wu.shape)),
    ]
    return pair_call(
        chain, normed_back_product, "normed_back", 2, chunks, half, d, ins,
        [((8, d), F32, whole((8, d)))],
    )


def weight_grad_kernel(counts, *refs):
    *lefts, right, out = refs
    i = pl.program_id(0)
    done = 0
    for left, count in zip(lefts, counts):

        @pl.when((i >= done) & (i < done + count))
        def _(left=left):
            out[...] = tn(left[...], right[...]).astype(BF16)

        done += count


def weight_grad(chain, name, lefts, right):
    length, d = right.shape
    wide = min(TILE, *[a.shape[1] for a in lefts])
    counts = tuple(a.shape[1] // wide for a in lefts)
    ins, done = [], 0
    for a, count in zip(lefts, counts):
        place = lambda i, done=done, count=count: jnp.clip(i - done, 0, count - 1)
        ins.append((a, pl.BlockSpec((length, wide), lambda i, f=place: (0, f(i)))))
        done += count
    return chain(
        partial(weight_grad_kernel, counts),
        name,
        done,
        ins + [(right, whole(right.shape))],
        [((done * wide, d), BF16, rows(d, wide))],
        flops=2 * length * d * done * wide,
    )[0]


def vectors_kernel(size, count, vectors, total, came, part, wide, sems):
    row, me = lax.axis_index("dp"), lax.axis_index("tensor")
    barrier = pltpu.get_barrier_semaphore()
    mesh = pl.DeviceIdType.MESH
    half = part.shape[0] // 2

    def by_row(n):
        peer = lax.rem(row + n, count)
        return pltpu.make_async_remote_copy(
            src_ref=vectors.at[peer], dst_ref=came.at[n], send_sem=sems.at[0, n],
            recv_sem=sems.at[1, n], device_id={"dp": peer}, device_id_type=mesh,
        )

    def by_column(n):
        peer = lax.rem(me + n, size)
        return pltpu.make_async_remote_copy(
            src_ref=part.at[pl.ds(0, half)], dst_ref=wide.at[n], send_sem=sems.at[2, n],
            recv_sem=sems.at[3, n], device_id={"tensor": peer}, device_id_type=mesh,
        )

    for n in range(1, count):
        pl.semaphore_signal(
            barrier, inc=1, device_id={"dp": lax.rem(row + n, count)}, device_id_type=mesh
        )
    for n in range(1, size):
        pl.semaphore_signal(
            barrier, inc=1, device_id={"tensor": lax.rem(me + n, size)}, device_id_type=mesh
        )
    pl.semaphore_wait(barrier, count + size - 2)
    for n in range(1, count):
        by_row(n).start()
    mine = vectors[row]
    for n in range(1, count):
        by_row(n).wait()
        mine = mine + came[n]
    part[...] = mine
    for n in range(1, size):
        by_column(n).start()
    upper = mine[:half]
    for n in range(1, size):
        by_column(n).wait()
        upper = upper + wide[n]
    total[:half] = upper
    total[half:] = mine[half:]


def add_vectors(chain, vectors, size, count):
    small = vectors.shape[1:]
    return chain(
        partial(vectors_kernel, size, count), "add_vectors", 1, [(vectors, whole(vectors.shape))],
        [(small, F32, whole(small))],
        scratch=[
            pltpu.VMEM((count, *small), F32), pltpu.VMEM(small, F32),
            pltpu.VMEM((size, small[0] // 2, small[1]), F32),
            pltpu.SemaphoreType.DMA((4, max(size, count))),
        ],
        collective=6,
    )[0]


def widen_kernel(turned, share_ref, *outs):
    at = 0
    for out, turn in zip(outs, turned):
        if len(out.shape) == 3:
            for c in range(out.shape[0]):
                out[c] = share_ref[at : at + out.shape[2]].astype(F32).T
                at += out.shape[2]
        elif turn:
            out[...] = share_ref[at : at + out.shape[1]].astype(F32).T
            at += out.shape[1]
        else:
            out[...] = share_ref[at : at + out.shape[0]].astype(F32)
            at += out.shape[0]


def widen(chain, share, shapes, turned):
    return chain(
        partial(widen_kernel, turned), "widen", 1, [(share, whole(share.shape))],
        [(shape, F32, whole(shape)) for shape in shapes], mib=32,
    )


def add_kernel(a_ref, b_ref, out_ref):
    out_ref[...] = (a_ref[...].astype(F32) + b_ref[...].astype(F32)).astype(out_ref.dtype)


def plus(chain, a, b):
    block = whole(a.shape)
    return chain(
        add_kernel, "plus", 1, [(a, block), (b, block)], [(a.shape, a.dtype, block)], mib=16
    )[0]


def choose_kernel(flag_ref, a_ref, b_ref, out_ref):
    out_ref[...] = jnp.where(flag_ref[0] > 0, b_ref[...], a_ref[...])


def choose(chain, flag, a, b):
    height, d = a.shape
    block = rows(d, height // 2)
    return chain(
        choose_kernel, "choose", 2, [(a, block), (b, block)], [(a.shape, BF16, block)],
        scalars=(flag,),
    )[0]


def assemble_kernel(core_ref, a_ref, b_ref, *rest):
    rest[-1][...] = jnp.where(core_ref[0] == pl.program_id(0), a_ref[...], b_ref[...])


def assemble(chain, core, chunk, length, a, b, so_far):
    height, d = a.shape
    block = whole((height, d))
    anywhere = pl.BlockSpec(memory_space=pl.ANY)
    return chain(
        assemble_kernel, "assemble", 2,
        [(a, block), (b, block)] + ([] if so_far is None else [(so_far, anywhere)]),
        [((length, d), BF16, pl.BlockSpec((height, d), lambda i, *s: (place_of(chunk, i), 0)))],
        scalars=(core,), alias=() if so_far is None else ((2, 0),), mib=16,
    )[0]


def close_chunk_kernel(closing, core_ref, *refs):
    refs[-1][...] = closing(*refs[:-1])


def close_chunk(chain, closing, core, chunk, a, b, own, small):
    height, d = a.shape
    part = height // 2
    block = rows(d, part)

    def mine(n):
        return pl.BlockSpec((part, n), lambda i, core: (2 * place_of(chunk, core[0]) + i, 0))

    return chain(
        partial(close_chunk_kernel, closing), "close", 2,
        [(a, block), (b, block)] + [(o, mine(o.shape[1])) for o in own] + [(small, whole(small.shape))],
        [(a.shape, BF16, block)],
        scalars=(core,),
    )[0]


def swap_cores(value, size):
    return lax.ppermute(value, "tensor", [(i, i ^ 1) for i in range(size)])


def along(value, hops):
    return lax.ppermute(
        value, "tensor", [(2 * a + c, 2 * b + c) for a, b in hops for c in (0, 1)]
    )


def grad_rows(a, b, x, stats, g, small):
    u = (a[...].astype(F32) + b[...].astype(F32)) * small[0:1]
    mean, inverse = stats[:, 0:1], stats[:, 1:2]
    scaled = (x[...].astype(F32) - mean) * inverse
    back_u = inverse * (
        u
        - jnp.mean(u, axis=-1, keepdims=True)
        - scaled * jnp.mean(u * scaled, axis=-1, keepdims=True)
    )
    return (g[...].astype(F32) + back_u).astype(BF16)


SPLIT = 4
PIECE = TILE // SPLIT


def line_kernel(
    first, gq, gk, gv, pre, x_block, stats_block, wq, wu, small, extra, x_all, g_all, stats_all, *refs
):
    parts, refs = refs[: first // SPLIT], refs[first // SPLIT :]
    output, grad, vectors = refs[:3]
    held, came, own, lines, across, x_own, g_own, stats_own, sums, by_dp, mine, by_tensor = refs[3:15]
    (
        load_sem, peer_send, peer_recv, in_send, in_recv, mid_send, mid_recv, out_send, out_recv,
        fin_send, fin_recv, keep_sem,
    ) = refs[15:]
    chunks = came.shape[0]
    i = pl.program_id(0)
    steps, pieces = 2 * chunks, SPLIT * chunks
    d = came.shape[2]
    row, me = lax.axis_index("dp"), lax.axis_index("tensor")
    count, size = by_dp.shape[0], by_tensor.shape[0]
    core = lax.rem(me, 2)
    chip = me // 2
    peer = me + 1 - 2 * core
    beside = 2 * (chip + 1 - 2 * lax.rem(chip, 2)) + core
    facing = 2 * (3 - chip) + core
    middle = (chip == 1) | (chip == 2)
    end = jnp.logical_not(middle)
    mesh = pl.DeviceIdType.MESH
    barrier = pltpu.get_barrier_semaphore()

    def remote(source, target, send_sem, recv_sem, device, axis="tensor"):
        return pltpu.make_async_remote_copy(
            src_ref=source, dst_ref=target, send_sem=send_sem, recv_sem=recv_sem,
            device_id={axis: device}, device_id_type=mesh,
        )

    shift = pieces - first
    every = pieces + first

    def place(p, before=0):
        start = place_of(p // SPLIT, core) * TILE + lax.rem(p, SPLIT) * PIECE - before
        return pl.ds(pl.multiple_of(start, PIECE), PIECE)

    def peer_copy(c):
        return remote(held.at[c], came.at[c], peer_send.at[c], peer_recv.at[c], peer)

    def in_copy(p):
        return remote(own.at[p], lines.at[p], in_send.at[p], in_recv.at[p], beside)

    def mid_copy(p):
        return remote(own.at[p], across.at[p], mid_send.at[p], mid_recv.at[p], facing)

    def out_copy(p):
        return remote(lines.at[p], lines.at[p], out_send.at[p], out_recv.at[p], beside)

    def fin_copy(p, target):
        return remote(lines.at[p], target, fin_send.at[p], fin_recv.at[p], peer)

    def keep_copy(p, target):
        return pltpu.make_async_copy(lines.at[p], target, keep_sem.at[p])

    def part_copy(p):
        return pltpu.make_async_copy(
            parts[p // SPLIT].at[pl.ds(p % SPLIT * PIECE, PIECE)], own.at[p], keep_sem.at[p]
        )

    def of(p, action):
        @pl.when(p < first)
        def _():
            action(p, output.at[place(p + shift, shift * 2 * PIECE)])

        @pl.when(p >= first)
        def _():
            action(p, grad.at[place(p - first)])

    def loads(p):
        return [
            pltpu.make_async_copy(array.at[place(p)], here.at[p], load_sem.at[n, p])
            for n, (array, here) in enumerate(((x_all, x_own), (g_all, g_own), (stats_all, stats_own)))
        ]

    def dp_copy(n):
        device = lax.rem(row + n, count)
        wide = d // count
        source = sums.at[:, pl.ds(pl.multiple_of(device * wide, 128), wide)]
        return remote(source, by_dp.at[n], load_sem.at[3, n], load_sem.at[4, n], device, "dp")

    def tensor_copy(n):
        device = lax.rem(me + n, size)
        return remote(mine, by_tensor.at[n], load_sem.at[5, n], load_sem.at[6, n], device)

    def hand_over(p, target):
        fin_copy(p, target).start()
        keep_copy(p, target).start()

    def take_in(p):
        in_copy(p).wait_recv()
        own[p] = (own[p].astype(F32) + lines[p].astype(F32)).astype(BF16)
        mid_copy(p).start()

    def finish(p):
        mid_copy(p).wait_recv()

        @pl.when(p < first)
        def _():
            q = p + shift
            lines[p] = output_rows(own[p], x_own[q], across[p], small[...])

        @pl.when(p >= first)
        def _():
            q = p - first
            lines[p] = grad_rows(own[p], across[p], x_own[q], stats_own[q], g_own[q], small[...])

        out_copy(p).start()
        of(p, hand_over)

    def each(action, begin=0, stop=every):
        lax.fori_loop(begin, stop, lambda p, _: (action(p), 0)[1], 0)

    @pl.when(i == 0)
    def _():
        for n in range(1, count):
            pl.semaphore_signal(
                barrier, inc=1, device_id={"dp": lax.rem(row + n, count)}, device_id_type=mesh
            )
        for n in range(1, size):
            pl.semaphore_signal(
                barrier, inc=1, device_id={"tensor": lax.rem(me + n, size)}, device_id_type=mesh
            )
        sums[...] = extra[...]
        for p in range(first):
            part_copy(p).start()
        pl.semaphore_wait(barrier, count + size - 2)
        for p in range(first):
            part_copy(p).wait()

    @pl.when((i == 0) & end)
    def _():
        each(lambda p: in_copy(p).start(), 0, first)

    @pl.when((i == 0) & middle)
    def _():
        each(lambda p: [load.start() for load in loads(p)], 0, pieces)

    @pl.when((i == 1) & middle)
    def _():
        each(lambda p: [load.wait() for load in loads(p)], 0, pieces)

    ours = lax.rem(i, 2)
    half = i // 2
    to = pl.ds(first + SPLIT * half, SPLIT)
    for cut in range(0, d, 2 * TILE):
        cut = slice(cut, cut + 2 * TILE)
        total = nt(pre[...], wu[cut])
        for c, g in enumerate((gq, gk, gv)):
            total = total + nt(g[...], wq[c, cut])
        scaled = (x_block[:, cut].astype(F32) - stats_block[:, 0:1]) * stats_block[:, 1:2]
        sums[0:1, cut] += jnp.sum(total * scaled, axis=0, keepdims=True)
        sums[1:2, cut] += jnp.sum(total, axis=0, keepdims=True)
        total = total.astype(BF16)

        @pl.when(ours == 0)
        def _():
            held[half, :, cut] = total

        @pl.when(ours == 1)
        def _():
            own[to, :, cut] = total.reshape(SPLIT, PIECE, 2 * TILE)

    @pl.when(ours == 0)
    def _():
        peer_copy(half).start()

    @pl.when(ours == 1)
    def _():
        peer_copy(half).wait_recv()
        total = own[to].astype(F32) + came[half].reshape(SPLIT, PIECE, d).astype(F32)
        own[to] = total.astype(BF16)

    @pl.when((ours == 1) & end)
    def _():
        for r in range(SPLIT):
            in_copy(first + SPLIT * half + r).start()

    early = steps
    begin = steps - early

    @pl.when((i >= begin) & middle)
    def _():
        take_in(i - begin)

    @pl.when((i > begin) & middle)
    def _():
        finish(i - begin - 1)

    @pl.when(i == steps - 1)
    def _():
        for n in range(1, count):
            dp_copy(n).start()

    def both(p, _):
        take_in(p)
        finish(p - 1)
        return 0

    def pass_on(p):
        out_copy(p).wait_recv()
        of(p, hand_over)

    some = early + 2 * (every - early) // 3

    @pl.when((i == steps - 1) & middle)
    def _():
        lax.fori_loop(early, some, both, 0)

    @pl.when((i == steps - 1) & end)
    def _():
        each(pass_on, 0, some)

    @pl.when(i == steps - 1)
    def _():
        wide = d // count
        total = sums[:, pl.ds(pl.multiple_of(row * wide, 128), wide)]
        for n in range(1, count):
            dp_copy(n).wait()
            total = total + by_dp[n]
        mine[...] = total
        for n in range(1, size):
            tensor_copy(n).start()

    @pl.when((i == steps - 1) & middle)
    def _():
        lax.fori_loop(some, every, both, 0)
        finish(every - 1)
        each(lambda p: (mid_copy(p).wait_send(), out_copy(p).wait_send()))

    @pl.when((i == steps - 1) & end)
    def _():
        each(pass_on, some)
        each(lambda p: in_copy(p).wait_send())

    @pl.when(i == steps - 1)
    def _():
        total = mine[...]
        for n in range(1, size):
            tensor_copy(n).wait()
            total = total + by_tensor[n]
        vectors[...] = jnp.concatenate([total[:2], mine[2:]])
        for c in range(chunks):
            peer_copy(c).wait_send()
        each(lambda p: of(p, lambda *a: (fin_copy(*a).wait(), keep_copy(*a).wait())))


def line_back(chain, parts, chunks, size, count, gq, gk, gv, pre, x, stats, wq, wu, small, extra, g):
    length, d = x.shape
    width, units = wq.shape[2], wu.shape[1]
    pieces, first = SPLIT * chunks, SPLIT * len(parts)

    def block(n):
        def index(i):
            core = lax.rem(lax.axis_index("tensor"), 2)
            mine = lax.rem(i, 2)
            return (place_of(i // 2, lax.rem(core + 1 + mine, 2)), 0)

        return pl.BlockSpec((TILE, n), index)

    def once(shape):
        zeros = (0,) * len(shape)
        return pl.BlockSpec(shape, lambda *i: zeros, pipeline_mode=pl.Buffered(1))

    far = pl.BlockSpec(memory_space=pltpu.HBM)
    rows_of = lambda n: pltpu.VMEM((n, PIECE, d), BF16)
    sems = pltpu.SemaphoreType.DMA
    vector = (8, d // count)
    return chain(
        partial(line_kernel, first),
        "line_back",
        2 * chunks,
        [(a, block(width)) for a in (gq, gk, gv)]
        + [
            (pre, block(units)), (x, block(d)), (stats, block(PAIR)), (wq, once(wq.shape)),
            (wu, once(wu.shape)), (small, once(small.shape)), (extra, once(extra.shape)),
            (x, far), (g, far), (stats, far),
        ]
        + [(p, far) for p in parts],
        [
            ((first * 2 * PIECE, d), BF16, far), ((length, d), BF16, far),
            (vector, F32, whole(vector)),
        ],
        scratch=[
            pltpu.VMEM((chunks, TILE, d), BF16), pltpu.VMEM((chunks, TILE, d), BF16),
            rows_of(first + pieces), rows_of(first + pieces), rows_of(first + pieces),
            rows_of(pieces), rows_of(pieces),
            pltpu.VMEM((pieces, PIECE, PAIR), F32),
            pltpu.VMEM((8, d), F32), pltpu.VMEM((count, *vector), F32), pltpu.VMEM(vector, F32),
            pltpu.VMEM((size, *vector), F32),
            sems((7, max(pieces, size, count))), sems((chunks,)), sems((chunks,)),
        ]
        + [sems((first + pieces,))] * 9,
        collective=5,
        flops=200e9,
        mib=62,
    )


def flow(chain, size, core, chunk, total, closing, results, key, length):
    chips = size // 2
    chip = lax.axis_index("tensor") // 2
    distance = jnp.where(chip < chips // 2, chips // 2 - 1 - chip, chip - chips // 2)
    for s in range(chips // 2 - 1):
        came = along(total, [(s, s + 1), (chips - 1 - s, chips - 2 - s)])
        yield
        total = plus(chain, total, came)
    a, b = chips // 2 - 1, chips // 2
    came = along(total, [(a, b), (b, a)])
    yield
    value = closing(chunk, total, came)
    for s in range(chips // 2 - 1):
        a, b = chips // 2 - 1 - s, chips // 2 + s
        came = along(value, [(a, a - 1), (b, b + 1)])
        yield
        value = choose(chain, (distance == s + 1).astype(jnp.int32)[None], value, came)
    peer = swap_cores(value, size)
    yield
    results[key] = assemble(chain, core, chunk, length, value, peer, results.get(key))


def on_device(
    size,
    inputs,
    segment_ids,
    norm_gain,
    norm_bias,
    qkv_weight,
    qkv_bias,
    out_weight,
    out_bias,
    up_weight,
    up_bias,
    down_weight,
    down_bias,
    cotangent,
):
    x, g, segment_row = inputs[0], cotangent[0], segment_ids[0]
    length, d = x.shape
    width, units = qkv_weight.shape[2], up_weight.shape[1]
    count = lax.axis_size("dp")
    core = (lax.axis_index("tensor") % 2).astype(jnp.int32)[None]

    start = jnp.sum((segment_row[None, :] < segment_row[:, None]).astype(jnp.int32), axis=1)
    small = jnp.stack([norm_gain, norm_bias, out_bias, down_bias] + [norm_gain] * 4).astype(F32)
    wq = qkv_weight.transpose(1, 0, 2)

    chain = Chain()
    normed, stats, q, k, v, hidden, slope, cos_wide, sin_wide = first(
        chain, x, small, wq, qkv_bias, up_weight, up_bias, start
    )
    mixed, log = attend(chain, start, q, k, v)
    rest = 2 if size == 8 else 0
    lower = length - rest * (length // CHUNKS)
    weights = (mixed, hidden, out_weight, down_weight)
    summed = lax.psum(branch(chain, lower, *weights), "tensor")
    parts = branch_rest(chain, rest, CHUNKS - rest, *weights) if rest else []

    pre, gm, delta, g_sums, up_sums = back(chain, g, slope, mixed, out_weight, down_weight)
    scatter = lambda a: lax.psum_scatter(a, "dp", scatter_dimension=1, tiled=True)
    near = scatter(weight_grad(chain, "weight_grad_g", [hidden, mixed], g))
    tiles = length // TILE
    *packed, qkv_sums, _ = attend_back(
        chain, 0, tiles, start, log, delta, q, k, v, gm, cos_wide, sin_wide, [log]
    )
    far = scatter(weight_grad(chain, "weight_grad_n", [pre, *packed], normed))

    by_share = lambda a: a.reshape(-1, count, HD // count).swapaxes(0, 1).reshape(count, -1)
    part = d // count
    narrow = jnp.concatenate([by_share(up_sums[0]), by_share(qkv_sums[:3])], axis=1)
    narrow = jnp.pad(narrow, ((0, 0), (0, part - narrow.shape[1]))).reshape(1, d)
    if size == 8:
        extra = jnp.concatenate([jnp.zeros((2, d), F32), g_sums[:1], narrow, jnp.zeros((4, d), F32)])
        upper, grad, vectors = line_back(
            chain, parts, CHUNKS, size, count, *packed, pre, x, stats, wq, up_weight, small, extra, g
        )
    else:

        results = {}

        def line(parts, closing, own, key):
            finish = lambda chunk, a, b: close_chunk(chain, closing, core, chunk, a, b, own, small)
            flows = [
                flow(chain, size, core, c, parts[c], finish, results, key, length)
                for c in range(CHUNKS)
            ]
            while flows:
                flows = [f for f in flows if next(f, flows) is None]

        norm_sums, *parts = normed_back(chain, CHUNKS, *packed, pre, x, stats, wq, up_weight)
        line(parts, grad_rows, [x, stats, g], "grad")
        vectors = jnp.concatenate([norm_sums[:2], g_sums[:1], narrow]).reshape(4, count, part)
        vectors = vectors.swapaxes(0, 1).reshape(count, -1, 128)
        vectors = add_vectors(chain, vectors, size, count).reshape(4, part)
    if size == 8:
        output, input_grad, down_share, out_share, up_share, qkv_share = last(
            chain, summed, x, small, upper, grad, near, far, width, units
        )
    else:
        output, input_grad = close_both(chain, summed, x, small, results["grad"])
        shapes = [(units, part), (width, part)]
        down_share, out_share = widen(chain, near, shapes, (False, False))
        shapes = [(part, units), (3, part, width)]
        up_share, qkv_share = widen(chain, far, shapes, (True, True))
    up_b_share = vectors[3, : units // count].reshape(-1, HD // count)
    qkv_b_share = vectors[3, units // count : (units + 3 * width) // count].reshape(3, -1, HD // count)

    return (
        output[None],
        input_grad[None],
        vectors[0],
        vectors[1],
        qkv_share.transpose(1, 0, 2),
        qkv_b_share,
        out_share,
        vectors[2],
        up_share,
        up_b_share,
        down_share,
        vectors[2],
    )


def solution(mesh):
    placed = (
        P("dp", None, None),
        P("dp", None),
        P(),
        P(),
        P(None, None, "tensor"),
        P(None, "tensor"),
        P("tensor", None),
        P(),
        P(None, "tensor"),
        P("tensor"),
        P("tensor", None),
        P(),
        P("dp", None, None),
    )
    return jax.shard_map(
        partial(on_device, mesh.shape["tensor"]),
        mesh=mesh,
        in_specs=placed,
        out_specs=(
            P("dp", None, None),
            P("dp", None, None),
            P("dp"),
            P("dp"),
            P("dp", None, "tensor"),
            P(None, "tensor", "dp"),
            P("tensor", "dp"),
            P("dp"),
            P("dp", "tensor"),
            P("tensor", "dp"),
            P("tensor", "dp"),
            P("dp"),
        ),
        check_vma=False,
    )
```
